32 devices in a mesh: tm: 4 (over x, core), space: 8 (over z, y).
Axes of the slice: x: 2, y: 2, z: 4, core: 2. Of those that a mesh axis runs over, the one named last changes fastest.
Arguments:
- guesses: float32 [4, 128, 4096], P('tm', 'space'), may hold values from -6 to 6
- cond_x: float32 [128, 4096], P('space'), may hold values from 0.025 to 0.24
- cond_y: float32 [128, 4096], P('space'), may hold values from 0.005 to 0.05
- source: float32 [128, 4096], P('space'), may hold values from -0.6 to 0.6
- inflow: float32 [64, 2048], P('space'), may hold values from -6 to 6
Outputs:
- corrected: float32 [4, 128, 4096], P('tm', 'space')
The draws below stay inside these ranges and needn't reach their ends.
All inputs are finite; a program needn't handle non-finite values.
Results may differ from the reference program's by a relative error of at most 0.00002.
Values sent between devices are 32-bit elements; how exact they have to be, the bound alone decides.
No kernel may reach another device: no remote copies, remote signals or barrier semaphores. Data moves between devices by JAX's collectives and lax.ppermute only.
A program may use at most 128 MiB of HBM per device.

```python
import math
import jax
import jax.numpy as jnp
from jax import lax

NY = 4096
FINE_STEPS = 4
GROUPS = 4
NX = 128


def level_of(own_key, shape, pieces, smallest, high):
    loudness, own = 1.0, jax.random.fold_in(own_key, 6)
    for dim, shards_of in pieces:
        heights = jnp.exp(jax.random.uniform(jax.random.fold_in(own, dim), (shards_of,), jnp.float32, smallest / len(pieces), high / len(pieces)))
        loudness = loudness * jnp.repeat(heights, shape[dim] // shards_of).reshape([-1 if axis == dim else 1 for axis in range(len(shape))])
    return loudness


def gaussian(own_key, extent, spread, limit, pieces=(), kind=jnp.bfloat16):
    array = jax.random.normal(own_key, extent, jnp.float32) * spread
    if len(pieces) > 0:
        array = level_of(own_key, extent, pieces, -0.22, 0.18) * array
    return jnp.clip(array, min=-limit, max=limit).astype(kind)


def setup_inputs(seed: int = 0) -> dict:
    arg_keys = jax.random.split(jax.random.key(seed), 6)
    return {
        "guesses": gaussian(arg_keys[0], (GROUPS, NX, NY), 1.0, 6.0, ((0, 4), (1, 8)), jnp.float32),
        "cond_x": jnp.clip(jnp.exp(math.log(0.24) - 2.261763 * jax.random.uniform(arg_keys[1], (NX, NY), jnp.float32) ** level_of(arg_keys[1], (NX, NY), ((0, 8),), -0.2, 0.2)), 0.025, 0.24),
        "cond_y": jnp.clip(jnp.exp(math.log(0.05) - 2.3025851 * jax.random.uniform(arg_keys[2], (NX, NY), jnp.float32) ** level_of(arg_keys[2], (NX, NY), ((0, 8),), -0.2, 0.2)), 0.005, 0.05),
        "source": gaussian(arg_keys[3], (NX, NY), 0.1, 0.6, ((0, 8),), jnp.float32),
        "inflow": gaussian(arg_keys[4], (NX // 2, NY // 2), 1.0, 6.0, ((0, 8),), jnp.float32),
    }


def fine_step(field, cond_x, cond_y, source):
    rows_pad = jnp.pad(field, ((1, 1), (0, 0)))
    cond_prev = jnp.pad(cond_x, ((1, 0), (0, 0)))[:-1]
    flux_sum = cond_x * (rows_pad[2:] - field) - cond_prev * (field - rows_pad[:-2])
    cols_pad = jnp.pad(field, ((0, 0), (1, 1)))
    cond_west = jnp.pad(cond_y, ((0, 0), (1, 0)))[:, :-1]
    flux_sum = flux_sum + cond_y * (cols_pad[:, 2:] - field) - cond_west * (field - cols_pad[:, :-2])
    return field + flux_sum + source


def restrict(field):
    lead = field.shape[:-2]
    shaped = field.reshape(lead + (field.shape[-2] // 2, 2, field.shape[-1] // 2, 2))
    return jnp.mean(shaped, axis=(-3, -1))


def reference(guesses, cond_x, cond_y, source, inflow):
    def propagate(field):
        for section in range(FINE_STEPS):
            field = fine_step(field, cond_x, cond_y, source)
        return field

    first_pass = lax.map(propagate, guesses)
    relaxed = jnp.concatenate([guesses[:1], first_pass[:-1]], axis=0)
    second_pass = lax.map(propagate, relaxed)
    residual = lax.map(restrict, second_pass[:-1] - relaxed[1:])
    coarse_x = restrict(cond_x)
    coarse_y = restrict(cond_y)
    error_field = inflow.astype(jnp.float32)
    errors = [error_field]
    for group in range(1, GROUPS):
        error_field = fine_step(error_field, coarse_x, coarse_y, 0.0) + residual[group - 1]
        errors.append(error_field)
    stacked = jnp.stack(errors)
    widened = jnp.repeat(jnp.repeat(stacked, 2, axis=1), 2, axis=2)
    return relaxed + widened
```

```python
import functools

import jax
import jax.numpy as jnp
from jax import lax
from jax.experimental import pallas as pl
from jax.experimental.pallas import tpu as pltpu
from jax.sharding import PartitionSpec as P

FINE_STEPS = 4
HALO = 12
LANE = 128
VMEM_LIMIT = 40 * 1024 * 1024


def padded(value, sides, width):
    for axis, dim in sides:
        devices, length = (lax.axis_size(axis), value.shape[dim])
        up = [(i, (i + 1) % devices) for i in range(devices - 1)]
        down = [(j, i) for i, j in up]
        last = lax.slice_in_dim(value, length - width, length, axis=dim)
        leading = lax.slice_in_dim(value, 0, width, axis=dim)
        before = lax.ppermute(last, axis, up)
        after = lax.ppermute(leading, axis, down)
        value = jnp.concatenate([before, value, after], axis=dim)
    return value


def from_behind(value, axis, steps):
    count = lax.axis_size(axis)
    leading, last = (max(0, -steps), min(count, count - steps))
    return lax.ppermute(value, axis, [(source, source + steps) for source in range(leading, last)])


def interior(field_ext, cond_rows, cond_cols):
    centre = field_ext[1:-1]
    flux_sum = cond_rows[1:-1] * (field_ext[2:] - centre) - cond_rows[:-2] * (
        centre - field_ext[:-2]
    )
    widened = jnp.pad(centre, ((0, 0), (1, 1)))
    cond_own = cond_cols[1:-1]
    cond_west = jnp.pad(cond_own, ((0, 0), (1, 0)))[:, :-1]
    flux_sum = (
        flux_sum + cond_own * (widened[:, 2:] - centre) - cond_west * (centre - widened[:, :-2])
    )
    return centre + flux_sum


def propagate(field, coef_pad):
    strip_rows = field.shape[0]
    cond_rows = coef_pad[0, 3 : strip_rows + 5]
    cond_cols = coef_pad[1, 3 : strip_rows + 5]
    source_rows = coef_pad[2, 4 : strip_rows + 4]
    for section in range(FINE_STEPS):
        extended = padded(field, (("space", 0),), 1)
        field = interior(extended, cond_rows, cond_cols) + source_rows
    return field


def restrict(field):
    lead = field.shape[:-2]
    shaped = field.reshape(lead + (field.shape[-2] // 2, 2, field.shape[-1] // 2, 2))
    return jnp.mean(shaped, axis=(-3, -1))


def general_shards(guesses, cond_x, cond_y, source, inflow):
    strip_rows = cond_x.shape[0]
    columns = cond_x.shape[1]
    stacked = jnp.stack([cond_x, cond_y, source])
    edge_rows = from_behind(cond_x[strip_rows - 2 :], "space", 1)
    cond_upper = jnp.concatenate([jnp.zeros((2, columns), jnp.float32), edge_rows], axis=0)
    blank_rows = jnp.zeros((4, columns), jnp.float32)
    upper = jnp.stack([cond_upper, blank_rows, blank_rows])
    lower = jnp.zeros((3, 4, columns), jnp.float32)
    coef_pad = jnp.concatenate([upper, stacked, lower], axis=1)
    first_group = lax.axis_index("tm") == 0
    c_point = guesses[0]
    first_pass = propagate(c_point, coef_pad)
    received = from_behind(first_pass, "tm", 1)
    relaxed = jnp.where(first_group, c_point, received)
    second_pass = propagate(relaxed, coef_pad)
    fine_next = from_behind(second_pass, "tm", 1)
    residual = restrict(fine_next - relaxed)
    residual = jnp.where(first_group, 0.0, residual)
    coarse_coef = restrict(coef_pad[:2, 2 : strip_rows + 6])

    def chain_round(index, error_field):
        extended = padded(error_field, (("space", 0),), 1)
        stepped = interior(extended, coarse_coef[0], coarse_coef[1])
        arrived = from_behind(stepped, "tm", 1)
        return jnp.where(first_group, inflow, arrived + residual)

    start_error = jnp.where(first_group, inflow, jnp.zeros_like(residual))
    error_field = lax.fori_loop(0, lax.axis_size("tm") - 1, chain_round, start_error)
    widened = jnp.repeat(jnp.repeat(error_field, 2, axis=0), 2, axis=1)
    return (relaxed + widened)[None]


def window_start(index, own, columns, lanes):
    return jnp.clip(own * index - LANE, 0, columns - lanes)


def pack_kernel(ids, guess, cond_x, cond_y, source, inflow, send, halo_a, halo_b, coefs, inflow_win, wide):
    blocks, rows, lanes = send.shape
    columns = guess.shape[1]
    own = columns // blocks
    for block in range(blocks):
        start = min(max(own * block - LANE, 0), columns - lanes)
        send[block] = guess[:, start : start + lanes]
    half = lax.broadcasted_iota(jnp.int32, (rows // 2, LANE), 1) // 2
    for part in range(columns // (2 * LANE)):
        piece = inflow[:, part * LANE : (part + 1) * LANE]
        for side in range(2):
            at = (2 * part + side) * LANE
            wide[:, at : at + LANE] = jnp.take_along_axis(piece, half + side * (LANE // 2), axis=1)
    window = pl.ds(pl.multiple_of(ids[0], LANE), lanes)
    for slot, ref in enumerate((cond_x, cond_y, source)):
        coefs[slot] = ref[:, window]
    inflow_win[...] = wide[:, window]

    def fill(bottom, top):
        for slot in range(3):
            bottom[slot * HALO : (slot + 1) * HALO] = coefs[slot, rows - HALO :]
            top[slot * HALO : (slot + 1) * HALO] = coefs[slot, :HALO]
        bottom[3 * HALO :] = inflow_win[rows // 2 - 4 :]
        top[3 * HALO :] = inflow_win[:4]

    @pl.when(ids[2] == 1)
    def _():
        fill(halo_a, halo_b)

    @pl.when(ids[2] == 0)
    def _():
        fill(halo_b, halo_a)


FIELD_ROWS = (12, 8, 4)


def edge_kernel(ids, fields, edge_a, edge_b):
    rows = fields.shape[1]

    def fill(bottom, top):
        at = 0
        for group, deep in enumerate(FIELD_ROWS):
            bottom[at : at + deep] = fields[group, rows - deep :]
            top[at : at + deep] = fields[group, :deep]
            at += deep

    @pl.when(ids[2] == 1)
    def _():
        fill(edge_a, edge_b)

    @pl.when(ids[2] == 0)
    def _():
        fill(edge_b, edge_a)


def spread(value):
    rows, lanes = value.shape
    row_even = lax.broadcasted_iota(jnp.int32, value.shape, 0) % 2 == 0
    lane_even = lax.broadcasted_iota(jnp.int32, value.shape, 1) % 2 == 0
    value = value + jnp.where(row_even, pltpu.roll(value, rows - 1, 0), pltpu.roll(value, 1, 0))
    value = value + jnp.where(lane_even, pltpu.roll(value, lanes - 1, 1), pltpu.roll(value, 1, 1))
    return value * 0.25


def sweep(get, cond_x, cond_y, put, first, last, chunks, width, limit):
    count = last - first
    lane = lax.broadcasted_iota(jnp.int32, (count, LANE), 1)
    row = lax.broadcasted_iota(jnp.int32, (count, LANE), 0) + first
    inside = row < limit

    def load(chunk):
        value = get(chunk)
        return value, pltpu.roll(value, LANE - width, 1)

    value, east = load(0)
    west_flux = jnp.zeros((count, LANE), jnp.float32)
    for chunk in range(chunks):
        at = slice(chunk * LANE, (chunk + 1) * LANE)
        if chunk + 1 < chunks:
            next_value, next_east = load(chunk + 1)
        else:
            next_value, next_east = None, jnp.zeros((count, LANE), jnp.float32)
        beside = jnp.where(lane >= LANE - width, next_east, east)
        flux_y = cond_y[first:last, at] * (beside - value)
        rolled = pltpu.roll(flux_y, width, 1)
        flux_w = jnp.where(lane < width, west_flux, rolled)
        below = pltpu.roll(value, count - width, 0)
        flux_x = cond_x[first:last, at] * (below - value)
        above = pltpu.roll(flux_x, width, 0)
        result = value + ((flux_x - above) + (flux_y - flux_w))
        put(chunk, at, result, inside)
        value, east, west_flux = next_value, next_east, rolled


def main_kernel(
    ids, fields, coefs, inflow_win, coef_a, coef_b, edge_a, edge_b, out,
    cond_x, cond_y, source, coarse_x, coarse_y, guess, work, first_pass, second_pass, error,
):
    groups, rows, lanes = fields.shape
    own = out.shape[2]
    high = rows + 2 * HALO
    chunks = lanes // LANE
    limit = jnp.where(ids[3] == 1, HALO + rows, high)
    twice = lax.broadcasted_iota(jnp.int32, (8, LANE), 0) // 2

    def assemble(upper_c, lower_c, upper_f, lower_f):
        for slot, ref in enumerate((cond_x, cond_y, source)):
            ref[:HALO] = upper_c[slot * HALO : (slot + 1) * HALO]
            ref[HALO + rows :] = lower_c[slot * HALO : (slot + 1) * HALO]
        at = 0
        for group, deep in enumerate(FIELD_ROWS):
            if deep < HALO:
                blank = jnp.zeros((HALO - deep, lanes), jnp.float32)
                guess[group, : HALO - deep] = blank
                guess[group, HALO + rows + deep :] = blank
            guess[group, HALO - deep : HALO] = upper_f[at : at + deep]
            guess[group, HALO + rows : HALO + rows + deep] = lower_f[at : at + deep]
            at += deep
        blank = jnp.zeros((HALO - 8, lanes), jnp.float32)
        error[0, : HALO - 8] = blank
        error[0, HALO + rows + 8 :] = blank
        for chunk in range(chunks):
            at = slice(chunk * LANE, (chunk + 1) * LANE)
            both = jnp.concatenate([upper_c[3 * HALO :, at], lower_c[3 * HALO :, at]], axis=0)
            error[0, HALO - 8 : HALO, at] = jnp.take_along_axis(both, twice, axis=0)
            error[0, HALO + rows : HALO + rows + 8, at] = jnp.take_along_axis(both, twice + 4, axis=0)

    @pl.when(ids[2] == 1)
    def _():
        assemble(coef_b, coef_a, edge_b, edge_a)

    @pl.when(ids[2] == 0)
    def _():
        assemble(coef_a, coef_b, edge_a, edge_b)

    own_rows = slice(HALO, HALO + rows)
    for slot, ref in enumerate((cond_x, cond_y, source)):
        ref[own_rows] = coefs[slot]
    for group in range(groups - 1):
        guess[group, own_rows] = fields[group]
    for chunk in range(chunks):
        at = slice(chunk * LANE, (chunk + 1) * LANE)
        for side in range(2):
            top = HALO + 8 * side
            error[0, top : top + 8, at] = jnp.take_along_axis(inflow_win[:, at], twice + 4 * side, axis=0)
        coarse_x[:, at] = spread(cond_x[:, at])
        coarse_y[:, at] = spread(cond_y[:, at])

    def step(from_ref, to_ref, first, last):
        def put(chunk, at, result, inside):
            result = result + source[first:last, at]
            to_ref[first:last, at] = jnp.where(inside, result, 0.0)

        def get(chunk):
            return from_ref[first:last, chunk * LANE : (chunk + 1) * LANE]

        sweep(get, cond_x, cond_y, put, first, last, chunks, 1, limit)

    def propagated(start, end, first, last):
        step(start, work.at[0], first, last)
        step(work.at[0], work.at[1], first, last)
        step(work.at[1], work.at[0], first, last)
        step(work.at[0], end, first, last)

    near, far = HALO - 4, HALO + rows + 4
    propagated(guess.at[0], first_pass.at[0], 0, high)
    propagated(guess.at[1], first_pass.at[1], 0, high)
    propagated(guess.at[2], first_pass.at[2], near, far)
    propagated(first_pass.at[0], second_pass.at[0], 0, high)
    propagated(first_pass.at[1], second_pass.at[1], near, far)

    ends = (first_pass.at[0], second_pass.at[0], second_pass.at[1])
    for group in range(1, groups):
        first, last = (0, high) if group < groups - 1 else (near, far)
        before = error.at[group - 1]

        def put(chunk, at, result, inside):
            residual = spread(ends[group - 1][first:last, at] - first_pass[group - 1, first:last, at])
            error[group, first:last, at] = jnp.where(inside, result + residual, 0.0)

        def get(chunk):
            return before[first:last, chunk * LANE : (chunk + 1) * LANE]

        sweep(get, coarse_x, coarse_y, put, first, last, chunks, 2, limit)

    window = pl.ds(pl.multiple_of(ids[1], LANE), own)
    for group in range(groups):
        relaxed = guess.at[0] if group == 0 else first_pass.at[group - 1]
        out[group] = relaxed[own_rows, window] + error[group, own_rows, window]


def unpack_kernel(blocks, out):
    own = blocks.shape[2]
    for block in range(blocks.shape[0]):
        out[0, :, block * own : (block + 1) * own] = blocks[block]


def call(kernel, outs, scratch, *operands):
    vmem = pl.BlockSpec(memory_space=pltpu.VMEM)
    smem = pl.BlockSpec(memory_space=pltpu.SMEM)
    return pl.pallas_call(
        kernel,
        out_shape=[jax.ShapeDtypeStruct(shape, jnp.float32) for shape in outs],
        in_specs=[smem if value.dtype == jnp.int32 else vmem for value in operands],
        out_specs=[vmem] * len(outs),
        scratch_shapes=[pltpu.VMEM(shape, jnp.float32) for shape in scratch],
        compiler_params=pltpu.CompilerParams(vmem_limit_bytes=VMEM_LIMIT),
    )(*operands)


def shards(guesses, cond_x, cond_y, source, inflow):
    groups, strips = lax.axis_size("tm"), lax.axis_size("space")
    rows, columns = cond_x.shape
    fits = groups == len(FIELD_ROWS) + 1 and strips % 2 == 0 and rows == 16
    if not fits or columns % (groups * LANE) != 0 or columns < (groups + 2) * LANE:
        return general_shards(guesses, cond_x, cond_y, source, inflow)
    own = columns // groups
    lanes = own + 2 * LANE
    high = rows + 2 * HALO
    member, strip = lax.axis_index("tm"), lax.axis_index("space")
    start = window_start(member, own, columns, lanes)
    ids = jnp.stack([start, own * member - start, 1 - strip % 2, (strip == strips - 1).astype(jnp.int32)])
    ids = ids.astype(jnp.int32)
    pairs_a = [(i, i ^ 1) for i in range(strips)]
    pairs_b = [(i, j) for k in range(1, strips - 1, 2) for i, j in ((k, k + 1), (k + 1, k))]

    send, halo_a, halo_b, coefs, inflow_win = call(
        pack_kernel,
        [(groups, rows, lanes), (3 * HALO + 4, lanes), (3 * HALO + 4, lanes), (3, rows, lanes), (rows // 2, lanes)],
        [(rows // 2, columns)],
        ids, guesses[0], cond_x, cond_y, source, inflow,
    )
    coef_b = lax.ppermute(halo_b, "space", pairs_b)
    coef_a = lax.ppermute(halo_a, "space", pairs_a)
    fields = lax.all_to_all(send, "tm", 0, 0, tiled=True)
    deep = sum(FIELD_ROWS)
    sent_a, sent_b = call(edge_kernel, [(deep, lanes)] * 2, [], ids, fields)
    edge_b = lax.ppermute(sent_b, "space", pairs_b)
    edge_a = lax.ppermute(sent_a, "space", pairs_a)
    (blocks,) = call(
        main_kernel,
        [(groups, rows, own)],
        [(high, lanes)] * 5
        + [(groups - 1, high, lanes), (2, high, lanes), (groups - 1, high, lanes), (groups - 2, high, lanes), (groups, high, lanes)],
        ids, fields, coefs, inflow_win, coef_a, coef_b, edge_a, edge_b,
    )
    blocks = lax.all_to_all(blocks, "tm", 0, 0, tiled=True)
    return call(unpack_kernel, [(1, rows, columns)], [], blocks)[0]


def solution(mesh):
    return jax.shard_map(
        shards,
        mesh=mesh,
        in_specs=(
            P("tm", "space", None),
            P("space", None),
            P("space", None),
            P("space", None),
            P("space", None),
        ),
        out_specs=P("tm", "space", None),
        check_vma=False,
    )
```

```python
import functools

import jax
import jax.numpy as jnp
from jax import lax
from jax.experimental import pallas as pl
from jax.experimental.pallas import tpu as pltpu
from jax.sharding import PartitionSpec as P

FINE_STEPS = 4
LANE = 128
SIDE = 64
HALO = 16
COEF_ROWS = (10, 9, 9)
FIELD_ROWS = (12, 8, 4)
COARSE_ROWS = 4
VMEM_LIMIT = 40 * 1024 * 1024


def padded(value, sides, width):
    for axis, dim in sides:
        devices, length = (lax.axis_size(axis), value.shape[dim])
        up = [(i, (i + 1) % devices) for i in range(devices - 1)]
        down = [(j, i) for i, j in up]
        last = lax.slice_in_dim(value, length - width, length, axis=dim)
        leading = lax.slice_in_dim(value, 0, width, axis=dim)
        before = lax.ppermute(last, axis, up)
        after = lax.ppermute(leading, axis, down)
        value = jnp.concatenate([before, value, after], axis=dim)
    return value


def from_behind(value, axis, steps):
    count = lax.axis_size(axis)
    leading, last = (max(0, -steps), min(count, count - steps))
    return lax.ppermute(value, axis, [(source, source + steps) for source in range(leading, last)])


def interior(field_ext, cond_rows, cond_cols):
    centre = field_ext[1:-1]
    flux_sum = cond_rows[1:-1] * (field_ext[2:] - centre) - cond_rows[:-2] * (
        centre - field_ext[:-2]
    )
    widened = jnp.pad(centre, ((0, 0), (1, 1)))
    cond_own = cond_cols[1:-1]
    cond_west = jnp.pad(cond_own, ((0, 0), (1, 0)))[:, :-1]
    flux_sum = (
        flux_sum + cond_own * (widened[:, 2:] - centre) - cond_west * (centre - widened[:, :-2])
    )
    return centre + flux_sum


def propagate(field, coef_pad):
    strip_rows = field.shape[0]
    cond_rows = coef_pad[0, 3 : strip_rows + 5]
    cond_cols = coef_pad[1, 3 : strip_rows + 5]
    source_rows = coef_pad[2, 4 : strip_rows + 4]
    for section in range(FINE_STEPS):
        extended = padded(field, (("space", 0),), 1)
        field = interior(extended, cond_rows, cond_cols) + source_rows
    return field


def restrict(field):
    lead = field.shape[:-2]
    shaped = field.reshape(lead + (field.shape[-2] // 2, 2, field.shape[-1] // 2, 2))
    return jnp.mean(shaped, axis=(-3, -1))


def general_shards(guesses, cond_x, cond_y, source, inflow):
    strip_rows = cond_x.shape[0]
    columns = cond_x.shape[1]
    stacked = jnp.stack([cond_x, cond_y, source])
    edge_rows = from_behind(cond_x[strip_rows - 2 :], "space", 1)
    cond_upper = jnp.concatenate([jnp.zeros((2, columns), jnp.float32), edge_rows], axis=0)
    blank_rows = jnp.zeros((4, columns), jnp.float32)
    upper = jnp.stack([cond_upper, blank_rows, blank_rows])
    lower = jnp.zeros((3, 4, columns), jnp.float32)
    coef_pad = jnp.concatenate([upper, stacked, lower], axis=1)
    first_group = lax.axis_index("tm") == 0
    c_point = guesses[0]
    first_pass = propagate(c_point, coef_pad)
    received = from_behind(first_pass, "tm", 1)
    relaxed = jnp.where(first_group, c_point, received)
    second_pass = propagate(relaxed, coef_pad)
    fine_next = from_behind(second_pass, "tm", 1)
    residual = restrict(fine_next - relaxed)
    residual = jnp.where(first_group, 0.0, residual)
    coarse_coef = restrict(coef_pad[:2, 2 : strip_rows + 6])

    def chain_round(index, error_field):
        extended = padded(error_field, (("space", 0),), 1)
        stepped = interior(extended, coarse_coef[0], coarse_coef[1])
        arrived = from_behind(stepped, "tm", 1)
        return jnp.where(first_group, inflow, arrived + residual)

    start_error = jnp.where(first_group, inflow, jnp.zeros_like(residual))
    error_field = lax.fori_loop(0, lax.axis_size("tm") - 1, chain_round, start_error)
    widened = jnp.repeat(jnp.repeat(error_field, 2, axis=0), 2, axis=1)
    return (relaxed + widened)[None]


def window(index, own, columns, lanes):
    return jnp.clip(own * index - SIDE, 0, columns - lanes), jnp.clip(own * index - LANE, 0, columns - lanes - LANE)


def shifted(load, chunk, shift):
    amount = lax.rem(2 * LANE - shift, LANE)
    here = pltpu.roll(load(chunk), amount, 1)
    there = pltpu.roll(load(chunk + 1), amount, 1)
    lane = lax.broadcasted_iota(jnp.int32, here.shape, 1)
    return jnp.where(lane < LANE - shift, here, there)


def piece(chunk):
    return slice(chunk * LANE, (chunk + 1) * LANE)


def pack_kernel(
    ids, guess, cond_x, cond_y, source, inflow, send, halo_a, halo_b, coefs, coarse,
    guess_in, coefs_in, sems,
):
    blocks, rows, lanes = send.shape
    columns = guess.shape[1]
    own = columns // blocks
    around = pl.ds(pl.multiple_of(ids[0], LANE), lanes + LANE)
    coarse_at = pl.ds(pl.multiple_of(ids[4], LANE), lanes)
    copies = [pltpu.make_async_copy(guess, guess_in, sems.at[0])]
    for slot, ref in enumerate((cond_x, cond_y, source)):
        copies.append(pltpu.make_async_copy(ref.at[:, around], coefs_in.at[slot], sems.at[1 + slot]))
    copies.append(pltpu.make_async_copy(inflow.at[:, coarse_at], coarse, sems.at[4]))
    for copy in copies:
        copy.start()
    copies[0].wait()
    for block in range(blocks):
        start = min(max(own * block - SIDE, 0), columns - lanes)
        send[block] = guess_in[:, start : start + lanes]
    for copy in copies[1:]:
        copy.wait()
    for slot in range(3):
        for chunk in range(lanes // LANE):
            coefs[slot, :, piece(chunk)] = shifted(lambda k: coefs_in[slot, :, piece(k)], chunk, ids[1])

    def fill(bottom, top):
        at = 0
        for slot, deep in enumerate(COEF_ROWS):
            bottom[at : at + deep] = coefs[slot, rows - deep :]
            top[at : at + deep] = coefs[slot, :deep]
            at += deep
        bottom[at:] = coarse[rows // 2 - COARSE_ROWS :]
        top[at:] = coarse[:COARSE_ROWS]

    @pl.when(ids[2] == 1)
    def _():
        fill(halo_a, halo_b)

    @pl.when(ids[2] == 0)
    def _():
        fill(halo_b, halo_a)


def edge_kernel(ids, fields, edge_a, edge_b):
    rows = fields.shape[1]

    def fill(bottom, top):
        at = 0
        for group, deep in enumerate(FIELD_ROWS):
            bottom[at : at + deep] = fields[group, rows - deep :]
            top[at : at + deep] = fields[group, :deep]
            at += deep

    @pl.when(ids[2] == 1)
    def _():
        fill(edge_a, edge_b)

    @pl.when(ids[2] == 0)
    def _():
        fill(edge_b, edge_a)


def spread(value):
    rows, lanes = value.shape
    value = value.reshape(rows // 8, 8, lanes)
    row_even = lax.broadcasted_iota(jnp.int32, value.shape, 1) % 2 == 0
    lane_even = lax.broadcasted_iota(jnp.int32, value.shape, 2) % 2 == 0
    value = value + jnp.where(row_even, pltpu.roll(value, 7, 1), pltpu.roll(value, 1, 1))
    value = value + jnp.where(lane_even, pltpu.roll(value, lanes - 1, 2), pltpu.roll(value, 1, 2))
    return (value * 0.25).reshape(rows, lanes)


def prepare_kernel(ids, coefs, coarse, coef_a, coef_b, cond_x, cond_y, source, coarse_x, coarse_y, error, tall):
    rows, lanes = coefs.shape[1:]
    chunks = lanes // LANE
    low = HALO + rows
    targets = (cond_x, cond_y, source)

    def assemble(upper, lower):
        at = 0
        for ref, deep in zip(targets, COEF_ROWS):
            for chunk in range(chunks):
                ref[chunk, HALO - deep : HALO] = upper[at : at + deep, piece(chunk)]
                ref[chunk, low : low + deep] = lower[at : at + deep, piece(chunk)]
            at += deep
        tall[:COARSE_ROWS] = upper[at:]
        tall[COARSE_ROWS + rows // 2 :] = lower[at:]

    @pl.when(ids[2] == 1)
    def _():
        assemble(coef_b, coef_a)

    @pl.when(ids[2] == 0)
    def _():
        assemble(coef_a, coef_b)

    tall[COARSE_ROWS : COARSE_ROWS + rows // 2] = coarse[...]
    for slot, ref in enumerate(targets):
        for chunk in range(chunks):
            ref[chunk, HALO:low] = coefs[slot, :, piece(chunk)]
    span = slice(HALO - 8, low + 8)
    for chunk in range(chunks):
        coarse_x[chunk, span] = spread(cond_x[chunk, span])
        coarse_y[chunk, span] = spread(cond_y[chunk, span])
    high = rows // 2 + 2 * COARSE_ROWS
    half = lax.broadcasted_iota(jnp.int32, (8, LANE), 1) // 2
    twice = lax.broadcasted_iota(jnp.int32, (8, LANE), 0) // 2
    first, shift = ids[5], ids[6]

    def load(chunk):
        at = jnp.minimum((first + chunk) * LANE, lanes - LANE)
        return tall[:, pl.ds(pl.multiple_of(at, LANE), LANE)]

    for pair in range((chunks + 1) // 2):
        compact = shifted(load, pair, shift)
        for side in range(2):
            chunk = 2 * pair + side
            if chunk < chunks:
                for part in range(high // 8):
                    wide = jnp.take_along_axis(compact[8 * part : 8 * part + 8], half + side * (LANE // 2), axis=1)
                    for end in range(2):
                        at = HALO - 2 * COARSE_ROWS + 16 * part + 8 * end
                        error[chunk, at : at + 8] = jnp.take_along_axis(wide, twice + 4 * end, axis=0)


def sweep(items, cond_x, cond_y, width, limit):
    chunks = cond_x.shape[0]
    states = []
    for values, put, first, count, added in items:
        value = values[0, first : first + count]
        states.append((value, pltpu.roll(value, LANE - width, 1), jnp.zeros_like(value)))
    for chunk in range(chunks):
        for item, (values, put, first, count, added) in enumerate(items):
            value, east, west_flux = states[item]
            lane = lax.broadcasted_iota(jnp.int32, value.shape, 1)
            row = lax.broadcasted_iota(jnp.int32, value.shape, 0)
            here = slice(first, first + count)
            above = slice(first - width, first - width + count)
            below = slice(first + width, first + width + count)
            if chunk + 1 < chunks:
                next_value = values[chunk + 1, here]
                next_east = pltpu.roll(next_value, LANE - width, 1)
            else:
                next_value, next_east = None, jnp.zeros_like(value)
            beside = jnp.where(lane >= LANE - width, next_east, east)
            flux_y = cond_y[chunk, here] * (beside - value)
            rolled = pltpu.roll(flux_y, width, 1)
            flux_w = jnp.where(lane < width, west_flux, rolled)
            flux_x = cond_x[chunk, here] * (values[chunk, below] - value)
            flux_u = cond_x[chunk, above] * (value - values[chunk, above])
            result = value + ((flux_x - flux_u) + (flux_y - flux_w)) + added(chunk, here)
            put[chunk, here] = jnp.where(row < limit - first, result, 0.0)
            states[item] = (next_value, next_east, rolled)


def reach(rows, deep):
    return HALO - deep, (rows + 2 * deep + 7) // 8 * 8


def main_kernel(
    ids, fields, cond_x, cond_y, source, coarse_x, coarse_y, start_error, edge_a, edge_b, out,
    guess, work, first_pass, second_pass, error,
):
    groups, rows, lanes = fields.shape
    chunks = lanes // LANE
    low = HALO + rows
    limit = jnp.where(ids[3] == 1, low, low + HALO)

    def assemble(upper, lower):
        at = 0
        for group, deep in enumerate(FIELD_ROWS):
            for chunk in range(chunks):
                guess[group, chunk, HALO - deep : HALO] = upper[at : at + deep, piece(chunk)]
                guess[group, chunk, low : low + deep] = lower[at : at + deep, piece(chunk)]
            at += deep

    @pl.when(ids[2] == 1)
    def _():
        assemble(edge_b, edge_a)

    @pl.when(ids[2] == 0)
    def _():
        assemble(edge_a, edge_b)

    for group in range(groups - 1):
        for chunk in range(chunks):
            guess[group, chunk, HALO:low] = fields[group, :, piece(chunk)]

    def add_source(chunk, here):
        return source[chunk, here]

    def propagate_all(starts, ends, deeps):
        for number in range(FINE_STEPS):
            items = []
            for slot, (start, end, deep) in enumerate(zip(starts, ends, deeps)):
                before = start if number == 0 else work.at[slot, number % 2]
                after = end if number == FINE_STEPS - 1 else work.at[slot, (number + 1) % 2]
                items.append((before, after, *reach(rows, deep + FINE_STEPS - 1 - number), add_source))
            sweep(items, cond_x, cond_y, 1, limit)

    propagate_all([guess.at[g] for g in range(3)], [first_pass.at[g] for g in range(3)], (6, 4, 0))
    propagate_all([first_pass.at[g] for g in range(2)], [second_pass.at[g] for g in range(2)], (2, 0))

    ends = (first_pass.at[0], second_pass.at[0], second_pass.at[1])
    for group in range(1, groups):
        reached, relaxed = ends[group - 1], first_pass.at[group - 1]
        before = start_error if group == 1 else error.at[group - 2]

        def residual(chunk, here, reached=reached, relaxed=relaxed):
            return spread(reached[chunk, here] - relaxed[chunk, here])

        sweep(
            [(before, error.at[group - 1], *reach(rows, 2 * (groups - 1 - group)), residual)],
            coarse_x, coarse_y, 2, limit,
        )

    for group in range(groups):
        relaxed = guess.at[0] if group == 0 else first_pass.at[group - 1]
        correction = start_error if group == 0 else error.at[group - 1]

        def load(chunk):
            return relaxed[chunk, HALO:low] + correction[chunk, HALO:low]

        for chunk in range(chunks - 1):
            out[group, :, piece(chunk)] = shifted(load, chunk, ids[1])


def unpack_kernel(blocks, out, sems):
    own = blocks.shape[2]
    copies = []
    for block in range(blocks.shape[0]):
        target = out.at[0, :, block * own : (block + 1) * own]
        copies.append(pltpu.make_async_copy(blocks.at[block], target, sems.at[block]))
    for copy in copies:
        copy.start()
    for copy in copies:
        copy.wait()


def call(kernel, outs, scratch, operands, whole=(), outside=False, copies=0):
    vmem, smem, anywhere = (pl.BlockSpec(memory_space=space) for space in (pltpu.VMEM, pltpu.SMEM, pl.ANY))
    specs = [
        anywhere if slot in whole else smem if value.dtype == jnp.int32 else vmem
        for slot, value in enumerate(operands)
    ]
    return pl.pallas_call(
        kernel,
        out_shape=[jax.ShapeDtypeStruct(shape, jnp.float32) for shape in outs],
        in_specs=specs,
        out_specs=[anywhere if outside else vmem] * len(outs),
        scratch_shapes=[pltpu.VMEM(shape, jnp.float32) for shape in scratch]
        + ([pltpu.SemaphoreType.DMA((copies,))] if copies else []),
        compiler_params=pltpu.CompilerParams(vmem_limit_bytes=VMEM_LIMIT),
    )(*operands)


def shards(guesses, cond_x, cond_y, source, inflow):
    groups, strips = lax.axis_size("tm"), lax.axis_size("space")
    rows, columns = cond_x.shape
    fits = groups == len(FIELD_ROWS) + 1 and strips % 2 == 0 and rows == 16
    if not fits or columns % (2 * groups * LANE) != 0 or columns < 2 * groups * LANE:
        return general_shards(guesses, cond_x, cond_y, source, inflow)
    own = columns // groups
    lanes = own + 2 * SIDE
    chunks = lanes // LANE
    member, strip = lax.axis_index("tm"), lax.axis_index("space")
    start, around = window(member, own, columns, lanes)
    coarse_start = jnp.minimum(start // 2 // LANE * LANE, columns // 2 - lanes)
    coarse_skip = start // 2 - coarse_start
    last = (strip == strips - 1).astype(jnp.int32)
    ids = [around, start - around, 1 - strip % 2, last, coarse_start, coarse_skip // LANE, coarse_skip % LANE]
    ids = jnp.stack([jnp.asarray(value, jnp.int32) for value in ids])
    pairs_a = [(i, i ^ 1) for i in range(strips)]
    pairs_b = [(i, j) for k in range(1, strips - 1, 2) for i, j in ((k, k + 1), (k + 1, k))]

    travel = sum(COEF_ROWS) + COARSE_ROWS
    send, halo_a, halo_b, coefs, coarse = call(
        pack_kernel,
        [(groups, rows, lanes), (travel, lanes), (travel, lanes), (3, rows, lanes), (rows // 2, lanes)],
        [(rows, columns), (3, rows, lanes + LANE)],
        [ids, guesses[0], cond_x, cond_y, source, inflow], whole=range(1, 6), copies=5,
    )
    coef_b = lax.ppermute(halo_b, "space", pairs_b)
    coef_a = lax.ppermute(halo_a, "space", pairs_a)
    fields = lax.all_to_all(send, "tm", 0, 0, tiled=True)
    deep = sum(FIELD_ROWS)
    sent_a, sent_b = call(edge_kernel, [(deep, lanes)] * 2, [], [ids, fields])
    edge_b = lax.ppermute(sent_b, "space", pairs_b)
    edge_a = lax.ppermute(sent_a, "space", pairs_a)
    buffer = (chunks, rows + 2 * HALO, LANE)
    prepared = call(
        prepare_kernel, [buffer] * 6, [(rows // 2 + 2 * COARSE_ROWS, lanes)], [ids, coefs, coarse, coef_a, coef_b]
    )
    (blocks,) = call(
        main_kernel,
        [(groups, rows, own)],
        [(3, *buffer), (3, 2, *buffer), (3, *buffer), (2, *buffer), (3, *buffer)],
        [ids, fields, *prepared, edge_a, edge_b],
    )
    blocks = lax.all_to_all(blocks, "tm", 0, 0, tiled=True)
    return call(unpack_kernel, [(1, rows, columns)], [], [blocks], outside=True, copies=groups)[0]


def solution(mesh):
    return jax.shard_map(
        shards,
        mesh=mesh,
        in_specs=(
            P("tm", "space", None),
            P("space", None),
            P("space", None),
            P("space", None),
            P("space", None),
        ),
        out_specs=P("tm", "space", None),
        check_vma=False,
    )
```

```python
import functools

import jax
import jax.numpy as jnp
from jax import lax
from jax.experimental import pallas as pl
from jax.experimental.pallas import tpu as pltpu
from jax.sharding import PartitionSpec as P

FINE_STEPS = 4
LANE = 128
SIDE = 64
HALO = 16
COEF_ROWS = (10, 9, 9)
FIELD_ROWS = (12, 8, 4)
COARSE_ROWS = 4
VMEM_LIMIT = 40 * 1024 * 1024


def padded(value, sides, width):
    for axis, dim in sides:
        devices, length = (lax.axis_size(axis), value.shape[dim])
        up = [(i, (i + 1) % devices) for i in range(devices - 1)]
        down = [(j, i) for i, j in up]
        last = lax.slice_in_dim(value, length - width, length, axis=dim)
        leading = lax.slice_in_dim(value, 0, width, axis=dim)
        before = lax.ppermute(last, axis, up)
        after = lax.ppermute(leading, axis, down)
        value = jnp.concatenate([before, value, after], axis=dim)
    return value


def from_behind(value, axis, steps):
    count = lax.axis_size(axis)
    leading, last = (max(0, -steps), min(count, count - steps))
    return lax.ppermute(value, axis, [(source, source + steps) for source in range(leading, last)])


def interior(field_ext, cond_rows, cond_cols):
    centre = field_ext[1:-1]
    flux_sum = cond_rows[1:-1] * (field_ext[2:] - centre) - cond_rows[:-2] * (
        centre - field_ext[:-2]
    )
    widened = jnp.pad(centre, ((0, 0), (1, 1)))
    cond_own = cond_cols[1:-1]
    cond_west = jnp.pad(cond_own, ((0, 0), (1, 0)))[:, :-1]
    flux_sum = (
        flux_sum + cond_own * (widened[:, 2:] - centre) - cond_west * (centre - widened[:, :-2])
    )
    return centre + flux_sum


def propagate(field, coef_pad):
    strip_rows = field.shape[0]
    cond_rows = coef_pad[0, 3 : strip_rows + 5]
    cond_cols = coef_pad[1, 3 : strip_rows + 5]
    source_rows = coef_pad[2, 4 : strip_rows + 4]
    for section in range(FINE_STEPS):
        extended = padded(field, (("space", 0),), 1)
        field = interior(extended, cond_rows, cond_cols) + source_rows
    return field


def restrict(field):
    lead = field.shape[:-2]
    shaped = field.reshape(lead + (field.shape[-2] // 2, 2, field.shape[-1] // 2, 2))
    return jnp.mean(shaped, axis=(-3, -1))


def general_shards(guesses, cond_x, cond_y, source, inflow):
    strip_rows = cond_x.shape[0]
    columns = cond_x.shape[1]
    stacked = jnp.stack([cond_x, cond_y, source])
    edge_rows = from_behind(cond_x[strip_rows - 2 :], "space", 1)
    cond_upper = jnp.concatenate([jnp.zeros((2, columns), jnp.float32), edge_rows], axis=0)
    blank_rows = jnp.zeros((4, columns), jnp.float32)
    upper = jnp.stack([cond_upper, blank_rows, blank_rows])
    lower = jnp.zeros((3, 4, columns), jnp.float32)
    coef_pad = jnp.concatenate([upper, stacked, lower], axis=1)
    first_group = lax.axis_index("tm") == 0
    c_point = guesses[0]
    first_pass = propagate(c_point, coef_pad)
    received = from_behind(first_pass, "tm", 1)
    relaxed = jnp.where(first_group, c_point, received)
    second_pass = propagate(relaxed, coef_pad)
    fine_next = from_behind(second_pass, "tm", 1)
    residual = restrict(fine_next - relaxed)
    residual = jnp.where(first_group, 0.0, residual)
    coarse_coef = restrict(coef_pad[:2, 2 : strip_rows + 6])

    def chain_round(index, error_field):
        extended = padded(error_field, (("space", 0),), 1)
        stepped = interior(extended, coarse_coef[0], coarse_coef[1])
        arrived = from_behind(stepped, "tm", 1)
        return jnp.where(first_group, inflow, arrived + residual)

    start_error = jnp.where(first_group, inflow, jnp.zeros_like(residual))
    error_field = lax.fori_loop(0, lax.axis_size("tm") - 1, chain_round, start_error)
    widened = jnp.repeat(jnp.repeat(error_field, 2, axis=0), 2, axis=1)
    return (relaxed + widened)[None]


def window(index, own, columns, lanes):
    return jnp.clip(own * index - SIDE, 0, columns - lanes), jnp.clip(own * index - LANE, 0, columns - lanes - LANE)


def shifted(load, chunk, shift):
    amount = lax.rem(2 * LANE - shift, LANE)
    here = pltpu.roll(load(chunk), amount, 1)
    there = pltpu.roll(load(chunk + 1), amount, 1)
    lane = lax.broadcasted_iota(jnp.int32, here.shape, 1)
    return jnp.where(lane < LANE - shift, here, there)


def piece(chunk):
    return slice(chunk * LANE, (chunk + 1) * LANE)


def pack_kernel(
    ids, guess, cond_x, cond_y, source, inflow, send, halo_a, halo_b, coefs, coarse,
    guess_in, coefs_in, sems,
):
    blocks, rows, lanes = send.shape
    columns = guess.shape[1]
    own = columns // blocks
    around = pl.ds(pl.multiple_of(ids[0], LANE), lanes + LANE)
    coarse_at = pl.ds(pl.multiple_of(ids[4], LANE), lanes)
    copies = [pltpu.make_async_copy(guess, guess_in, sems.at[0])]
    for slot, ref in enumerate((cond_x, cond_y, source)):
        copies.append(pltpu.make_async_copy(ref.at[:, around], coefs_in.at[slot], sems.at[1 + slot]))
    copies.append(pltpu.make_async_copy(inflow.at[:, coarse_at], coarse, sems.at[4]))
    for copy in copies:
        copy.start()
    copies[0].wait()
    for block in range(blocks):
        start = min(max(own * block - SIDE, 0), columns - lanes)
        send[block] = guess_in[:, start : start + lanes]
    for copy in copies[1:]:
        copy.wait()
    for slot in range(3):
        for chunk in range(lanes // LANE):
            coefs[slot, :, piece(chunk)] = shifted(lambda k: coefs_in[slot, :, piece(k)], chunk, ids[1])

    def fill(bottom, top):
        at = 0
        for slot, deep in enumerate(COEF_ROWS):
            bottom[at : at + deep] = coefs[slot, rows - deep :]
            top[at : at + deep] = coefs[slot, :deep]
            at += deep
        bottom[at:] = coarse[rows // 2 - COARSE_ROWS :]
        top[at:] = coarse[:COARSE_ROWS]

    @pl.when(ids[2] == 1)
    def _():
        fill(halo_a, halo_b)

    @pl.when(ids[2] == 0)
    def _():
        fill(halo_b, halo_a)


def edge_kernel(ids, fields, edge_a, edge_b):
    rows = fields.shape[1]

    def fill(bottom, top):
        at = 0
        for group, deep in enumerate(FIELD_ROWS):
            bottom[at : at + deep] = fields[group, rows - deep :]
            top[at : at + deep] = fields[group, :deep]
            at += deep

    @pl.when(ids[2] == 1)
    def _():
        fill(edge_a, edge_b)

    @pl.when(ids[2] == 0)
    def _():
        fill(edge_b, edge_a)


def spread(value):
    rows, lanes = value.shape
    value = value.reshape(rows // 8, 8, lanes)
    row_even = lax.broadcasted_iota(jnp.int32, value.shape, 1) % 2 == 0
    lane_even = lax.broadcasted_iota(jnp.int32, value.shape, 2) % 2 == 0
    value = value + jnp.where(row_even, pltpu.roll(value, 7, 1), pltpu.roll(value, 1, 1))
    value = value + jnp.where(lane_even, pltpu.roll(value, lanes - 1, 2), pltpu.roll(value, 1, 2))
    return (value * 0.25).reshape(rows, lanes)


def weights(cond_x, cond_y, chunk, rows, width, limit, out):
    diagonal, up, east, west = out
    chunks = cond_x.shape[0]
    first, count = rows
    here = slice(first, first + count)
    own_x, own_y = cond_x[chunk, here], cond_y[chunk, here]
    above = cond_x[chunk, first - width : first - width + count]
    lane = lax.broadcasted_iota(jnp.int32, own_x.shape, 1)
    row = lax.broadcasted_iota(jnp.int32, own_x.shape, 0)
    before = pltpu.roll(cond_y[chunk - 1, here], width, 1) if chunk else jnp.zeros_like(own_y)
    beside = jnp.where(lane < width, before, pltpu.roll(own_y, width, 1))
    diagonal[chunk, here] = 1.0 - ((own_x + above) + (own_y + beside))
    up[chunk, here] = jnp.where(row < limit - first, above, 0.0)
    west[chunk, here] = beside
    east[chunk, here] = jnp.where(lane < LANE - width, own_y, 0.0) if chunk == chunks - 1 else own_y


def prepare_kernel(
    ids, coefs, coarse, coef_a, coef_b,
    cond_x, source, diagonal, up, east, west, coarse_x, coarse_d, coarse_u, coarse_e, coarse_w, error,
    cond_y, coarse_y, tall,
):
    rows, lanes = coefs.shape[1:]
    chunks = lanes // LANE
    low = HALO + rows
    limit = jnp.where(ids[3] == 1, low, low + HALO)
    targets = (cond_x, cond_y, source)

    def assemble(upper, lower):
        at = 0
        for ref, deep in zip(targets, COEF_ROWS):
            for chunk in range(chunks):
                ref[chunk, HALO - deep : HALO] = upper[at : at + deep, piece(chunk)]
                ref[chunk, low : low + deep] = lower[at : at + deep, piece(chunk)]
            at += deep
        tall[:COARSE_ROWS] = upper[at:]
        tall[COARSE_ROWS + rows // 2 :] = lower[at:]

    @pl.when(ids[2] == 1)
    def _():
        assemble(coef_b, coef_a)

    @pl.when(ids[2] == 0)
    def _():
        assemble(coef_a, coef_b)

    tall[COARSE_ROWS : COARSE_ROWS + rows // 2] = coarse[...]
    for slot, ref in enumerate(targets):
        for chunk in range(chunks):
            ref[chunk, HALO:low] = coefs[slot, :, piece(chunk)]
    for chunk in range(chunks):
        weights(cond_x, cond_y, chunk, reach(rows, 9), 1, limit, (diagonal, up, east, west))
    span = slice(HALO - 8, low + 8)
    for chunk in range(chunks):
        coarse_x[chunk, span] = spread(cond_x[chunk, span])
        coarse_y[chunk, span] = spread(cond_y[chunk, span])
    for chunk in range(chunks):
        weights(coarse_x, coarse_y, chunk, reach(rows, 4), 2, limit, (coarse_d, coarse_u, coarse_e, coarse_w))
    high = rows // 2 + 2 * COARSE_ROWS
    half = lax.broadcasted_iota(jnp.int32, (8, LANE), 1) // 2
    twice = lax.broadcasted_iota(jnp.int32, (8, LANE), 0) // 2
    first, shift = ids[5], ids[6]

    def load(chunk):
        at = jnp.minimum((first + chunk) * LANE, lanes - LANE)
        return tall[:, pl.ds(pl.multiple_of(at, LANE), LANE)]

    for pair in range((chunks + 1) // 2):
        compact = shifted(load, pair, shift)
        for side in range(2):
            chunk = 2 * pair + side
            if chunk < chunks:
                for part in range(high // 8):
                    wide = jnp.take_along_axis(compact[8 * part : 8 * part + 8], half + side * (LANE // 2), axis=1)
                    for end in range(2):
                        at = HALO - 2 * COARSE_ROWS + 16 * part + 8 * end
                        error[chunk, at : at + 8] = jnp.take_along_axis(wide, twice + 4 * end, axis=0)


def sweep(values, put, rows, width, factors, added):
    diagonal, up, down, east, west = factors
    chunks = diagonal.shape[0]
    first, count = rows
    here = slice(first, first + count)
    above = slice(first - width, first - width + count)
    below = slice(first + width, first + width + count)
    lane = lax.broadcasted_iota(jnp.int32, (count, LANE), 1)

    def load(chunk):
        value = values[chunk, here]
        return value, pltpu.roll(value, LANE - width, 1), pltpu.roll(value, width, 1)

    before, now, after = None, load(0), None
    for chunk in range(chunks):
        after = load(chunk + 1) if chunk + 1 < chunks else None
        value, right, left = now
        if after is not None:
            right = jnp.where(lane < LANE - width, right, after[1])
        if before is not None:
            left = jnp.where(lane < width, before[2], left)
        across = east[chunk, here] * right + west[chunk, here] * left
        along = down[chunk, here] * values[chunk, below] + up[chunk, here] * values[chunk, above]
        put[chunk, here] = (diagonal[chunk, here] * value + added(chunk, here)) + (across + along)
        before, now = now, after


def reach(rows, deep):
    return HALO - deep, (rows + 2 * deep + 7) // 8 * 8


def main_kernel(
    ids, fields, cond_x, source, diagonal, up, east, west, coarse_x, coarse_d, coarse_u, coarse_e, coarse_w,
    start_error, edge_a, edge_b, out,
    guess, work, error,
):
    groups, rows, lanes = fields.shape
    chunks = lanes // LANE
    low = HALO + rows
    given = groups - 1

    def assemble(upper, lower):
        at = 0
        for group, deep in enumerate(FIELD_ROWS):
            for chunk in range(chunks):
                guess[group, chunk, HALO - deep : HALO] = upper[at : at + deep, piece(chunk)]
                guess[group, chunk, low : low + deep] = lower[at : at + deep, piece(chunk)]
            at += deep

    @pl.when(ids[2] == 1)
    def _():
        assemble(edge_b, edge_a)

    @pl.when(ids[2] == 0)
    def _():
        assemble(edge_a, edge_b)

    for group in range(given):
        for chunk in range(chunks):
            guess[group, chunk, HALO:low] = fields[group, :, piece(chunk)]
    span = slice(HALO - 8, low + 8)
    error[0, :, span] = start_error[:, span]

    fine = (diagonal, up, cond_x, east, west)
    coarse = (coarse_d, coarse_u, coarse_x, coarse_e, coarse_w)

    def add_source(chunk, here):
        return source[chunk, here]

    def propagate(slot, deep):
        stops = [guess.at[slot], work.at[0], work.at[1], work.at[0], guess.at[slot + given]]
        for number in range(FINE_STEPS):
            reached = reach(rows, deep + FINE_STEPS - 1 - number)
            sweep(stops[number], stops[number + 1], reached, 1, fine, add_source)

    @pl.loop(0, given)
    def _(group):
        propagate(group, 6)

    @pl.loop(given, 2 * given - 1)
    def _(group):
        propagate(group, 2)

    @pl.loop(1, groups)
    def _(group):
        reached = jnp.where(group == 1, given, 2 * given - 2 + group)
        relaxed = given - 1 + group

        def residual(chunk, here):
            return spread(guess[reached, chunk, here] - guess[relaxed, chunk, here])

        sweep(error.at[group - 1], error.at[group], reach(rows, 4), 2, coarse, residual)

    @pl.loop(0, groups)
    def _(group):
        relaxed = jnp.where(group == 0, 0, given - 1 + group)

        def load(chunk):
            return guess[relaxed, chunk, HALO:low] + error[group, chunk, HALO:low]

        for chunk in range(chunks - 1):
            out[group, :, piece(chunk)] = shifted(load, chunk, ids[1])


def unpack_kernel(blocks, out, sems):
    own = blocks.shape[2]
    copies = []
    for block in range(blocks.shape[0]):
        target = out.at[0, :, block * own : (block + 1) * own]
        copies.append(pltpu.make_async_copy(blocks.at[block], target, sems.at[block]))
    for copy in copies:
        copy.start()
    for copy in copies:
        copy.wait()


def call(kernel, outs, scratch, operands, whole=(), outside=False, copies=0):
    vmem, smem, anywhere = (pl.BlockSpec(memory_space=space) for space in (pltpu.VMEM, pltpu.SMEM, pltpu.HBM))
    specs = [
        anywhere if slot in whole else smem if value.dtype == jnp.int32 else vmem
        for slot, value in enumerate(operands)
    ]
    return pl.pallas_call(
        kernel,
        out_shape=[jax.ShapeDtypeStruct(shape, jnp.float32) for shape in outs],
        in_specs=specs,
        out_specs=[anywhere if outside else vmem] * len(outs),
        scratch_shapes=[pltpu.VMEM(shape, jnp.float32) for shape in scratch]
        + ([pltpu.SemaphoreType.DMA((copies,))] if copies else []),
        compiler_params=pltpu.CompilerParams(vmem_limit_bytes=VMEM_LIMIT),
    )(*operands)


def shards(guesses, cond_x, cond_y, source, inflow):
    groups, strips = lax.axis_size("tm"), lax.axis_size("space")
    rows, columns = cond_x.shape
    fits = groups == len(FIELD_ROWS) + 1 and strips % 2 == 0 and rows == 16
    if not fits or columns % (2 * groups * LANE) != 0 or columns < 2 * groups * LANE:
        return general_shards(guesses, cond_x, cond_y, source, inflow)
    own = columns // groups
    lanes = own + 2 * SIDE
    chunks = lanes // LANE
    member, strip = lax.axis_index("tm"), lax.axis_index("space")
    start, around = window(member, own, columns, lanes)
    coarse_start = jnp.minimum(start // 2 // LANE * LANE, columns // 2 - lanes)
    coarse_skip = start // 2 - coarse_start
    last = (strip == strips - 1).astype(jnp.int32)
    ids = [around, start - around, 1 - strip % 2, last, coarse_start, coarse_skip // LANE, coarse_skip % LANE]
    ids = jnp.stack([jnp.asarray(value, jnp.int32) for value in ids])
    pairs_a = [(i, i ^ 1) for i in range(strips)]
    pairs_b = [(i, j) for k in range(1, strips - 1, 2) for i, j in ((k, k + 1), (k + 1, k))]

    travel = sum(COEF_ROWS) + COARSE_ROWS
    send, halo_a, halo_b, coefs, coarse = call(
        pack_kernel,
        [(groups, rows, lanes), (travel, lanes), (travel, lanes), (3, rows, lanes), (rows // 2, lanes)],
        [(rows, columns), (3, rows, lanes + LANE)],
        [ids, guesses[0], cond_x, cond_y, source, inflow], whole=range(1, 6), copies=5,
    )
    coef_b = lax.ppermute(halo_b, "space", pairs_b)
    coef_a = lax.ppermute(halo_a, "space", pairs_a)
    fields = lax.all_to_all(send, "tm", 0, 0, tiled=True)
    deep = sum(FIELD_ROWS)
    sent_a, sent_b = call(edge_kernel, [(deep, lanes)] * 2, [], [ids, fields])
    edge_b = lax.ppermute(sent_b, "space", pairs_b)
    edge_a = lax.ppermute(sent_a, "space", pairs_a)
    buffer = (chunks, rows + 2 * HALO, LANE)
    prepared = call(
        prepare_kernel,
        [buffer] * 12,
        [buffer, buffer, (rows // 2 + 2 * COARSE_ROWS, lanes)],
        [ids, coefs, coarse, coef_a, coef_b],
    )
    (blocks,) = call(
        main_kernel,
        [(groups, rows, own)],
        [(3 * groups - 4, *buffer), (2, *buffer), (groups, *buffer)],
        [ids, fields, *prepared, edge_a, edge_b],
    )
    blocks = lax.all_to_all(blocks, "tm", 0, 0, tiled=True)
    return call(unpack_kernel, [(1, rows, columns)], [], [blocks], outside=True, copies=groups)[0]


def solution(mesh):
    return jax.shard_map(
        shards,
        mesh=mesh,
        in_specs=(
            P("tm", "space", None),
            P("space", None),
            P("space", None),
            P("space", None),
            P("space", None),
        ),
        out_specs=P("tm", "space", None),
        check_vma=False,
    )
```

```python
import functools

import jax
import jax.numpy as jnp
from jax import lax
from jax.experimental import pallas as pl
from jax.experimental.pallas import tpu as pltpu
from jax.sharding import PartitionSpec as P

FINE_STEPS = 4
LANE = 128
SIDE = 64
HALO = 16
COEF_ROWS = (10, 9, 9)
FIELD_ROWS = (12, 8, 4)
COARSE_ROWS = 4
VMEM_LIMIT = 40 * 1024 * 1024


def padded(value, sides, width):
    for axis, dim in sides:
        devices, length = (lax.axis_size(axis), value.shape[dim])
        up = [(i, (i + 1) % devices) for i in range(devices - 1)]
        down = [(j, i) for i, j in up]
        last = lax.slice_in_dim(value, length - width, length, axis=dim)
        leading = lax.slice_in_dim(value, 0, width, axis=dim)
        before = lax.ppermute(last, axis, up)
        after = lax.ppermute(leading, axis, down)
        value = jnp.concatenate([before, value, after], axis=dim)
    return value


def from_behind(value, axis, steps):
    count = lax.axis_size(axis)
    leading, last = (max(0, -steps), min(count, count - steps))
    return lax.ppermute(value, axis, [(source, source + steps) for source in range(leading, last)])


def interior(field_ext, cond_rows, cond_cols):
    centre = field_ext[1:-1]
    flux_sum = cond_rows[1:-1] * (field_ext[2:] - centre) - cond_rows[:-2] * (
        centre - field_ext[:-2]
    )
    widened = jnp.pad(centre, ((0, 0), (1, 1)))
    cond_own = cond_cols[1:-1]
    cond_west = jnp.pad(cond_own, ((0, 0), (1, 0)))[:, :-1]
    flux_sum = (
        flux_sum + cond_own * (widened[:, 2:] - centre) - cond_west * (centre - widened[:, :-2])
    )
    return centre + flux_sum


def propagate(field, coef_pad):
    strip_rows = field.shape[0]
    cond_rows = coef_pad[0, 3 : strip_rows + 5]
    cond_cols = coef_pad[1, 3 : strip_rows + 5]
    source_rows = coef_pad[2, 4 : strip_rows + 4]
    for section in range(FINE_STEPS):
        extended = padded(field, (("space", 0),), 1)
        field = interior(extended, cond_rows, cond_cols) + source_rows
    return field


def restrict(field):
    lead = field.shape[:-2]
    shaped = field.reshape(lead + (field.shape[-2] // 2, 2, field.shape[-1] // 2, 2))
    return jnp.mean(shaped, axis=(-3, -1))


def general_shards(guesses, cond_x, cond_y, source, inflow):
    strip_rows = cond_x.shape[0]
    columns = cond_x.shape[1]
    stacked = jnp.stack([cond_x, cond_y, source])
    edge_rows = from_behind(cond_x[strip_rows - 2 :], "space", 1)
    cond_upper = jnp.concatenate([jnp.zeros((2, columns), jnp.float32), edge_rows], axis=0)
    blank_rows = jnp.zeros((4, columns), jnp.float32)
    upper = jnp.stack([cond_upper, blank_rows, blank_rows])
    lower = jnp.zeros((3, 4, columns), jnp.float32)
    coef_pad = jnp.concatenate([upper, stacked, lower], axis=1)
    first_group = lax.axis_index("tm") == 0
    c_point = guesses[0]
    first_pass = propagate(c_point, coef_pad)
    received = from_behind(first_pass, "tm", 1)
    relaxed = jnp.where(first_group, c_point, received)
    second_pass = propagate(relaxed, coef_pad)
    fine_next = from_behind(second_pass, "tm", 1)
    residual = restrict(fine_next - relaxed)
    residual = jnp.where(first_group, 0.0, residual)
    coarse_coef = restrict(coef_pad[:2, 2 : strip_rows + 6])

    def chain_round(index, error_field):
        extended = padded(error_field, (("space", 0),), 1)
        stepped = interior(extended, coarse_coef[0], coarse_coef[1])
        arrived = from_behind(stepped, "tm", 1)
        return jnp.where(first_group, inflow, arrived + residual)

    start_error = jnp.where(first_group, inflow, jnp.zeros_like(residual))
    error_field = lax.fori_loop(0, lax.axis_size("tm") - 1, chain_round, start_error)
    widened = jnp.repeat(jnp.repeat(error_field, 2, axis=0), 2, axis=1)
    return (relaxed + widened)[None]


def place(groups, strips, columns, member):
    own = columns // groups
    lanes = own + 2 * SIDE
    start = jnp.clip(own * member - SIDE, 0, columns - lanes)
    around = jnp.clip(own * member - LANE, 0, columns - lanes - LANE)
    coarse = jnp.minimum(start // 2 // LANE * LANE, columns // 2 - lanes)
    return around, start - around, coarse, start // 2 - coarse


def sides(rows):
    strip, strips = lax.axis_index("space"), lax.axis_size("space")
    return lax.rem(strip, 2) == 0, jnp.where(strip == strips - 1, HALO + rows, 2 * HALO + rows)


def by_side(even, fill, first, second):
    @pl.when(even)
    def _():
        fill(first, second)

    @pl.when(jnp.logical_not(even))
    def _():
        fill(second, first)


def shifted(load, chunk, shift):
    amount = lax.rem(2 * LANE - shift, LANE)
    here = pltpu.roll(load(chunk), amount, 1)
    there = pltpu.roll(load(chunk + 1), amount, 1)
    lane = lax.broadcasted_iota(jnp.int32, here.shape, 1)
    return jnp.where(lane < LANE - shift, here, there)


def piece(chunk):
    return slice(chunk * LANE, (chunk + 1) * LANE)


def pack_kernel(
    guess, cond_x, cond_y, source, inflow, own, to_core, to_x, to_both, halo_a, halo_b, coefs, coarse,
    guess_in, coefs_in, sems,
):
    rows, lanes = own.shape
    columns = guess.shape[1]
    chunks = lanes // LANE
    groups, strips, member = lax.axis_size("tm"), lax.axis_size("space"), lax.axis_index("tm")
    outs = (own, to_core, to_x, to_both)
    copies, shifts = [], []
    for slot in range(groups):
        around, shift, _, _ = place(groups, strips, columns, member ^ slot)
        at = pl.ds(pl.multiple_of(around, LANE), lanes + LANE)
        copies.append(pltpu.make_async_copy(guess.at[:, at], guess_in.at[slot], sems.at[slot]))
        shifts.append(shift)
    around, shift, coarse_at, _ = place(groups, strips, columns, member)
    at = pl.ds(pl.multiple_of(around, LANE), lanes + LANE)
    for slot, ref in enumerate((cond_x, cond_y, source)):
        copies.append(pltpu.make_async_copy(ref.at[:, at], coefs_in.at[slot], sems.at[groups + slot]))
    at = pl.ds(pl.multiple_of(coarse_at, LANE), lanes)
    copies.append(pltpu.make_async_copy(inflow.at[:, at], coarse, sems.at[groups + 3]))
    for copy in copies:
        copy.start()
    for slot in range(groups):
        copies[slot].wait()
        for chunk in range(chunks):
            outs[slot][:, piece(chunk)] = shifted(lambda k: guess_in[slot, :, piece(k)], chunk, shifts[slot])
    for copy in copies[groups:]:
        copy.wait()
    for slot in range(3):
        for chunk in range(chunks):
            coefs[slot, :, piece(chunk)] = shifted(lambda k: coefs_in[slot, :, piece(k)], chunk, shift)

    def fill(bottom, top):
        at = 0
        for slot, deep in enumerate(COEF_ROWS):
            bottom[at : at + deep] = coefs[slot, rows - deep :]
            top[at : at + deep] = coefs[slot, :deep]
            at += deep
        bottom[at:] = coarse[rows // 2 - COARSE_ROWS :]
        top[at:] = coarse[:COARSE_ROWS]

    by_side(sides(rows)[0], fill, halo_a, halo_b)


def edge_kernel(own, from_core, from_x, from_both, edge_a, edge_b, fields):
    member = lax.axis_index("tm")
    for slot, ref in enumerate((own, from_core, from_x, from_both)):
        fields[member ^ slot] = ref[...]
    rows = own.shape[0]

    def fill(bottom, top):
        at = 0
        for group, deep in enumerate(FIELD_ROWS):
            bottom[at : at + deep] = fields[group, rows - deep :]
            top[at : at + deep] = fields[group, :deep]
            at += deep

    by_side(sides(rows)[0], fill, edge_a, edge_b)


def spread(value):
    rows, lanes = value.shape
    value = value.reshape(rows // 8, 8, lanes)
    row_even = lax.broadcasted_iota(jnp.int32, value.shape, 1) % 2 == 0
    lane_even = lax.broadcasted_iota(jnp.int32, value.shape, 2) % 2 == 0
    value = value + jnp.where(row_even, pltpu.roll(value, 7, 1), pltpu.roll(value, 1, 1))
    value = value + jnp.where(lane_even, pltpu.roll(value, lanes - 1, 2), pltpu.roll(value, 1, 2))
    return (value * 0.25).reshape(rows, lanes)


def weights(cond_x, cond_y, chunk, rows, width, limit, out):
    diagonal, up, east, west = out
    chunks = cond_x.shape[0]
    first, count = rows
    here = slice(first, first + count)
    own_x, own_y = cond_x[chunk, here], cond_y[chunk, here]
    above = cond_x[chunk, first - width : first - width + count]
    lane = lax.broadcasted_iota(jnp.int32, own_x.shape, 1)
    row = lax.broadcasted_iota(jnp.int32, own_x.shape, 0)
    before = pltpu.roll(cond_y[chunk - 1, here], width, 1) if chunk else jnp.zeros_like(own_y)
    beside = jnp.where(lane < width, before, pltpu.roll(own_y, width, 1))
    diagonal[chunk, here] = 1.0 - ((own_x + above) + (own_y + beside))
    up[chunk, here] = jnp.where(row < limit - first, above, 0.0)
    west[chunk, here] = beside
    east[chunk, here] = jnp.where(lane < LANE - width, own_y, 0.0) if chunk == chunks - 1 else own_y


def prepare_kernel(
    coefs, coarse, coef_a, coef_b,
    cond_x, source, diagonal, up, east, west, coarse_x, coarse_d, coarse_u, coarse_e, coarse_w, error,
    cond_y, coarse_y, tall,
):
    rows, lanes = coefs.shape[1:]
    chunks = lanes // LANE
    low = HALO + rows
    even, limit = sides(rows)
    targets = (cond_x, cond_y, source)

    def assemble(upper, lower):
        at = 0
        for ref, deep in zip(targets, COEF_ROWS):
            for chunk in range(chunks):
                ref[chunk, HALO - deep : HALO] = upper[at : at + deep, piece(chunk)]
                ref[chunk, low : low + deep] = lower[at : at + deep, piece(chunk)]
            at += deep
        tall[:COARSE_ROWS] = upper[at:]
        tall[COARSE_ROWS + rows // 2 :] = lower[at:]

    by_side(even, lambda lower, upper: assemble(upper, lower), coef_a, coef_b)

    tall[COARSE_ROWS : COARSE_ROWS + rows // 2] = coarse[...]
    for slot, ref in enumerate(targets):
        for chunk in range(chunks):
            ref[chunk, HALO:low] = coefs[slot, :, piece(chunk)]
    for chunk in range(chunks):
        weights(cond_x, cond_y, chunk, reach(rows, 9), 1, limit, (diagonal, up, east, west))
    span = slice(HALO - 8, low + 8)
    for chunk in range(chunks):
        coarse_x[chunk, span] = spread(cond_x[chunk, span])
        coarse_y[chunk, span] = spread(cond_y[chunk, span])
    for chunk in range(chunks):
        weights(coarse_x, coarse_y, chunk, reach(rows, 4), 2, limit, (coarse_d, coarse_u, coarse_e, coarse_w))
    high = rows // 2 + 2 * COARSE_ROWS
    half = lax.broadcasted_iota(jnp.int32, (8, LANE), 1) // 2
    twice = lax.broadcasted_iota(jnp.int32, (8, LANE), 0) // 2
    groups, strips, member = lax.axis_size("tm"), lax.axis_size("space"), lax.axis_index("tm")
    skip = place(groups, strips, groups * (lanes - 2 * SIDE), member)[3]
    first, shift = skip // LANE, lax.rem(skip, LANE)

    def load(chunk):
        at = jnp.minimum((first + chunk) * LANE, lanes - LANE)
        return tall[:, pl.ds(pl.multiple_of(at, LANE), LANE)]

    for pair in range((chunks + 1) // 2):
        compact = shifted(load, pair, shift)
        for side in range(2):
            chunk = 2 * pair + side
            if chunk < chunks:
                for part in range(high // 8):
                    wide = jnp.take_along_axis(compact[8 * part : 8 * part + 8], half + side * (LANE // 2), axis=1)
                    for end in range(2):
                        at = HALO - 2 * COARSE_ROWS + 16 * part + 8 * end
                        error[chunk, at : at + 8] = jnp.take_along_axis(wide, twice + 4 * end, axis=0)


def sweep(values, put, rows, width, factors, added):
    diagonal, up, down, east, west = factors
    chunks = diagonal.shape[0]
    first, count = rows
    here = slice(first, first + count)
    above = slice(first - width, first - width + count)
    below = slice(first + width, first + width + count)
    lane = lax.broadcasted_iota(jnp.int32, (count, LANE), 1)

    def load(chunk):
        value = values[chunk, here]
        return value, pltpu.roll(value, LANE - width, 1), pltpu.roll(value, width, 1)

    before, now, after = None, load(0), None
    for chunk in range(chunks):
        after = load(chunk + 1) if chunk + 1 < chunks else None
        value, right, left = now
        if after is not None:
            right = jnp.where(lane < LANE - width, right, after[1])
        if before is not None:
            left = jnp.where(lane < width, before[2], left)
        across = east[chunk, here] * right + west[chunk, here] * left
        along = down[chunk, here] * values[chunk, below] + up[chunk, here] * values[chunk, above]
        put[chunk, here] = (diagonal[chunk, here] * value + added(chunk, here)) + (across + along)
        before, now = now, after


def reach(rows, deep):
    return HALO - deep, (rows + 2 * deep + 7) // 8 * 8


def main_kernel(
    fields, cond_x, source, diagonal, up, east, west, coarse_x, coarse_d, coarse_u, coarse_e, coarse_w,
    start_error, edge_a, edge_b, own, to_core, to_x, to_both,
    guess, work, error,
):
    groups, rows, lanes = fields.shape
    chunks = lanes // LANE
    low = HALO + rows
    given = groups - 1

    def assemble(upper, lower):
        at = 0
        for group, deep in enumerate(FIELD_ROWS):
            for chunk in range(chunks):
                guess[group, chunk, HALO - deep : HALO] = upper[at : at + deep, piece(chunk)]
                guess[group, chunk, low : low + deep] = lower[at : at + deep, piece(chunk)]
            at += deep

    by_side(sides(rows)[0], lambda lower, upper: assemble(upper, lower), edge_a, edge_b)

    for group in range(given):
        for chunk in range(chunks):
            guess[group, chunk, HALO:low] = fields[group, :, piece(chunk)]
    span = slice(HALO - 8, low + 8)
    error[0, :, span] = start_error[:, span]

    fine = (diagonal, up, cond_x, east, west)
    coarse = (coarse_d, coarse_u, coarse_x, coarse_e, coarse_w)

    def add_source(chunk, here):
        return source[chunk, here]

    def propagate(slot, deep):
        stops = [guess.at[slot], work.at[0], work.at[1], work.at[0], guess.at[slot + given]]
        for number in range(FINE_STEPS):
            reached = reach(rows, deep + FINE_STEPS - 1 - number)
            sweep(stops[number], stops[number + 1], reached, 1, fine, add_source)

    @pl.loop(0, given)
    def _(group):
        propagate(group, 6)

    @pl.loop(given, 2 * given - 1)
    def _(group):
        propagate(group, 2)

    @pl.loop(1, groups)
    def _(group):
        reached = jnp.where(group == 1, given, 2 * given - 2 + group)
        relaxed = given - 1 + group

        def residual(chunk, here):
            return spread(guess[reached, chunk, here] - guess[relaxed, chunk, here])

        sweep(error.at[group - 1], error.at[group], reach(rows, 4), 2, coarse, residual)

    member = lax.axis_index("tm")
    shift = place(groups, lax.axis_size("space"), groups * own.shape[1], member)[1]
    for slot, out in enumerate((own, to_core, to_x, to_both)):
        group = member ^ slot
        relaxed = jnp.where(group == 0, 0, given - 1 + group)

        def load(chunk):
            return guess[relaxed, chunk, HALO:low] + error[group, chunk, HALO:low]

        for chunk in range(chunks - 1):
            out[:, piece(chunk)] = shifted(load, chunk, shift)


def unpack_kernel(own, from_core, from_x, from_both, out, sems):
    width = own.shape[1]
    member = lax.axis_index("tm")
    copies = []
    for slot, ref in enumerate((own, from_core, from_x, from_both)):
        at = pl.ds(pl.multiple_of((member ^ slot) * width, LANE), width)
        copies.append(pltpu.make_async_copy(ref, out.at[0, :, at], sems.at[slot]))
    for copy in copies:
        copy.start()
    for copy in copies:
        copy.wait()


def call(kernel, outs, scratch, operands, whole=(), outside=False, copies=0):
    vmem, anywhere = (pl.BlockSpec(memory_space=space) for space in (pltpu.VMEM, pltpu.HBM))
    specs = [anywhere if slot in whole else vmem for slot in range(len(operands))]
    operands = [
        pltpu.with_memory_space_constraint(value, pltpu.HBM) if slot in whole else value
        for slot, value in enumerate(operands)
    ]
    return pl.pallas_call(
        kernel,
        out_shape=[jax.ShapeDtypeStruct(shape, jnp.float32) for shape in outs],
        in_specs=specs,
        out_specs=[anywhere if outside else vmem] * len(outs),
        scratch_shapes=[pltpu.VMEM(shape, jnp.float32) for shape in scratch]
        + ([pltpu.SemaphoreType.DMA((copies,))] if copies else []),
        compiler_params=pltpu.CompilerParams(vmem_limit_bytes=VMEM_LIMIT),
    )(*operands)


def shards(guesses, cond_x, cond_y, source, inflow):
    groups, strips = lax.axis_size("tm"), lax.axis_size("space")
    rows, columns = cond_x.shape
    fits = groups == len(FIELD_ROWS) + 1 and strips % 2 == 0 and rows == 16
    if not fits or columns % (2 * groups * LANE) != 0 or columns < 2 * groups * LANE:
        return general_shards(guesses, cond_x, cond_y, source, inflow)
    own = columns // groups
    lanes = own + 2 * SIDE
    pairs_a = [(i, i ^ 1) for i in range(strips)]
    pairs_b = [(i, j) for k in range(1, strips - 1, 2) for i, j in ((k, k + 1), (k + 1, k))]

    def trade(blocks):
        moved = [blocks[0]]
        for slot in range(1, groups):
            moved.append(lax.ppermute(blocks[slot], "tm", [(i, i ^ slot) for i in range(groups)]))
        return moved

    travel = sum(COEF_ROWS) + COARSE_ROWS
    *blocks, halo_a, halo_b, coefs, coarse = call(
        pack_kernel,
        [(rows, lanes)] * groups + [(travel, lanes), (travel, lanes), (3, rows, lanes), (rows // 2, lanes)],
        [(groups, rows, lanes + LANE), (3, rows, lanes + LANE)],
        [guesses[0], cond_x, cond_y, source, inflow], whole=range(5), copies=groups + 4,
    )
    coef_a = lax.ppermute(halo_a, "space", pairs_a)
    coef_b = lax.ppermute(halo_b, "space", pairs_b)
    blocks = trade(blocks)
    deep = sum(FIELD_ROWS)
    sent_a, sent_b, fields = call(edge_kernel, [(deep, lanes)] * 2 + [(groups, rows, lanes)], [], blocks)
    edge_a = lax.ppermute(sent_a, "space", pairs_a)
    edge_b = lax.ppermute(sent_b, "space", pairs_b)
    buffer = (lanes // LANE, rows + 2 * HALO, LANE)
    prepared = call(
        prepare_kernel,
        [buffer] * 12,
        [buffer, buffer, (rows // 2 + 2 * COARSE_ROWS, lanes)],
        [coefs, coarse, coef_a, coef_b],
    )
    blocks = call(
        main_kernel,
        [(rows, own)] * groups,
        [(3 * groups - 4, *buffer), (2, *buffer), (groups, *buffer)],
        [fields, *prepared, edge_a, edge_b],
    )
    return call(unpack_kernel, [(1, rows, columns)], [], trade(blocks), outside=True, copies=groups)[0]


def solution(mesh):
    return jax.shard_map(
        shards,
        mesh=mesh,
        in_specs=(
            P("tm", "space", None),
            P("space", None),
            P("space", None),
            P("space", None),
            P("space", None),
        ),
        out_specs=P("tm", "space", None),
        check_vma=False,
    )
```

```python
import functools

import jax
import jax.numpy as jnp
from jax import lax
from jax.experimental import pallas as pl
from jax.experimental.pallas import tpu as pltpu
from jax.sharding import PartitionSpec as P

FINE_STEPS = 4
LANE = 128
SIDE = 64
HALO = 16
COEF_ROWS = (10, 9, 9)
FIELD_ROWS = (12, 8, 4)
COARSE_ROWS = 4
VMEM_LIMIT = 40 * 1024 * 1024


def padded(value, sides, width):
    for axis, dim in sides:
        devices, length = (lax.axis_size(axis), value.shape[dim])
        up = [(i, (i + 1) % devices) for i in range(devices - 1)]
        down = [(j, i) for i, j in up]
        last = lax.slice_in_dim(value, length - width, length, axis=dim)
        leading = lax.slice_in_dim(value, 0, width, axis=dim)
        before = lax.ppermute(last, axis, up)
        after = lax.ppermute(leading, axis, down)
        value = jnp.concatenate([before, value, after], axis=dim)
    return value


def from_behind(value, axis, steps):
    count = lax.axis_size(axis)
    leading, last = (max(0, -steps), min(count, count - steps))
    return lax.ppermute(value, axis, [(source, source + steps) for source in range(leading, last)])


def interior(field_ext, cond_rows, cond_cols):
    centre = field_ext[1:-1]
    flux_sum = cond_rows[1:-1] * (field_ext[2:] - centre) - cond_rows[:-2] * (
        centre - field_ext[:-2]
    )
    widened = jnp.pad(centre, ((0, 0), (1, 1)))
    cond_own = cond_cols[1:-1]
    cond_west = jnp.pad(cond_own, ((0, 0), (1, 0)))[:, :-1]
    flux_sum = (
        flux_sum + cond_own * (widened[:, 2:] - centre) - cond_west * (centre - widened[:, :-2])
    )
    return centre + flux_sum


def propagate(field, coef_pad):
    strip_rows = field.shape[0]
    cond_rows = coef_pad[0, 3 : strip_rows + 5]
    cond_cols = coef_pad[1, 3 : strip_rows + 5]
    source_rows = coef_pad[2, 4 : strip_rows + 4]
    for section in range(FINE_STEPS):
        extended = padded(field, (("space", 0),), 1)
        field = interior(extended, cond_rows, cond_cols) + source_rows
    return field


def restrict(field):
    lead = field.shape[:-2]
    shaped = field.reshape(lead + (field.shape[-2] // 2, 2, field.shape[-1] // 2, 2))
    return jnp.mean(shaped, axis=(-3, -1))


def general_shards(guesses, cond_x, cond_y, source, inflow):
    strip_rows = cond_x.shape[0]
    columns = cond_x.shape[1]
    stacked = jnp.stack([cond_x, cond_y, source])
    edge_rows = from_behind(cond_x[strip_rows - 2 :], "space", 1)
    cond_upper = jnp.concatenate([jnp.zeros((2, columns), jnp.float32), edge_rows], axis=0)
    blank_rows = jnp.zeros((4, columns), jnp.float32)
    upper = jnp.stack([cond_upper, blank_rows, blank_rows])
    lower = jnp.zeros((3, 4, columns), jnp.float32)
    coef_pad = jnp.concatenate([upper, stacked, lower], axis=1)
    first_group = lax.axis_index("tm") == 0
    c_point = guesses[0]
    first_pass = propagate(c_point, coef_pad)
    received = from_behind(first_pass, "tm", 1)
    relaxed = jnp.where(first_group, c_point, received)
    second_pass = propagate(relaxed, coef_pad)
    fine_next = from_behind(second_pass, "tm", 1)
    residual = restrict(fine_next - relaxed)
    residual = jnp.where(first_group, 0.0, residual)
    coarse_coef = restrict(coef_pad[:2, 2 : strip_rows + 6])

    def chain_round(index, error_field):
        extended = padded(error_field, (("space", 0),), 1)
        stepped = interior(extended, coarse_coef[0], coarse_coef[1])
        arrived = from_behind(stepped, "tm", 1)
        return jnp.where(first_group, inflow, arrived + residual)

    start_error = jnp.where(first_group, inflow, jnp.zeros_like(residual))
    error_field = lax.fori_loop(0, lax.axis_size("tm") - 1, chain_round, start_error)
    widened = jnp.repeat(jnp.repeat(error_field, 2, axis=0), 2, axis=1)
    return (relaxed + widened)[None]


def place(groups, strips, columns, member):
    own = columns // groups
    lanes = own + 2 * SIDE
    start = jnp.clip(own * member - SIDE, 0, columns - lanes)
    around = jnp.clip(own * member - LANE, 0, columns - lanes - LANE)
    coarse = jnp.minimum(start // 2 // LANE * LANE, columns // 2 - lanes)
    return around, start - around, coarse, start // 2 - coarse


def sides(rows):
    strip, strips = lax.axis_index("space"), lax.axis_size("space")
    return lax.rem(strip, 2) == 0, jnp.where(strip == strips - 1, HALO + rows, 2 * HALO + rows)


def by_side(even, fill, first, second):
    @pl.when(even)
    def _():
        fill(first, second)

    @pl.when(jnp.logical_not(even))
    def _():
        fill(second, first)


def shifted(load, chunk, shift):
    amount = lax.rem(2 * LANE - shift, LANE)
    here = pltpu.roll(load(chunk), amount, 1)
    there = pltpu.roll(load(chunk + 1), amount, 1)
    lane = lax.broadcasted_iota(jnp.int32, here.shape, 1)
    return jnp.where(lane < LANE - shift, here, there)


def piece(chunk):
    return slice(chunk * LANE, (chunk + 1) * LANE)


def pack_kernel(
    guess, cond_x, cond_y, source, inflow, own, to_core, to_x, to_both, halo_a, halo_b, coefs, coarse,
    guess_in, coefs_in, sems,
):
    rows, lanes = own.shape
    columns = guess.shape[1]
    chunks = lanes // LANE
    groups, strips, member = lax.axis_size("tm"), lax.axis_size("space"), lax.axis_index("tm")
    outs = (own, to_core, to_x, to_both)
    copies, shifts = [], []
    for slot in range(groups):
        around, shift, _, _ = place(groups, strips, columns, member ^ slot)
        at = pl.ds(pl.multiple_of(around, LANE), lanes + LANE)
        copies.append(pltpu.make_async_copy(guess.at[:, at], guess_in.at[slot], sems.at[slot]))
        shifts.append(shift)
    around, shift, coarse_at, _ = place(groups, strips, columns, member)
    at = pl.ds(pl.multiple_of(around, LANE), lanes + LANE)
    for slot, ref in enumerate((cond_x, cond_y, source)):
        copies.append(pltpu.make_async_copy(ref.at[:, at], coefs_in.at[slot], sems.at[groups + slot]))
    at = pl.ds(pl.multiple_of(coarse_at, LANE), lanes)
    copies.append(pltpu.make_async_copy(inflow.at[:, at], coarse, sems.at[groups + 3]))
    for copy in copies:
        copy.start()
    for slot in range(groups):
        copies[slot].wait()
        for chunk in range(chunks):
            outs[slot][:, piece(chunk)] = shifted(lambda k: guess_in[slot, :, piece(k)], chunk, shifts[slot])
    for copy in copies[groups:]:
        copy.wait()
    for slot in range(3):
        for chunk in range(chunks):
            coefs[slot, :, piece(chunk)] = shifted(lambda k: coefs_in[slot, :, piece(k)], chunk, shift)

    def fill(bottom, top):
        at = 0
        for slot, deep in enumerate(COEF_ROWS):
            bottom[at : at + deep] = coefs[slot, rows - deep :]
            top[at : at + deep] = coefs[slot, :deep]
            at += deep
        bottom[at:] = coarse[rows // 2 - COARSE_ROWS :]
        top[at:] = coarse[:COARSE_ROWS]

    by_side(sides(rows)[0], fill, halo_a, halo_b)


def edge_kernel(own, from_core, from_x, from_both, edge_a, edge_b, fields):
    member = lax.axis_index("tm")
    for slot, ref in enumerate((own, from_core, from_x, from_both)):
        fields[member ^ slot] = ref[...]
    rows = own.shape[0]

    def fill(bottom, top):
        at = 0
        for group, deep in enumerate(FIELD_ROWS):
            bottom[at : at + deep] = fields[group, rows - deep :]
            top[at : at + deep] = fields[group, :deep]
            at += deep

    by_side(sides(rows)[0], fill, edge_a, edge_b)


def spread(value):
    rows, lanes = value.shape
    value = value.reshape(rows // 8, 8, lanes)
    row_even = lax.broadcasted_iota(jnp.int32, value.shape, 1) % 2 == 0
    lane_even = lax.broadcasted_iota(jnp.int32, value.shape, 2) % 2 == 0
    value = value + jnp.where(row_even, pltpu.roll(value, 7, 1), pltpu.roll(value, 1, 1))
    value = value + jnp.where(lane_even, pltpu.roll(value, lanes - 1, 2), pltpu.roll(value, 1, 2))
    return (value * 0.25).reshape(rows, lanes)


def weights(cond_x, cond_y, chunk, rows, width, limit, out):
    diagonal, up, east, west = out
    chunks = cond_x.shape[0]
    first, count = rows
    here = slice(first, first + count)
    own_x, own_y = cond_x[chunk, here], cond_y[chunk, here]
    above = cond_x[chunk, first - width : first - width + count]
    lane = lax.broadcasted_iota(jnp.int32, own_x.shape, 1)
    row = lax.broadcasted_iota(jnp.int32, own_x.shape, 0)
    before = pltpu.roll(cond_y[chunk - 1, here], width, 1) if chunk else jnp.zeros_like(own_y)
    beside = jnp.where(lane < width, before, pltpu.roll(own_y, width, 1))
    diagonal[chunk, here] = 1.0 - ((own_x + above) + (own_y + beside))
    up[chunk, here] = jnp.where(row < limit - first, above, 0.0)
    west[chunk, here] = beside
    east[chunk, here] = jnp.where(lane < LANE - width, own_y, 0.0) if chunk == chunks - 1 else own_y


def prepare_kernel(
    coefs, coarse, coef_a, coef_b,
    cond_x, source, diagonal, up, east, west, coarse_x, coarse_d, coarse_u, coarse_e, coarse_w, error,
    cond_y, coarse_y, tall,
):
    rows, lanes = coefs.shape[1:]
    chunks = lanes // LANE
    low = HALO + rows
    even, limit = sides(rows)
    targets = (cond_x, cond_y, source)

    def assemble(upper, lower):
        at = 0
        for ref, deep in zip(targets, COEF_ROWS):
            for chunk in range(chunks):
                ref[chunk, HALO - deep : HALO] = upper[at : at + deep, piece(chunk)]
                ref[chunk, low : low + deep] = lower[at : at + deep, piece(chunk)]
            at += deep
        tall[:COARSE_ROWS] = upper[at:]
        tall[COARSE_ROWS + rows // 2 :] = lower[at:]

    by_side(even, lambda lower, upper: assemble(upper, lower), coef_a, coef_b)

    tall[COARSE_ROWS : COARSE_ROWS + rows // 2] = coarse[...]
    for slot, ref in enumerate(targets):
        for chunk in range(chunks):
            ref[chunk, HALO:low] = coefs[slot, :, piece(chunk)]
    for chunk in range(chunks):
        weights(cond_x, cond_y, chunk, reach(rows, 9), 1, limit, (diagonal, up, east, west))
    span = slice(HALO - 8, low + 8)
    for chunk in range(chunks):
        coarse_x[chunk, span] = spread(cond_x[chunk, span])
        coarse_y[chunk, span] = spread(cond_y[chunk, span])
    for chunk in range(chunks):
        weights(coarse_x, coarse_y, chunk, reach(rows, 4), 2, limit, (coarse_d, coarse_u, coarse_e, coarse_w))
    high = rows // 2 + 2 * COARSE_ROWS
    half = lax.broadcasted_iota(jnp.int32, (8, LANE), 1) // 2
    twice = lax.broadcasted_iota(jnp.int32, (8, LANE), 0) // 2
    groups, strips, member = lax.axis_size("tm"), lax.axis_size("space"), lax.axis_index("tm")
    skip = place(groups, strips, groups * (lanes - 2 * SIDE), member)[3]
    first, shift = skip // LANE, lax.rem(skip, LANE)

    def load(chunk):
        at = jnp.minimum((first + chunk) * LANE, lanes - LANE)
        return tall[:, pl.ds(pl.multiple_of(at, LANE), LANE)]

    for pair in range((chunks + 1) // 2):
        compact = shifted(load, pair, shift)
        for side in range(2):
            chunk = 2 * pair + side
            if chunk < chunks:
                for part in range(high // 8):
                    wide = jnp.take_along_axis(compact[8 * part : 8 * part + 8], half + side * (LANE // 2), axis=1)
                    for end in range(2):
                        at = HALO - 2 * COARSE_ROWS + 16 * part + 8 * end
                        error[chunk, at : at + 8] = jnp.take_along_axis(wide, twice + 4 * end, axis=0)


def sweep(values, put, rows, width, factors, added):
    diagonal, up, down, east, west = factors
    chunks = diagonal.shape[0]
    first, count = rows
    here = slice(first, first + count)
    above = slice(first - width, first - width + count)
    below = slice(first + width, first + width + count)
    lane = lax.broadcasted_iota(jnp.int32, (count, LANE), 1)

    def load(chunk):
        value = values[chunk, here]
        return value, pltpu.roll(value, LANE - width, 1), pltpu.roll(value, width, 1)

    before, now, after = None, load(0), None
    for chunk in range(chunks):
        after = load(chunk + 1) if chunk + 1 < chunks else None
        value, right, left = now
        if after is not None:
            right = jnp.where(lane < LANE - width, right, after[1])
        if before is not None:
            left = jnp.where(lane < width, before[2], left)
        across = east[chunk, here] * right + west[chunk, here] * left
        along = down[chunk, here] * values[chunk, below] + up[chunk, here] * values[chunk, above]
        put[chunk, here] = (diagonal[chunk, here] * value + added(chunk, here)) + (across + along)
        before, now = now, after


def reach(rows, deep):
    return HALO - deep, (rows + 2 * deep + 7) // 8 * 8


def main_kernel(
    fields, cond_x, source, diagonal, up, east, west, coarse_x, coarse_d, coarse_u, coarse_e, coarse_w,
    start_error, edge_a, edge_b, own, to_core, to_x, to_both,
    guess, work, error,
):
    groups, rows, lanes = fields.shape
    chunks = lanes // LANE
    low = HALO + rows
    given = groups - 1

    def assemble(upper, lower):
        at = 0
        for group, deep in enumerate(FIELD_ROWS):
            for chunk in range(chunks):
                guess[group, chunk, HALO - deep : HALO] = upper[at : at + deep, piece(chunk)]
                guess[group, chunk, low : low + deep] = lower[at : at + deep, piece(chunk)]
            at += deep

    by_side(sides(rows)[0], lambda lower, upper: assemble(upper, lower), edge_a, edge_b)

    for group in range(given):
        for chunk in range(chunks):
            guess[group, chunk, HALO:low] = fields[group, :, piece(chunk)]
    span = slice(HALO - 8, low + 8)
    error[0, :, span] = start_error[:, span]

    fine = (diagonal, up, cond_x, east, west)
    coarse = (coarse_d, coarse_u, coarse_x, coarse_e, coarse_w)

    def add_source(chunk, here):
        return source[chunk, here]

    def propagate(slots, deeps):
        for number in range(FINE_STEPS):
            for lane, (slot, deep) in enumerate(zip(slots, deeps)):
                first, second = work.at[2 * lane], work.at[2 * lane + 1]
                stops = [guess.at[slot], first, second, first, guess.at[slot + given]]
                reached = reach(rows, deep + FINE_STEPS - 1 - number)
                sweep(stops[number], stops[number + 1], reached, 1, fine, add_source)

    propagate((0, 1, 2), (6, 4, 0))
    propagate((3, 4), (2, 0))

    for group in range(1, groups):
        reached = given if group == 1 else 2 * given - 2 + group
        relaxed = given - 1 + group

        def residual(chunk, here, reached=reached, relaxed=relaxed):
            return spread(guess[reached, chunk, here] - guess[relaxed, chunk, here])

        sweep(error.at[group - 1], error.at[group], reach(rows, 2 * (groups - 1 - group)), 2, coarse, residual)

    member = lax.axis_index("tm")
    shift = place(groups, lax.axis_size("space"), groups * own.shape[1], member)[1]
    for slot, out in enumerate((own, to_core, to_x, to_both)):
        group = member ^ slot
        relaxed = jnp.where(group == 0, 0, given - 1 + group)

        def load(chunk):
            return guess[relaxed, chunk, HALO:low] + error[group, chunk, HALO:low]

        for chunk in range(chunks - 1):
            out[:, piece(chunk)] = shifted(load, chunk, shift)


def unpack_kernel(own, from_core, from_x, from_both, out, sems):
    width = own.shape[1]
    member = lax.axis_index("tm")
    copies = []
    for slot, ref in enumerate((own, from_core, from_x, from_both)):
        at = pl.ds(pl.multiple_of((member ^ slot) * width, LANE), width)
        copies.append(pltpu.make_async_copy(ref, out.at[0, :, at], sems.at[slot]))
    for copy in copies:
        copy.start()
    for copy in copies:
        copy.wait()


def call(kernel, outs, scratch, operands, whole=(), outside=False, copies=0):
    vmem, anywhere = (pl.BlockSpec(memory_space=space) for space in (pltpu.VMEM, pltpu.HBM))
    specs = [anywhere if slot in whole else vmem for slot in range(len(operands))]
    operands = [
        pltpu.with_memory_space_constraint(value, pltpu.HBM) if slot in whole else value
        for slot, value in enumerate(operands)
    ]
    return pl.pallas_call(
        kernel,
        out_shape=[jax.ShapeDtypeStruct(shape, jnp.float32) for shape in outs],
        in_specs=specs,
        out_specs=[anywhere if outside else vmem] * len(outs),
        scratch_shapes=[pltpu.VMEM(shape, jnp.float32) for shape in scratch]
        + ([pltpu.SemaphoreType.DMA((copies,))] if copies else []),
        compiler_params=pltpu.CompilerParams(vmem_limit_bytes=VMEM_LIMIT),
    )(*operands)


def shards(guesses, cond_x, cond_y, source, inflow):
    groups, strips = lax.axis_size("tm"), lax.axis_size("space")
    rows, columns = cond_x.shape
    fits = groups == len(FIELD_ROWS) + 1 and strips % 2 == 0 and rows == 16
    if not fits or columns % (2 * groups * LANE) != 0 or columns < 2 * groups * LANE:
        return general_shards(guesses, cond_x, cond_y, source, inflow)
    own = columns // groups
    lanes = own + 2 * SIDE
    pairs_a = [(i, i ^ 1) for i in range(strips)]
    pairs_b = [(i, j) for k in range(1, strips - 1, 2) for i, j in ((k, k + 1), (k + 1, k))]

    def trade(blocks):
        moved = [blocks[0]]
        for slot in range(1, groups):
            moved.append(lax.ppermute(blocks[slot], "tm", [(i, i ^ slot) for i in range(groups)]))
        return moved

    travel = sum(COEF_ROWS) + COARSE_ROWS
    *blocks, halo_a, halo_b, coefs, coarse = call(
        pack_kernel,
        [(rows, lanes)] * groups + [(travel, lanes), (travel, lanes), (3, rows, lanes), (rows // 2, lanes)],
        [(groups, rows, lanes + LANE), (3, rows, lanes + LANE)],
        [guesses[0], cond_x, cond_y, source, inflow], whole=range(5), copies=groups + 4,
    )
    coef_a = lax.ppermute(halo_a, "space", pairs_a)
    coef_b = lax.ppermute(halo_b, "space", pairs_b)
    blocks = trade(blocks)
    deep = sum(FIELD_ROWS)
    sent_a, sent_b, fields = call(edge_kernel, [(deep, lanes)] * 2 + [(groups, rows, lanes)], [], blocks)
    edge_a = lax.ppermute(sent_a, "space", pairs_a)
    edge_b = lax.ppermute(sent_b, "space", pairs_b)
    buffer = (lanes // LANE, rows + 2 * HALO, LANE)
    prepared = call(
        prepare_kernel,
        [buffer] * 12,
        [buffer, buffer, (rows // 2 + 2 * COARSE_ROWS, lanes)],
        [coefs, coarse, coef_a, coef_b],
    )
    blocks = call(
        main_kernel,
        [(rows, own)] * groups,
        [(3 * groups - 4, *buffer), (2 * groups - 2, *buffer), (groups, *buffer)],
        [fields, *prepared, edge_a, edge_b],
    )
    return call(unpack_kernel, [(1, rows, columns)], [], trade(blocks), outside=True, copies=groups)[0]


def solution(mesh):
    return jax.shard_map(
        shards,
        mesh=mesh,
        in_specs=(
            P("tm", "space", None),
            P("space", None),
            P("space", None),
            P("space", None),
            P("space", None),
        ),
        out_specs=P("tm", "space", None),
        check_vma=False,
    )
```

```python
import functools

import jax
import jax.numpy as jnp
from jax import lax
from jax.experimental import pallas as pl
from jax.experimental.pallas import tpu as pltpu
from jax.sharding import PartitionSpec as P

FINE_STEPS = 4
LANE = 128
FRINGE = 16
HALO = 16
COEF_ROWS = (10, 9, 9)
FIELD_ROWS = (10, 8, 4)
COARSE_ROWS = 3
VMEM_LIMIT = 40 * 1024 * 1024


def padded(value, sides, width):
    for axis, dim in sides:
        devices, length = (lax.axis_size(axis), value.shape[dim])
        up = [(i, (i + 1) % devices) for i in range(devices - 1)]
        down = [(j, i) for i, j in up]
        last = lax.slice_in_dim(value, length - width, length, axis=dim)
        leading = lax.slice_in_dim(value, 0, width, axis=dim)
        before = lax.ppermute(last, axis, up)
        after = lax.ppermute(leading, axis, down)
        value = jnp.concatenate([before, value, after], axis=dim)
    return value


def from_behind(value, axis, steps):
    count = lax.axis_size(axis)
    leading, last = (max(0, -steps), min(count, count - steps))
    return lax.ppermute(value, axis, [(source, source + steps) for source in range(leading, last)])


def interior(field_ext, cond_rows, cond_cols):
    centre = field_ext[1:-1]
    flux_sum = cond_rows[1:-1] * (field_ext[2:] - centre) - cond_rows[:-2] * (
        centre - field_ext[:-2]
    )
    widened = jnp.pad(centre, ((0, 0), (1, 1)))
    cond_own = cond_cols[1:-1]
    cond_west = jnp.pad(cond_own, ((0, 0), (1, 0)))[:, :-1]
    flux_sum = (
        flux_sum + cond_own * (widened[:, 2:] - centre) - cond_west * (centre - widened[:, :-2])
    )
    return centre + flux_sum


def propagate(field, coef_pad):
    strip_rows = field.shape[0]
    cond_rows = coef_pad[0, 3 : strip_rows + 5]
    cond_cols = coef_pad[1, 3 : strip_rows + 5]
    source_rows = coef_pad[2, 4 : strip_rows + 4]
    for section in range(FINE_STEPS):
        extended = padded(field, (("space", 0),), 1)
        field = interior(extended, cond_rows, cond_cols) + source_rows
    return field


def restrict(field):
    lead = field.shape[:-2]
    shaped = field.reshape(lead + (field.shape[-2] // 2, 2, field.shape[-1] // 2, 2))
    return jnp.mean(shaped, axis=(-3, -1))


def general_shards(guesses, cond_x, cond_y, source, inflow):
    strip_rows = cond_x.shape[0]
    columns = cond_x.shape[1]
    stacked = jnp.stack([cond_x, cond_y, source])
    edge_rows = from_behind(cond_x[strip_rows - 2 :], "space", 1)
    cond_upper = jnp.concatenate([jnp.zeros((2, columns), jnp.float32), edge_rows], axis=0)
    blank_rows = jnp.zeros((4, columns), jnp.float32)
    upper = jnp.stack([cond_upper, blank_rows, blank_rows])
    lower = jnp.zeros((3, 4, columns), jnp.float32)
    coef_pad = jnp.concatenate([upper, stacked, lower], axis=1)
    first_group = lax.axis_index("tm") == 0
    c_point = guesses[0]
    first_pass = propagate(c_point, coef_pad)
    received = from_behind(first_pass, "tm", 1)
    relaxed = jnp.where(first_group, c_point, received)
    second_pass = propagate(relaxed, coef_pad)
    fine_next = from_behind(second_pass, "tm", 1)
    residual = restrict(fine_next - relaxed)
    residual = jnp.where(first_group, 0.0, residual)
    coarse_coef = restrict(coef_pad[:2, 2 : strip_rows + 6])

    def chain_round(index, error_field):
        extended = padded(error_field, (("space", 0),), 1)
        stepped = interior(extended, coarse_coef[0], coarse_coef[1])
        arrived = from_behind(stepped, "tm", 1)
        return jnp.where(first_group, inflow, arrived + residual)

    start_error = jnp.where(first_group, inflow, jnp.zeros_like(residual))
    error_field = lax.fori_loop(0, lax.axis_size("tm") - 1, chain_round, start_error)
    widened = jnp.repeat(jnp.repeat(error_field, 2, axis=0), 2, axis=1)
    return (relaxed + widened)[None]


def piece(chunk):
    return slice(chunk * LANE, (chunk + 1) * LANE)


def lanes_of(shape):
    return lax.broadcasted_iota(jnp.int32, shape, len(shape) - 1)


def fringe_of(left, right, member, width):
    lane = lanes_of(left.shape)
    last = lax.axis_size("tm") - 1
    value = jnp.where(lane < jnp.where(member < last, width, 0), right, 0.0)
    return jnp.where(lane >= jnp.where(member > 0, LANE - width, LANE), left, value)


def fold(source, rows):
    part = rows // 4
    total = source[:part]
    for turn in range(1, 4):
        total = total + pltpu.roll(source[turn * part : (turn + 1) * part], 2 * FRINGE * turn, 1)
    return total


def unfold(folded, target, rows):
    part = rows // 4
    lane = lanes_of(folded.shape)
    used = (lane < FRINGE) | (lane >= LANE - FRINGE)
    for turn in range(4):
        turned = pltpu.roll(folded, LANE - 2 * FRINGE * turn, 1) if turn else folded
        target[turn * part : (turn + 1) * part] = jnp.where(used, turned, 0.0)


def sides(rows):
    strip, strips = lax.axis_index("space"), lax.axis_size("space")
    return lax.rem(strip, 2) == 0, jnp.where(strip == strips - 1, HALO + rows, 2 * HALO + rows)


def by_side(even, fill, first, second):
    @pl.when(even)
    def _():
        fill(first, second)

    @pl.when(jnp.logical_not(even))
    def _():
        fill(second, first)


def pack_kernel(
    guess, cond_x, cond_y, source, inflow, own, to_core, to_x, to_both, halo_a, halo_b, coefs, coarse,
    guess_in, coefs_in, inflow_in, spare, sems,
):
    rows, columns = guess.shape
    groups, member = lax.axis_size("tm"), lax.axis_index("tm")
    width = columns // groups
    chunks = width // LANE

    def at(column):
        return pl.ds(pl.multiple_of(column, LANE), LANE)

    around = jnp.clip(width * member - LANE, 0, columns - width - 2 * LANE)
    span = pl.ds(pl.multiple_of(around, LANE), width + 2 * LANE)
    copies = [pltpu.make_async_copy(guess, guess_in, sems.at[0])]
    for slot, ref in enumerate((cond_x, cond_y, source)):
        copies.append(pltpu.make_async_copy(ref.at[:, span], coefs_in.at[slot], sems.at[1 + slot]))
    copies.append(pltpu.make_async_copy(inflow, inflow_in, sems.at[4]))
    for copy in copies:
        copy.start()
    copies[0].wait()
    for slot, out in enumerate((own, to_core, to_x, to_both)):
        target = member ^ slot
        first = width * target
        for chunk in range(chunks):
            out[chunk * rows : (chunk + 1) * rows] = guess_in[:, at(first + chunk * LANE)]
        left = guess_in[:, at(jnp.maximum(first - LANE, 0))]
        right = guess_in[:, at(jnp.minimum(first + width, columns - LANE))]
        spare[:rows] = fringe_of(left, right, target, FRINGE)
        out[chunks * rows : chunks * rows + rows // 4] = fold(spare, rows)
    for copy in copies[1:]:
        copy.wait()
    skip = width * member - around
    for slot in range(3):
        for chunk in range(chunks):
            coefs[slot, chunk] = coefs_in[slot, :, at(skip + chunk * LANE)]
        left = coefs_in[slot, :, at(jnp.maximum(skip - LANE, 0))]
        right = coefs_in[slot, :, at(jnp.minimum(skip + width, width + LANE))]
        coefs[slot, chunks] = fringe_of(left, right, member, FRINGE)
    first, half = width // 2 * member, chunks // 2
    for chunk in range(half):
        coarse[chunk] = inflow_in[:, at(first + chunk * LANE)]
    left = inflow_in[:, at(jnp.maximum(first - LANE, 0))]
    right = inflow_in[:, at(jnp.minimum(first + width // 2, columns // 2 - LANE))]
    coarse[half] = fringe_of(left, right, member, FRINGE // 2)

    def take(halo, bottom):
        base = fringe = 0
        for slot, deep in enumerate(COEF_ROWS):
            edge = slice(rows - deep, rows) if bottom else slice(0, deep)
            for chunk in range(chunks):
                halo[base : base + deep] = coefs[slot, chunk, edge]
                base += deep
            spare[fringe : fringe + deep] = coefs[slot, chunks, edge]
            fringe += deep
        halo[base : base + fringe // 4] = fold(spare, fringe)
        base += fringe // 4
        edge = slice(rows // 2 - COARSE_ROWS, rows // 2) if bottom else slice(0, COARSE_ROWS)
        for chunk in range(half + 1):
            halo[base : base + COARSE_ROWS] = coarse[chunk, edge]
            base += COARSE_ROWS

    def fill(below, above):
        take(below, True)
        take(above, False)

    by_side(sides(rows)[0], fill, halo_a, halo_b)


def edge_kernel(own, from_core, from_x, from_both, edge_a, edge_b, fields, spare):
    member = lax.axis_index("tm")
    chunks, rows = fields.shape[1] - 1, fields.shape[2]
    for slot, ref in enumerate((own, from_core, from_x, from_both)):
        target = fields.at[member ^ slot]
        for chunk in range(chunks):
            target[chunk] = ref[chunk * rows : (chunk + 1) * rows]
        unfold(ref[chunks * rows : chunks * rows + rows // 4], target.at[chunks], rows)

    def take(edge, bottom):
        base = fringe = 0
        for group, deep in enumerate(FIELD_ROWS):
            here = slice(rows - deep, rows) if bottom else slice(0, deep)
            for chunk in range(chunks):
                edge[base : base + deep] = fields[group, chunk, here]
                base += deep
            spare[fringe : fringe + deep] = fields[group, chunks, here]
            fringe += deep
        fringe = (fringe + 3) // 4 * 4
        edge[base : base + fringe // 4] = fold(spare, fringe)

    def fill(below, above):
        take(below, True)
        take(above, False)

    spare[...] = jnp.zeros_like(spare)
    by_side(sides(rows)[0], fill, edge_a, edge_b)


def spread(value):
    rows, lanes = value.shape
    value = value.reshape(rows // 8, 8, lanes)
    row_even = lax.broadcasted_iota(jnp.int32, value.shape, 1) % 2 == 0
    lane_even = lax.broadcasted_iota(jnp.int32, value.shape, 2) % 2 == 0
    value = value + jnp.where(row_even, pltpu.roll(value, 7, 1), pltpu.roll(value, 1, 1))
    value = value + jnp.where(lane_even, pltpu.roll(value, lanes - 1, 2), pltpu.roll(value, 1, 2))
    return (value * 0.25).reshape(rows, lanes)


def weights(cond_x, cond_y, chunk, rows, width, limit, out):
    diagonal, up, west = out
    chunks = cond_x.shape[0]
    first, count = rows
    here = slice(first, first + count)
    own_x, own_y = cond_x[chunk, here], cond_y[chunk, here]
    above = cond_x[chunk, first - width : first - width + count]
    lane = lanes_of(own_x.shape)
    row = lax.broadcasted_iota(jnp.int32, own_x.shape, 0)
    before = pltpu.roll(cond_y[(chunk - 1) % chunks, here], width, 1)
    beside = jnp.where(lane < width, before, pltpu.roll(own_y, width, 1))
    diagonal[chunk, here] = 1.0 - ((own_x + above) + (own_y + beside))
    up[chunk, here] = jnp.where(row < limit - first, above, 0.0)
    if chunk == chunks - 1:
        closed = jnp.where(lax.axis_index("tm") == lax.axis_size("tm") - 1, width, 0)
        beside = jnp.where(lane < closed, 0.0, beside)
    west[chunk, here] = beside


def prepare_kernel(
    coefs, coarse, coef_a, coef_b,
    cond_x, cond_y, source, diagonal, up, west, coarse_x, coarse_y, coarse_d, coarse_u, coarse_w, error,
    tall, spare,
):
    _, chunks, rows, _ = coefs.shape
    chunks, half = chunks - 1, (chunks - 1) // 2
    low = HALO + rows
    even, limit = sides(rows)
    targets = (cond_x, cond_y, source)
    tall[...] = jnp.zeros_like(tall)

    def give(halo, below):
        base = fringe = 0
        for ref, deep in zip(targets, COEF_ROWS):
            first = low if below else HALO - deep
            for chunk in range(chunks):
                ref[chunk, first : first + deep] = halo[base : base + deep]
                base += deep
        total = sum(COEF_ROWS)
        unfold(halo[base : base + total // 4], spare, total)
        base += total // 4
        for ref, deep in zip(targets, COEF_ROWS):
            first = low if below else HALO - deep
            ref[chunks, first : first + deep] = spare[fringe : fringe + deep]
            fringe += deep
        first = 4 + rows // 2 if below else 4 - COARSE_ROWS
        for chunk in range(half + 1):
            tall[chunk, first : first + COARSE_ROWS] = halo[base : base + COARSE_ROWS]
            base += COARSE_ROWS

    def fill(below, above):
        give(below, True)
        give(above, False)

    by_side(even, fill, coef_a, coef_b)
    for slot, ref in enumerate(targets):
        ref[:, HALO:low] = coefs[slot]
    tall[:, 4 : 4 + rows // 2] = coarse[...]
    for chunk in range(chunks + 1):
        weights(cond_x, cond_y, chunk, reach(rows, 9), 1, limit, (diagonal, up, west))
    span = slice(HALO - 8, low + 8)
    for chunk in range(chunks + 1):
        coarse_x[chunk, span] = spread(cond_x[chunk, span])
        coarse_y[chunk, span] = spread(cond_y[chunk, span])
    for chunk in range(chunks + 1):
        weights(coarse_x, coarse_y, chunk, reach(rows, 4), 2, limit, (coarse_d, coarse_u, coarse_w))
    lane = lanes_of((8, LANE))
    twice = lax.broadcasted_iota(jnp.int32, (8, LANE), 0) // 2
    for chunk in range(chunks + 1):
        side = chunk % 2 * (LANE // 2)
        pick = lane // 2 + (side if chunk < chunks else jnp.where(lane < LANE // 2, 0, LANE // 2))
        for part in range((rows // 2 + 8) // 8):
            wide = jnp.take_along_axis(tall[chunk // 2, 8 * part : 8 * part + 8], pick, axis=1)
            for end in range(2):
                at = HALO - 8 + 16 * part + 8 * end
                error[chunk, at : at + 8] = jnp.take_along_axis(wide, twice + 4 * end, axis=0)


def sweep(values, put, rows, width, factors, added):
    diagonal, up, down, east, west = factors
    chunks = diagonal.shape[0]
    first, count = rows
    here = slice(first, first + count)
    above = slice(first - width, first - width + count)
    below = slice(first + width, first + width + count)
    lane = lanes_of((count, LANE))

    def load(chunk):
        value = values[chunk % chunks, here]
        return value, pltpu.roll(value, LANE - width, 1), pltpu.roll(value, width, 1)

    before, now = load(-1), load(0)
    for chunk in range(chunks):
        after = load(chunk + 1)
        right = jnp.where(lane < LANE - width, now[1], after[1])
        left = jnp.where(lane < width, before[2], now[2])
        across = east[chunk, here] * right + west[chunk, here] * left
        along = down[chunk, here] * values[chunk, below] + up[chunk, here] * values[chunk, above]
        put[chunk, here] = (diagonal[chunk, here] * now[0] + added(chunk, here)) + (across + along)
        before, now = now, after


def reach(rows, deep):
    return HALO - deep, (rows + 2 * deep + 7) // 8 * 8


def main_kernel(
    fields, cond_x, cond_y, source, diagonal, up, west, coarse_x, coarse_y, coarse_d, coarse_u, coarse_w,
    start_error, edge_a, edge_b, own, to_core, to_x, to_both,
    guess, work, error, spare,
):
    groups, chunks, rows, _ = fields.shape
    chunks -= 1
    low = HALO + rows
    given = groups - 1

    def give(edge, below):
        base = fringe = 0
        for group, deep in enumerate(FIELD_ROWS):
            first = low if below else HALO - deep
            for chunk in range(chunks):
                guess[group, chunk, first : first + deep] = edge[base : base + deep]
                base += deep
        total = (sum(FIELD_ROWS) + 3) // 4 * 4
        unfold(edge[base : base + total // 4], spare, total)
        for group, deep in enumerate(FIELD_ROWS):
            first = low if below else HALO - deep
            guess[group, chunks, first : first + deep] = spare[fringe : fringe + deep]
            fringe += deep

    def fill(below, above):
        give(below, True)
        give(above, False)

    by_side(sides(rows)[0], fill, edge_a, edge_b)
    for group in range(given):
        guess[group, :, HALO:low] = fields[group]
    span = slice(HALO - 8, low + 8)
    error[0, :, span] = start_error[:, span]

    fine = (diagonal, up, cond_x, cond_y, west)
    coarse = (coarse_d, coarse_u, coarse_x, coarse_y, coarse_w)

    def add_source(chunk, here):
        return source[chunk, here]

    def propagate(slots, deeps):
        for number in range(FINE_STEPS):
            for lane, (slot, deep) in enumerate(zip(slots, deeps)):
                first, second = work.at[2 * lane], work.at[2 * lane + 1]
                stops = [guess.at[slot], first, second, first, guess.at[slot + given]]
                reached = reach(rows, deep + FINE_STEPS - 1 - number)
                sweep(stops[number], stops[number + 1], reached, 1, fine, add_source)

    propagate((0, 1, 2), (6, 4, 0))
    propagate((3, 4), (2, 0))

    for group in range(1, groups):
        reached = given if group == 1 else 2 * given - 2 + group
        relaxed = given - 1 + group

        def residual(chunk, here, reached=reached, relaxed=relaxed):
            return spread(guess[reached, chunk, here] - guess[relaxed, chunk, here])

        sweep(error.at[group - 1], error.at[group], reach(rows, 2 * (groups - 1 - group)), 2, coarse, residual)

    member = lax.axis_index("tm")
    for slot, out in enumerate((own, to_core, to_x, to_both)):
        group = member ^ slot
        relaxed = jnp.where(group == 0, 0, given - 1 + group)
        for chunk in range(chunks):
            out[:, piece(chunk)] = guess[relaxed, chunk, HALO:low] + error[group, chunk, HALO:low]


def unpack_kernel(own, from_core, from_x, from_both, out, sems):
    width = own.shape[1]
    member = lax.axis_index("tm")
    copies = []
    for slot, ref in enumerate((own, from_core, from_x, from_both)):
        at = pl.ds(pl.multiple_of((member ^ slot) * width, LANE), width)
        copies.append(pltpu.make_async_copy(ref, out.at[0, :, at], sems.at[slot]))
    for copy in copies:
        copy.start()
    for copy in copies:
        copy.wait()


def call(kernel, outs, scratch, operands, whole=(), outside=False, copies=0):
    vmem, anywhere = (pl.BlockSpec(memory_space=space) for space in (pltpu.VMEM, pltpu.HBM))
    specs = [anywhere if slot in whole else vmem for slot in range(len(operands))]
    operands = [
        pltpu.with_memory_space_constraint(value, pltpu.HBM) if slot in whole else value
        for slot, value in enumerate(operands)
    ]
    return pl.pallas_call(
        kernel,
        out_shape=[jax.ShapeDtypeStruct(shape, jnp.float32) for shape in outs],
        in_specs=specs,
        out_specs=[anywhere if outside else vmem] * len(outs),
        scratch_shapes=[pltpu.VMEM(shape, jnp.float32) for shape in scratch]
        + ([pltpu.SemaphoreType.DMA((copies,))] if copies else []),
        compiler_params=pltpu.CompilerParams(vmem_limit_bytes=VMEM_LIMIT),
    )(*operands)


def shards(guesses, cond_x, cond_y, source, inflow):
    groups, strips = lax.axis_size("tm"), lax.axis_size("space")
    rows, columns = cond_x.shape
    fits = groups == len(FIELD_ROWS) + 1 and strips % 2 == 0 and rows == 16
    if not fits or columns % (2 * groups * LANE) != 0:
        return general_shards(guesses, cond_x, cond_y, source, inflow)
    own = columns // groups
    chunks = own // LANE
    pairs_a = [(i, i ^ 1) for i in range(strips)]
    pairs_b = [(i, j) for k in range(1, strips - 1, 2) for i, j in ((k, k + 1), (k + 1, k))]

    def trade(blocks):
        moved = [blocks[0]]
        for slot in range(1, groups):
            moved.append(lax.ppermute(blocks[slot], "tm", [(i, i ^ slot) for i in range(groups)]))
        return moved

    def whole(count):
        return (count + 7) // 8 * 8

    def folded(count):
        return count * chunks + (count + 3) // 4

    block = (whole(folded(rows)), LANE)
    halo = (whole(folded(sum(COEF_ROWS)) + (chunks // 2 + 1) * COARSE_ROWS), LANE)
    edge = (whole(folded(sum(FIELD_ROWS))), LANE)
    spare = (32, LANE)
    *blocks, halo_a, halo_b, coefs, coarse = call(
        pack_kernel,
        [block] * groups + [halo, halo, (3, chunks + 1, rows, LANE), (chunks // 2 + 1, rows // 2, LANE)],
        [(rows, columns), (3, rows, own + 2 * LANE), (rows // 2, columns // 2), spare],
        [guesses[0], cond_x, cond_y, source, inflow], whole=range(5), copies=5,
    )
    coef_a = lax.ppermute(halo_a, "space", pairs_a)
    coef_b = lax.ppermute(halo_b, "space", pairs_b)
    blocks = trade(blocks)
    sent_a, sent_b, fields = call(edge_kernel, [edge, edge, (groups, chunks + 1, rows, LANE)], [spare], blocks)
    edge_a = lax.ppermute(sent_a, "space", pairs_a)
    edge_b = lax.ppermute(sent_b, "space", pairs_b)
    buffer = (chunks + 1, rows + 2 * HALO, LANE)
    prepared = call(
        prepare_kernel, [buffer] * 12, [(chunks // 2 + 1, rows // 2 + 8, LANE), spare], [coefs, coarse, coef_a, coef_b]
    )
    blocks = call(
        main_kernel,
        [(rows, own)] * groups,
        [(3 * groups - 4, *buffer), (2 * groups - 2, *buffer), (groups, *buffer), spare],
        [fields, *prepared, edge_a, edge_b],
    )
    return call(unpack_kernel, [(1, rows, columns)], [], trade(blocks), outside=True, copies=groups)[0]


def solution(mesh):
    return jax.shard_map(
        shards,
        mesh=mesh,
        in_specs=(
            P("tm", "space", None),
            P("space", None),
            P("space", None),
            P("space", None),
            P("space", None),
        ),
        out_specs=P("tm", "space", None),
        check_vma=False,
    )
```

```python
import functools

import jax
import jax.numpy as jnp
from jax import lax
from jax.experimental import pallas as pl
from jax.experimental.pallas import tpu as pltpu
from jax.sharding import PartitionSpec as P

FINE_STEPS = 4
LANE = 128
FRINGE = 16
HALO = 16
COEF_ROWS = (10, 9, 9)
FIELD_ROWS = (10, 8, 4)
COARSE_ROWS = 3
VMEM_LIMIT = 40 * 1024 * 1024


def padded(value, sides, width):
    for axis, dim in sides:
        devices, length = (lax.axis_size(axis), value.shape[dim])
        up = [(i, (i + 1) % devices) for i in range(devices - 1)]
        down = [(j, i) for i, j in up]
        last = lax.slice_in_dim(value, length - width, length, axis=dim)
        leading = lax.slice_in_dim(value, 0, width, axis=dim)
        before = lax.ppermute(last, axis, up)
        after = lax.ppermute(leading, axis, down)
        value = jnp.concatenate([before, value, after], axis=dim)
    return value


def from_behind(value, axis, steps):
    count = lax.axis_size(axis)
    leading, last = (max(0, -steps), min(count, count - steps))
    return lax.ppermute(value, axis, [(source, source + steps) for source in range(leading, last)])


def interior(field_ext, cond_rows, cond_cols):
    centre = field_ext[1:-1]
    flux_sum = cond_rows[1:-1] * (field_ext[2:] - centre) - cond_rows[:-2] * (
        centre - field_ext[:-2]
    )
    widened = jnp.pad(centre, ((0, 0), (1, 1)))
    cond_own = cond_cols[1:-1]
    cond_west = jnp.pad(cond_own, ((0, 0), (1, 0)))[:, :-1]
    flux_sum = (
        flux_sum + cond_own * (widened[:, 2:] - centre) - cond_west * (centre - widened[:, :-2])
    )
    return centre + flux_sum


def propagate(field, coef_pad):
    strip_rows = field.shape[0]
    cond_rows = coef_pad[0, 3 : strip_rows + 5]
    cond_cols = coef_pad[1, 3 : strip_rows + 5]
    source_rows = coef_pad[2, 4 : strip_rows + 4]
    for section in range(FINE_STEPS):
        extended = padded(field, (("space", 0),), 1)
        field = interior(extended, cond_rows, cond_cols) + source_rows
    return field


def restrict(field):
    lead = field.shape[:-2]
    shaped = field.reshape(lead + (field.shape[-2] // 2, 2, field.shape[-1] // 2, 2))
    return jnp.mean(shaped, axis=(-3, -1))


def general_shards(guesses, cond_x, cond_y, source, inflow):
    strip_rows = cond_x.shape[0]
    columns = cond_x.shape[1]
    stacked = jnp.stack([cond_x, cond_y, source])
    edge_rows = from_behind(cond_x[strip_rows - 2 :], "space", 1)
    cond_upper = jnp.concatenate([jnp.zeros((2, columns), jnp.float32), edge_rows], axis=0)
    blank_rows = jnp.zeros((4, columns), jnp.float32)
    upper = jnp.stack([cond_upper, blank_rows, blank_rows])
    lower = jnp.zeros((3, 4, columns), jnp.float32)
    coef_pad = jnp.concatenate([upper, stacked, lower], axis=1)
    first_group = lax.axis_index("tm") == 0
    c_point = guesses[0]
    first_pass = propagate(c_point, coef_pad)
    received = from_behind(first_pass, "tm", 1)
    relaxed = jnp.where(first_group, c_point, received)
    second_pass = propagate(relaxed, coef_pad)
    fine_next = from_behind(second_pass, "tm", 1)
    residual = restrict(fine_next - relaxed)
    residual = jnp.where(first_group, 0.0, residual)
    coarse_coef = restrict(coef_pad[:2, 2 : strip_rows + 6])

    def chain_round(index, error_field):
        extended = padded(error_field, (("space", 0),), 1)
        stepped = interior(extended, coarse_coef[0], coarse_coef[1])
        arrived = from_behind(stepped, "tm", 1)
        return jnp.where(first_group, inflow, arrived + residual)

    start_error = jnp.where(first_group, inflow, jnp.zeros_like(residual))
    error_field = lax.fori_loop(0, lax.axis_size("tm") - 1, chain_round, start_error)
    widened = jnp.repeat(jnp.repeat(error_field, 2, axis=0), 2, axis=1)
    return (relaxed + widened)[None]


def piece(chunk):
    return slice(chunk * LANE, (chunk + 1) * LANE)


def lanes_of(shape):
    return lax.broadcasted_iota(jnp.int32, shape, len(shape) - 1)


def fringe_of(left, right, member, width):
    lane = lanes_of(left.shape)
    last = lax.axis_size("tm") - 1
    value = jnp.where(lane < jnp.where(member < last, width, 0), right, 0.0)
    return jnp.where(lane >= jnp.where(member > 0, LANE - width, LANE), left, value)


def fold(source, rows):
    part = rows // 4
    total = source[:part]
    for turn in range(1, 4):
        total = total + pltpu.roll(source[turn * part : (turn + 1) * part], 2 * FRINGE * turn, 1)
    return total


def unfold(folded, target, rows):
    part = rows // 4
    lane = lanes_of(folded.shape)
    used = (lane < FRINGE) | (lane >= LANE - FRINGE)
    for turn in range(4):
        turned = pltpu.roll(folded, LANE - 2 * FRINGE * turn, 1) if turn else folded
        target[turn * part : (turn + 1) * part] = jnp.where(used, turned, 0.0)


def sides(rows):
    strip, strips = lax.axis_index("space"), lax.axis_size("space")
    return lax.rem(strip, 2) == 0, jnp.where(strip == strips - 1, HALO + rows, 2 * HALO + rows)


def by_side(even, fill, first, second):
    @pl.when(even)
    def _():
        fill(first, second)

    @pl.when(jnp.logical_not(even))
    def _():
        fill(second, first)


def pack_kernel(
    guess, cond_x, cond_y, source, inflow, own, to_core, to_x, to_both, halo_a, halo_b, coefs, coarse,
    guess_in, coefs_in, inflow_in, spare, sems,
):
    rows, columns = guess.shape
    groups, member = lax.axis_size("tm"), lax.axis_index("tm")
    width = columns // groups
    chunks = width // LANE

    def at(column):
        return pl.ds(pl.multiple_of(column, LANE), LANE)

    around = jnp.clip(width * member - LANE, 0, columns - width - 2 * LANE)
    span = pl.ds(pl.multiple_of(around, LANE), width + 2 * LANE)
    copies = [pltpu.make_async_copy(guess, guess_in, sems.at[0])]
    for slot, ref in enumerate((cond_x, cond_y, source)):
        copies.append(pltpu.make_async_copy(ref.at[:, span], coefs_in.at[slot], sems.at[1 + slot]))
    copies.append(pltpu.make_async_copy(inflow, inflow_in, sems.at[4]))
    for copy in copies:
        copy.start()
    copies[0].wait()
    for slot, out in enumerate((own, to_core, to_x, to_both)):
        target = member ^ slot
        first = width * target
        for chunk in range(chunks):
            out[chunk * rows : (chunk + 1) * rows] = guess_in[:, at(first + chunk * LANE)]
        left = guess_in[:, at(jnp.maximum(first - LANE, 0))]
        right = guess_in[:, at(jnp.minimum(first + width, columns - LANE))]
        spare[:rows] = fringe_of(left, right, target, FRINGE)
        out[chunks * rows : chunks * rows + rows // 4] = fold(spare, rows)
    for copy in copies[1:]:
        copy.wait()
    skip = width * member - around
    for slot in range(3):
        for chunk in range(chunks):
            coefs[slot, chunk] = coefs_in[slot, :, at(skip + chunk * LANE)]
        left = coefs_in[slot, :, at(jnp.maximum(skip - LANE, 0))]
        right = coefs_in[slot, :, at(jnp.minimum(skip + width, width + LANE))]
        coefs[slot, chunks] = fringe_of(left, right, member, FRINGE)
    first, half = width // 2 * member, chunks // 2
    for chunk in range(half):
        coarse[chunk] = inflow_in[:, at(first + chunk * LANE)]
    left = inflow_in[:, at(jnp.maximum(first - LANE, 0))]
    right = inflow_in[:, at(jnp.minimum(first + width // 2, columns // 2 - LANE))]
    coarse[half] = fringe_of(left, right, member, FRINGE // 2)

    def take(halo, bottom):
        base = fringe = 0
        for slot, deep in enumerate(COEF_ROWS):
            edge = slice(rows - deep, rows) if bottom else slice(0, deep)
            for chunk in range(chunks):
                halo[base : base + deep] = coefs[slot, chunk, edge]
                base += deep
            spare[fringe : fringe + deep] = coefs[slot, chunks, edge]
            fringe += deep
        halo[base : base + fringe // 4] = fold(spare, fringe)
        base += fringe // 4
        edge = slice(rows // 2 - COARSE_ROWS, rows // 2) if bottom else slice(0, COARSE_ROWS)
        for chunk in range(half + 1):
            halo[base : base + COARSE_ROWS] = coarse[chunk, edge]
            base += COARSE_ROWS

    def fill(below, above):
        take(below, True)
        take(above, False)

    by_side(sides(rows)[0], fill, halo_a, halo_b)


def edge_kernel(own, from_core, from_x, from_both, edge_a, edge_b, fields, spare):
    member = lax.axis_index("tm")
    chunks, rows = fields.shape[1] - 1, fields.shape[2]
    for slot, ref in enumerate((own, from_core, from_x, from_both)):
        target = fields.at[member ^ slot]
        for chunk in range(chunks):
            target[chunk] = ref[chunk * rows : (chunk + 1) * rows]
        unfold(ref[chunks * rows : chunks * rows + rows // 4], target.at[chunks], rows)

    def take(edge, bottom):
        base = fringe = 0
        for group, deep in enumerate(FIELD_ROWS):
            here = slice(rows - deep, rows) if bottom else slice(0, deep)
            for chunk in range(chunks):
                edge[base : base + deep] = fields[group, chunk, here]
                base += deep
            spare[fringe : fringe + deep] = fields[group, chunks, here]
            fringe += deep
        fringe = (fringe + 3) // 4 * 4
        edge[base : base + fringe // 4] = fold(spare, fringe)

    def fill(below, above):
        take(below, True)
        take(above, False)

    spare[...] = jnp.zeros_like(spare)
    by_side(sides(rows)[0], fill, edge_a, edge_b)


def spread(value):
    rows, lanes = value.shape
    value = value.reshape(rows // 8, 8, lanes)
    row_even = lax.broadcasted_iota(jnp.int32, value.shape, 1) % 2 == 0
    lane_even = lax.broadcasted_iota(jnp.int32, value.shape, 2) % 2 == 0
    value = value + jnp.where(row_even, pltpu.roll(value, 7, 1), pltpu.roll(value, 1, 1))
    value = value + jnp.where(lane_even, pltpu.roll(value, lanes - 1, 2), pltpu.roll(value, 1, 2))
    return (value * 0.25).reshape(rows, lanes)


def weights(cond_x, cond_y, chunk, rows, width, limit, out):
    diagonal, up, west = out
    chunks = cond_x.shape[0]
    first, count = rows
    here = slice(first, first + count)
    own_x, own_y = cond_x[chunk, here], cond_y[chunk, here]
    above = cond_x[chunk, first - width : first - width + count]
    lane = lanes_of(own_x.shape)
    row = lax.broadcasted_iota(jnp.int32, own_x.shape, 0)
    before = pltpu.roll(cond_y[(chunk - 1) % chunks, here], width, 1)
    beside = jnp.where(lane < width, before, pltpu.roll(own_y, width, 1))
    diagonal[chunk, here] = 1.0 - ((own_x + above) + (own_y + beside))
    up[chunk, here] = jnp.where(row < limit - first, above, 0.0)
    if chunk == chunks - 1:
        closed = jnp.where(lax.axis_index("tm") == lax.axis_size("tm") - 1, width, 0)
        beside = jnp.where(lane < closed, 0.0, beside)
    west[chunk, here] = beside


def prepare_kernel(
    coefs, coarse, coef_a, coef_b,
    cond_x, cond_y, response, diagonal, up, west, coarse_x, coarse_y, coarse_d, coarse_u, coarse_w, error, carried,
    tall, spare, source, work,
):
    _, chunks, rows, _ = coefs.shape
    chunks, half = chunks - 1, (chunks - 1) // 2
    low = HALO + rows
    even, limit = sides(rows)
    targets = (cond_x, cond_y, source)
    tall[...] = jnp.zeros_like(tall)

    def give(halo, below):
        base = fringe = 0
        for ref, deep in zip(targets, COEF_ROWS):
            first = low if below else HALO - deep
            for chunk in range(chunks):
                ref[chunk, first : first + deep] = halo[base : base + deep]
                base += deep
        total = sum(COEF_ROWS)
        unfold(halo[base : base + total // 4], spare, total)
        base += total // 4
        for ref, deep in zip(targets, COEF_ROWS):
            first = low if below else HALO - deep
            ref[chunks, first : first + deep] = spare[fringe : fringe + deep]
            fringe += deep
        first = 4 + rows // 2 if below else 4 - COARSE_ROWS
        for chunk in range(half + 1):
            tall[chunk, first : first + COARSE_ROWS] = halo[base : base + COARSE_ROWS]
            base += COARSE_ROWS

    def fill(below, above):
        give(below, True)
        give(above, False)

    by_side(even, fill, coef_a, coef_b)
    for slot, ref in enumerate(targets):
        ref[:, HALO:low] = coefs[slot]
    tall[:, 4 : 4 + rows // 2] = coarse[...]
    for chunk in range(chunks + 1):
        weights(cond_x, cond_y, chunk, reach(rows, 9), 1, limit, (diagonal, up, west))
    near = slice(HALO - 8, low + 8)
    for chunk in range(chunks + 1):
        coarse_x[chunk, near] = spread(cond_x[chunk, near])
        coarse_y[chunk, near] = spread(cond_y[chunk, near])
    for chunk in range(chunks + 1):
        weights(coarse_x, coarse_y, chunk, reach(rows, 4), 2, limit, (coarse_d, coarse_u, coarse_w))
    lane = lanes_of((8, LANE))
    twice = lax.broadcasted_iota(jnp.int32, (8, LANE), 0) // 2
    for chunk in range(chunks + 1):
        side = chunk % 2 * (LANE // 2)
        pick = lane // 2 + (side if chunk < chunks else jnp.where(lane < LANE // 2, 0, LANE // 2))
        for part in range((rows // 2 + 8) // 8):
            wide = jnp.take_along_axis(tall[chunk // 2, 8 * part : 8 * part + 8], pick, axis=1)
            for end in range(2):
                at = HALO - 8 + 16 * part + 8 * end
                error[chunk, at : at + 8] = jnp.take_along_axis(wide, twice + 4 * end, axis=0)
    fine = (diagonal, up, cond_x, cond_y, west)
    stops = [source] + [work.at[number] for number in range(FINE_STEPS - 1)]
    for number in range(FINE_STEPS - 1):
        sweep([(stops[number], stops[number + 1], span(rows, 8 - number), None)], 1, fine)
    first, count = reach(rows, 6)
    here = slice(first, first + count)
    for chunk in range(chunks + 1):
        total = source[chunk, here]
        for number in range(FINE_STEPS - 1):
            total = total + work[number, chunk, here]
        response[chunk, here] = total
    sweep([(error, carried, span(rows, 4), None)], 2, (coarse_d, coarse_u, coarse_x, coarse_y, coarse_w))


def sweep(items, width, factors):
    diagonal, up, down, east, west = factors
    chunks = diagonal.shape[0]
    lane = lanes_of((8, LANE))
    origin = min(item[2][0] for item in items)
    end = max(item[2][1] for item in items)
    for first in range(origin, end, 8):
        here, above, below = (slice(first + move, first + move + 8) for move in (0, -width, width))
        active = [item for item in items if item[2][0] < first + 8 and item[2][1] > first]

        def load(values, chunk):
            value = values[chunk % chunks, here]
            return value, pltpu.roll(value, LANE - width, 1), pltpu.roll(value, width, 1)

        states = [[load(item[0], -1), load(item[0], 0)] for item in active]
        for chunk in range(chunks):
            own = [ref[chunk, here] for ref in (diagonal, up, down, east, west)]
            for (values, put, _, added), state in zip(active, states):
                before, now = state
                after = load(values, chunk + 1)
                right = jnp.where(lane < LANE - width, now[1], after[1])
                left = jnp.where(lane < width, before[2], now[2])
                total = (own[3] * right + own[4] * left) + (own[2] * values[chunk, below] + own[1] * values[chunk, above])
                total = own[0] * now[0] + total
                put[chunk, here] = total if added is None else total + added(chunk, here)
                state[:] = [now, after]


def reach(rows, deep):
    return HALO - deep, (rows + 2 * deep + 7) // 8 * 8


def span(rows, deep):
    return HALO - deep, HALO + rows + deep


def main_kernel(
    fields, cond_x, cond_y, response, diagonal, up, west, coarse_x, coarse_y, coarse_d, coarse_u, coarse_w,
    start_error, carried, edge_a, edge_b, own, to_core, to_x, to_both,
    guess, work, error, spare,
):
    groups, chunks, rows, _ = fields.shape
    chunks -= 1
    low = HALO + rows
    given = groups - 1

    def give(edge, below):
        base = fringe = 0
        for group, deep in enumerate(FIELD_ROWS):
            first = low if below else HALO - deep
            for chunk in range(chunks):
                guess[group, chunk, first : first + deep] = edge[base : base + deep]
                base += deep
        total = (sum(FIELD_ROWS) + 3) // 4 * 4
        unfold(edge[base : base + total // 4], spare, total)
        for group, deep in enumerate(FIELD_ROWS):
            first = low if below else HALO - deep
            guess[group, chunks, first : first + deep] = spare[fringe : fringe + deep]
            fringe += deep

    def fill(below, above):
        give(below, True)
        give(above, False)

    by_side(sides(rows)[0], fill, edge_a, edge_b)
    for group in range(given):
        guess[group, :, HALO:low] = fields[group]
    fine = (diagonal, up, cond_x, cond_y, west)
    coarse = (coarse_d, coarse_u, coarse_x, coarse_y, coarse_w)

    def add_response(chunk, here):
        return response[chunk, here]

    def propagate(slots, deeps):
        for number in range(FINE_STEPS):
            items = []
            for place, (slot, deep) in enumerate(zip(slots, deeps)):
                first, second = work.at[2 * place], work.at[2 * place + 1]
                stops = [guess.at[slot], first, second, first, guess.at[slot + given]]
                needed = span(rows, deep + FINE_STEPS - 1 - number)
                added = add_response if number == FINE_STEPS - 1 else None
                items.append((stops[number], stops[number + 1], needed, added))
            sweep(items, 1, fine)

    propagate((0, 1, 2), (6, 4, 0))
    propagate((3, 4), (2, 0))

    def residual(group, chunk, here):
        reached = given if group == 1 else 2 * given - 2 + group
        return spread(guess[reached, chunk, here] - guess[given - 1 + group, chunk, here])

    first, count = reach(rows, 2 * (groups - 2))
    here = slice(first, first + count)
    for chunk in range(chunks + 1):
        error[1, chunk, here] = carried[chunk, here] + residual(1, chunk, here)
    for group in range(2, groups):
        needed = span(rows, 2 * (groups - 1 - group))
        sweep([(error.at[group - 1], error.at[group], needed, functools.partial(residual, group))], 2, coarse)
    error[0, :, HALO:low] = start_error[:, HALO:low]

    member = lax.axis_index("tm")
    for slot, out in enumerate((own, to_core, to_x, to_both)):
        group = member ^ slot
        relaxed = jnp.where(group == 0, 0, given - 1 + group)
        for chunk in range(chunks):
            out[:, piece(chunk)] = guess[relaxed, chunk, HALO:low] + error[group, chunk, HALO:low]


def unpack_kernel(own, from_core, from_x, from_both, out, sems):
    width = own.shape[1]
    member = lax.axis_index("tm")
    copies = []
    for slot, ref in enumerate((own, from_core, from_x, from_both)):
        at = pl.ds(pl.multiple_of((member ^ slot) * width, LANE), width)
        copies.append(pltpu.make_async_copy(ref, out.at[0, :, at], sems.at[slot]))
    for copy in copies:
        copy.start()
    for copy in copies:
        copy.wait()


def call(kernel, outs, scratch, operands, whole=(), outside=False, copies=0):
    vmem, anywhere = (pl.BlockSpec(memory_space=space) for space in (pltpu.VMEM, pltpu.HBM))
    specs = [anywhere if slot in whole else vmem for slot in range(len(operands))]
    operands = [
        pltpu.with_memory_space_constraint(value, pltpu.HBM) if slot in whole else value
        for slot, value in enumerate(operands)
    ]
    return pl.pallas_call(
        kernel,
        out_shape=[jax.ShapeDtypeStruct(shape, jnp.float32) for shape in outs],
        in_specs=specs,
        out_specs=[anywhere if outside else vmem] * len(outs),
        scratch_shapes=[pltpu.VMEM(shape, jnp.float32) for shape in scratch]
        + ([pltpu.SemaphoreType.DMA((copies,))] if copies else []),
        compiler_params=pltpu.CompilerParams(vmem_limit_bytes=VMEM_LIMIT),
    )(*operands)


def shards(guesses, cond_x, cond_y, source, inflow):
    groups, strips = lax.axis_size("tm"), lax.axis_size("space")
    rows, columns = cond_x.shape
    fits = groups == len(FIELD_ROWS) + 1 and strips % 2 == 0 and rows == 16
    if not fits or columns % (2 * groups * LANE) != 0:
        return general_shards(guesses, cond_x, cond_y, source, inflow)
    own = columns // groups
    chunks = own // LANE
    pairs_a = [(i, i ^ 1) for i in range(strips)]
    pairs_b = [(i, j) for k in range(1, strips - 1, 2) for i, j in ((k, k + 1), (k + 1, k))]

    def trade(blocks):
        moved = [blocks[0]]
        for slot in range(1, groups):
            moved.append(lax.ppermute(blocks[slot], "tm", [(i, i ^ slot) for i in range(groups)]))
        return moved

    def whole(count):
        return (count + 7) // 8 * 8

    def folded(count):
        return count * chunks + (count + 3) // 4

    block = (whole(folded(rows)), LANE)
    halo = (whole(folded(sum(COEF_ROWS)) + (chunks // 2 + 1) * COARSE_ROWS), LANE)
    edge = (whole(folded(sum(FIELD_ROWS))), LANE)
    spare = (32, LANE)
    *blocks, halo_a, halo_b, coefs, coarse = call(
        pack_kernel,
        [block] * groups + [halo, halo, (3, chunks + 1, rows, LANE), (chunks // 2 + 1, rows // 2, LANE)],
        [(rows, columns), (3, rows, own + 2 * LANE), (rows // 2, columns // 2), spare],
        [guesses[0], cond_x, cond_y, source, inflow], whole=range(5), copies=5,
    )
    coef_a = lax.ppermute(halo_a, "space", pairs_a)
    coef_b = lax.ppermute(halo_b, "space", pairs_b)
    blocks = trade(blocks)
    sent_a, sent_b, fields = call(edge_kernel, [edge, edge, (groups, chunks + 1, rows, LANE)], [spare], blocks)
    edge_a = lax.ppermute(sent_a, "space", pairs_a)
    edge_b = lax.ppermute(sent_b, "space", pairs_b)
    buffer = (chunks + 1, rows + 2 * HALO, LANE)
    prepared = call(
        prepare_kernel,
        [buffer] * 13,
        [(chunks // 2 + 1, rows // 2 + 8, LANE), spare, buffer, (FINE_STEPS - 1, *buffer)],
        [coefs, coarse, coef_a, coef_b],
    )
    blocks = call(
        main_kernel,
        [(rows, own)] * groups,
        [(3 * groups - 4, *buffer), (2 * groups - 2, *buffer), (groups, *buffer), spare],
        [fields, *prepared, edge_a, edge_b],
    )
    return call(unpack_kernel, [(1, rows, columns)], [], trade(blocks), outside=True, copies=groups)[0]


def solution(mesh):
    return jax.shard_map(
        shards,
        mesh=mesh,
        in_specs=(
            P("tm", "space", None),
            P("space", None),
            P("space", None),
            P("space", None),
            P("space", None),
        ),
        out_specs=P("tm", "space", None),
        check_vma=False,
    )
```

```python
import functools

import jax
import jax.numpy as jnp
from jax import lax
from jax.experimental import pallas as pl
from jax.experimental.pallas import tpu as pltpu
from jax.sharding import PartitionSpec as P

FINE_STEPS = 4
LANE = 128
FRINGE = 16
HALO = 16
COEF_ROWS = (10, 9, 9)
FIELD_ROWS = (10, 8, 4)
COARSE_ROWS = 3
VMEM_LIMIT = 40 * 1024 * 1024


def padded(value, sides, width):
    for axis, dim in sides:
        devices, length = (lax.axis_size(axis), value.shape[dim])
        up = [(i, (i + 1) % devices) for i in range(devices - 1)]
        down = [(j, i) for i, j in up]
        last = lax.slice_in_dim(value, length - width, length, axis=dim)
        leading = lax.slice_in_dim(value, 0, width, axis=dim)
        before = lax.ppermute(last, axis, up)
        after = lax.ppermute(leading, axis, down)
        value = jnp.concatenate([before, value, after], axis=dim)
    return value


def from_behind(value, axis, steps):
    count = lax.axis_size(axis)
    leading, last = (max(0, -steps), min(count, count - steps))
    return lax.ppermute(value, axis, [(source, source + steps) for source in range(leading, last)])


def interior(field_ext, cond_rows, cond_cols):
    centre = field_ext[1:-1]
    flux_sum = cond_rows[1:-1] * (field_ext[2:] - centre) - cond_rows[:-2] * (
        centre - field_ext[:-2]
    )
    widened = jnp.pad(centre, ((0, 0), (1, 1)))
    cond_own = cond_cols[1:-1]
    cond_west = jnp.pad(cond_own, ((0, 0), (1, 0)))[:, :-1]
    flux_sum = (
        flux_sum + cond_own * (widened[:, 2:] - centre) - cond_west * (centre - widened[:, :-2])
    )
    return centre + flux_sum


def propagate(field, coef_pad):
    strip_rows = field.shape[0]
    cond_rows = coef_pad[0, 3 : strip_rows + 5]
    cond_cols = coef_pad[1, 3 : strip_rows + 5]
    source_rows = coef_pad[2, 4 : strip_rows + 4]
    for section in range(FINE_STEPS):
        extended = padded(field, (("space", 0),), 1)
        field = interior(extended, cond_rows, cond_cols) + source_rows
    return field


def restrict(field):
    lead = field.shape[:-2]
    shaped = field.reshape(lead + (field.shape[-2] // 2, 2, field.shape[-1] // 2, 2))
    return jnp.mean(shaped, axis=(-3, -1))


def general_shards(guesses, cond_x, cond_y, source, inflow):
    strip_rows = cond_x.shape[0]
    columns = cond_x.shape[1]
    stacked = jnp.stack([cond_x, cond_y, source])
    edge_rows = from_behind(cond_x[strip_rows - 2 :], "space", 1)
    cond_upper = jnp.concatenate([jnp.zeros((2, columns), jnp.float32), edge_rows], axis=0)
    blank_rows = jnp.zeros((4, columns), jnp.float32)
    upper = jnp.stack([cond_upper, blank_rows, blank_rows])
    lower = jnp.zeros((3, 4, columns), jnp.float32)
    coef_pad = jnp.concatenate([upper, stacked, lower], axis=1)
    first_group = lax.axis_index("tm") == 0
    c_point = guesses[0]
    first_pass = propagate(c_point, coef_pad)
    received = from_behind(first_pass, "tm", 1)
    relaxed = jnp.where(first_group, c_point, received)
    second_pass = propagate(relaxed, coef_pad)
    fine_next = from_behind(second_pass, "tm", 1)
    residual = restrict(fine_next - relaxed)
    residual = jnp.where(first_group, 0.0, residual)
    coarse_coef = restrict(coef_pad[:2, 2 : strip_rows + 6])

    def chain_round(index, error_field):
        extended = padded(error_field, (("space", 0),), 1)
        stepped = interior(extended, coarse_coef[0], coarse_coef[1])
        arrived = from_behind(stepped, "tm", 1)
        return jnp.where(first_group, inflow, arrived + residual)

    start_error = jnp.where(first_group, inflow, jnp.zeros_like(residual))
    error_field = lax.fori_loop(0, lax.axis_size("tm") - 1, chain_round, start_error)
    widened = jnp.repeat(jnp.repeat(error_field, 2, axis=0), 2, axis=1)
    return (relaxed + widened)[None]


def piece(chunk):
    return slice(chunk * LANE, (chunk + 1) * LANE)


def lanes_of(shape):
    return lax.broadcasted_iota(jnp.int32, shape, len(shape) - 1)


def fringe_of(left, right, member, width):
    lane = lanes_of(left.shape)
    last = lax.axis_size("tm") - 1
    value = jnp.where(lane < jnp.where(member < last, width, 0), right, 0.0)
    return jnp.where(lane >= jnp.where(member > 0, LANE - width, LANE), left, value)


def fold(source, rows):
    part = rows // 4
    total = source[:part]
    for turn in range(1, 4):
        total = total + pltpu.roll(source[turn * part : (turn + 1) * part], 2 * FRINGE * turn, 1)
    return total


def unfold(folded, target, rows):
    part = rows // 4
    lane = lanes_of(folded.shape)
    used = (lane < FRINGE) | (lane >= LANE - FRINGE)
    for turn in range(4):
        turned = pltpu.roll(folded, LANE - 2 * FRINGE * turn, 1) if turn else folded
        target[turn * part : (turn + 1) * part] = jnp.where(used, turned, 0.0)


def sides(rows):
    strip, strips = lax.axis_index("space"), lax.axis_size("space")
    return lax.rem(strip, 2) == 0, jnp.where(strip == strips - 1, HALO + rows, 2 * HALO + rows)


def by_side(even, fill, first, second):
    @pl.when(even)
    def _():
        fill(first, second)

    @pl.when(jnp.logical_not(even))
    def _():
        fill(second, first)


def pack_kernel(
    guess, cond_x, cond_y, source, inflow, own, to_core, to_x, to_both, halo_a, halo_b, coefs, coarse,
    guess_in, coefs_in, inflow_in, spare, sems,
):
    rows, columns = guess.shape
    groups, member = lax.axis_size("tm"), lax.axis_index("tm")
    width = columns // groups
    chunks = width // LANE

    def at(column):
        return pl.ds(pl.multiple_of(column, LANE), LANE)

    around = jnp.clip(width * member - LANE, 0, columns - width - 2 * LANE)
    span = pl.ds(pl.multiple_of(around, LANE), width + 2 * LANE)
    copies = [pltpu.make_async_copy(guess, guess_in, sems.at[0])]
    for slot, ref in enumerate((cond_x, cond_y, source)):
        copies.append(pltpu.make_async_copy(ref.at[:, span], coefs_in.at[slot], sems.at[1 + slot]))
    copies.append(pltpu.make_async_copy(inflow, inflow_in, sems.at[4]))
    for copy in copies:
        copy.start()
    copies[0].wait()
    for slot, out in enumerate((own, to_core, to_x, to_both)):
        target = member ^ slot
        first = width * target
        for chunk in range(chunks):
            out[chunk * rows : (chunk + 1) * rows] = guess_in[:, at(first + chunk * LANE)]
        left = guess_in[:, at(jnp.maximum(first - LANE, 0))]
        right = guess_in[:, at(jnp.minimum(first + width, columns - LANE))]
        spare[:rows] = fringe_of(left, right, target, FRINGE)
        out[chunks * rows : chunks * rows + rows // 4] = fold(spare, rows)
    for copy in copies[1:]:
        copy.wait()
    skip = width * member - around
    for slot in range(3):
        for chunk in range(chunks):
            coefs[slot, chunk] = coefs_in[slot, :, at(skip + chunk * LANE)]
        left = coefs_in[slot, :, at(jnp.maximum(skip - LANE, 0))]
        right = coefs_in[slot, :, at(jnp.minimum(skip + width, width + LANE))]
        coefs[slot, chunks] = fringe_of(left, right, member, FRINGE)
    first, half = width // 2 * member, chunks // 2
    for chunk in range(half):
        coarse[chunk] = inflow_in[:, at(first + chunk * LANE)]
    left = inflow_in[:, at(jnp.maximum(first - LANE, 0))]
    right = inflow_in[:, at(jnp.minimum(first + width // 2, columns // 2 - LANE))]
    coarse[half] = fringe_of(left, right, member, FRINGE // 2)

    def take(halo, bottom):
        base = fringe = 0
        for slot, deep in enumerate(COEF_ROWS):
            edge = slice(rows - deep, rows) if bottom else slice(0, deep)
            for chunk in range(chunks):
                halo[base : base + deep] = coefs[slot, chunk, edge]
                base += deep
            spare[fringe : fringe + deep] = coefs[slot, chunks, edge]
            fringe += deep
        halo[base : base + fringe // 4] = fold(spare, fringe)
        base += fringe // 4
        edge = slice(rows // 2 - COARSE_ROWS, rows // 2) if bottom else slice(0, COARSE_ROWS)
        for chunk in range(half + 1):
            halo[base : base + COARSE_ROWS] = coarse[chunk, edge]
            base += COARSE_ROWS

    def fill(below, above):
        take(below, True)
        take(above, False)

    by_side(sides(rows)[0], fill, halo_a, halo_b)


def edge_kernel(own, from_core, from_x, from_both, edge_a, edge_b, fields, spare):
    member = lax.axis_index("tm")
    chunks, rows = fields.shape[1] - 1, fields.shape[2]
    for slot, ref in enumerate((own, from_core, from_x, from_both)):
        target = fields.at[member ^ slot]
        for chunk in range(chunks):
            target[chunk] = ref[chunk * rows : (chunk + 1) * rows]
        unfold(ref[chunks * rows : chunks * rows + rows // 4], target.at[chunks], rows)

    def take(edge, bottom):
        base = fringe = 0
        for group, deep in enumerate(FIELD_ROWS):
            here = slice(rows - deep, rows) if bottom else slice(0, deep)
            for chunk in range(chunks):
                edge[base : base + deep] = fields[group, chunk, here]
                base += deep
            spare[fringe : fringe + deep] = fields[group, chunks, here]
            fringe += deep
        fringe = (fringe + 3) // 4 * 4
        edge[base : base + fringe // 4] = fold(spare, fringe)

    def fill(below, above):
        take(below, True)
        take(above, False)

    spare[...] = jnp.zeros_like(spare)
    by_side(sides(rows)[0], fill, edge_a, edge_b)


def spread(value):
    rows, lanes = value.shape
    value = value.reshape(rows // 8, 8, lanes)
    row_even = lax.broadcasted_iota(jnp.int32, value.shape, 1) % 2 == 0
    lane_even = lax.broadcasted_iota(jnp.int32, value.shape, 2) % 2 == 0
    value = value + jnp.where(row_even, pltpu.roll(value, 7, 1), pltpu.roll(value, 1, 1))
    value = value + jnp.where(lane_even, pltpu.roll(value, lanes - 1, 2), pltpu.roll(value, 1, 2))
    return (value * 0.25).reshape(rows, lanes)


def weights(cond_x, cond_y, chunk, rows, width, limit, out):
    diagonal, up, west = out
    chunks = cond_x.shape[0]
    first, count = rows
    here = slice(first, first + count)
    own_x, own_y = cond_x[chunk, here], cond_y[chunk, here]
    above = cond_x[chunk, first - width : first - width + count]
    lane = lanes_of(own_x.shape)
    row = lax.broadcasted_iota(jnp.int32, own_x.shape, 0)
    before = pltpu.roll(cond_y[(chunk - 1) % chunks, here], width, 1)
    beside = jnp.where(lane < width, before, pltpu.roll(own_y, width, 1))
    diagonal[chunk, here] = 1.0 - ((own_x + above) + (own_y + beside))
    up[chunk, here] = jnp.where(row < limit - first, above, 0.0)
    if chunk == chunks - 1:
        closed = jnp.where(lax.axis_index("tm") == lax.axis_size("tm") - 1, width, 0)
        beside = jnp.where(lane < closed, 0.0, beside)
    west[chunk, here] = beside


def prepare_kernel(
    coefs, coarse, coef_a, coef_b,
    cond_x, cond_y, response, diagonal, up, west, coarse_x, coarse_y, coarse_d, coarse_u, coarse_w, error, carried,
    tall, spare, source, work,
):
    _, chunks, rows, _ = coefs.shape
    chunks, half = chunks - 1, (chunks - 1) // 2
    low = HALO + rows
    even, limit = sides(rows)
    targets = (cond_x, cond_y, source)
    tall[...] = jnp.zeros_like(tall)

    def give(halo, below):
        base = fringe = 0
        for ref, deep in zip(targets, COEF_ROWS):
            first = low if below else HALO - deep
            for chunk in range(chunks):
                ref[chunk, first : first + deep] = halo[base : base + deep]
                base += deep
        total = sum(COEF_ROWS)
        unfold(halo[base : base + total // 4], spare, total)
        base += total // 4
        for ref, deep in zip(targets, COEF_ROWS):
            first = low if below else HALO - deep
            ref[chunks, first : first + deep] = spare[fringe : fringe + deep]
            fringe += deep
        first = 4 + rows // 2 if below else 4 - COARSE_ROWS
        for chunk in range(half + 1):
            tall[chunk, first : first + COARSE_ROWS] = halo[base : base + COARSE_ROWS]
            base += COARSE_ROWS

    def fill(below, above):
        give(below, True)
        give(above, False)

    by_side(even, fill, coef_a, coef_b)
    for slot, ref in enumerate(targets):
        ref[:, HALO:low] = coefs[slot]
    tall[:, 4 : 4 + rows // 2] = coarse[...]
    for chunk in range(chunks + 1):
        weights(cond_x, cond_y, chunk, reach(rows, 9), 1, limit, (diagonal, up, west))
    near = slice(HALO - 8, low + 8)
    for chunk in range(chunks + 1):
        coarse_x[chunk, near] = spread(cond_x[chunk, near])
        coarse_y[chunk, near] = spread(cond_y[chunk, near])
    for chunk in range(chunks + 1):
        weights(coarse_x, coarse_y, chunk, reach(rows, 4), 2, limit, (coarse_d, coarse_u, coarse_w))
    lane = lanes_of((8, LANE))
    twice = lax.broadcasted_iota(jnp.int32, (8, LANE), 0) // 2
    for chunk in range(chunks + 1):
        side = chunk % 2 * (LANE // 2)
        pick = lane // 2 + (side if chunk < chunks else jnp.where(lane < LANE // 2, 0, LANE // 2))
        for part in range((rows // 2 + 8) // 8):
            wide = jnp.take_along_axis(tall[chunk // 2, 8 * part : 8 * part + 8], pick, axis=1)
            for end in range(2):
                at = HALO - 8 + 16 * part + 8 * end
                error[chunk, at : at + 8] = jnp.take_along_axis(wide, twice + 4 * end, axis=0)
    fine = (diagonal, up, cond_x, cond_y, west)
    stops = [source] + [work.at[number] for number in range(FINE_STEPS - 1)]
    for number in range(FINE_STEPS - 1):
        sweep([(stops[number], stops[number + 1], span(rows, 8 - number), None)], 1, fine)
    first, count = reach(rows, 6)
    here = slice(first, first + count)
    for chunk in range(chunks + 1):
        total = source[chunk, here]
        for number in range(FINE_STEPS - 1):
            total = total + work[number, chunk, here]
        response[chunk, here] = total
    sweep([(error, carried, span(rows, 4), None)], 2, (coarse_d, coarse_u, coarse_x, coarse_y, coarse_w))


def sweep(items, width, factors):
    diagonal, up, down, east, west = factors
    chunks = diagonal.shape[0]
    lane = lanes_of((8, LANE))
    origin = min(item[2][0] for item in items)
    end = max(item[2][1] for item in items)
    for first in range(origin, end, 8):
        here, above, below = (slice(first + move, first + move + 8) for move in (0, -width, width))
        active = [item for item in items if item[2][0] < first + 8 and item[2][1] > first]

        def load(values, chunk):
            value = values[chunk % chunks, here]
            return value, pltpu.roll(value, LANE - width, 1), pltpu.roll(value, width, 1)

        states = [[load(item[0], -1), load(item[0], 0)] for item in active]
        ends = [tuple(state) for state in states]
        for chunk in range(chunks):
            own = [ref[chunk, here] for ref in (diagonal, up, down, east, west)]
            for (values, put, _, added), state, (last, start) in zip(active, states, ends):
                before, now = state
                after = start if chunk + 1 == chunks else last if chunk + 2 == chunks else load(values, chunk + 1)
                right = jnp.where(lane < LANE - width, now[1], after[1])
                left = jnp.where(lane < width, before[2], now[2])
                total = (own[3] * right + own[4] * left) + (own[2] * values[chunk, below] + own[1] * values[chunk, above])
                total = own[0] * now[0] + total
                put[chunk, here] = total if added is None else total + added(chunk, here)
                state[:] = [now, after]


def reach(rows, deep):
    return HALO - deep, (rows + 2 * deep + 7) // 8 * 8


def span(rows, deep):
    return HALO - deep, HALO + rows + deep


def main_kernel(
    fields, cond_x, cond_y, response, diagonal, up, west, coarse_x, coarse_y, coarse_d, coarse_u, coarse_w,
    start_error, carried, edge_a, edge_b, own, to_core, to_x, to_both,
    guess, work, error, spare,
):
    groups, chunks, rows, _ = fields.shape
    chunks -= 1
    low = HALO + rows
    given = groups - 1

    def give(edge, below):
        base = fringe = 0
        for group, deep in enumerate(FIELD_ROWS):
            first = low if below else HALO - deep
            for chunk in range(chunks):
                guess[group, chunk, first : first + deep] = edge[base : base + deep]
                base += deep
        total = (sum(FIELD_ROWS) + 3) // 4 * 4
        unfold(edge[base : base + total // 4], spare, total)
        for group, deep in enumerate(FIELD_ROWS):
            first = low if below else HALO - deep
            guess[group, chunks, first : first + deep] = spare[fringe : fringe + deep]
            fringe += deep

    def fill(below, above):
        give(below, True)
        give(above, False)

    by_side(sides(rows)[0], fill, edge_a, edge_b)
    for group in range(given):
        guess[group, :, HALO:low] = fields[group]
    fine = (diagonal, up, cond_x, cond_y, west)
    coarse = (coarse_d, coarse_u, coarse_x, coarse_y, coarse_w)

    def add_response(chunk, here):
        return response[chunk, here]

    def propagate(slots, deeps):
        for number in range(FINE_STEPS):
            items = []
            for place, (slot, deep) in enumerate(zip(slots, deeps)):
                first, second = work.at[2 * place], work.at[2 * place + 1]
                stops = [guess.at[slot], first, second, first, guess.at[slot + given]]
                needed = span(rows, deep + FINE_STEPS - 1 - number)
                added = add_response if number == FINE_STEPS - 1 else None
                items.append((stops[number], stops[number + 1], needed, added))
            sweep(items, 1, fine)

    propagate((0, 1, 2), (6, 4, 0))
    propagate((3, 4), (2, 0))

    def residual(group, chunk, here):
        reached = given if group == 1 else 2 * given - 2 + group
        return spread(guess[reached, chunk, here] - guess[given - 1 + group, chunk, here])

    first, count = reach(rows, 2 * (groups - 2))
    here = slice(first, first + count)
    for chunk in range(chunks + 1):
        error[1, chunk, here] = carried[chunk, here] + residual(1, chunk, here)
    for group in range(2, groups):
        needed = span(rows, 2 * (groups - 1 - group))
        sweep([(error.at[group - 1], error.at[group], needed, functools.partial(residual, group))], 2, coarse)
    error[0, :, HALO:low] = start_error[:, HALO:low]

    member = lax.axis_index("tm")
    for slot, out in enumerate((own, to_core, to_x, to_both)):
        group = member ^ slot
        relaxed = jnp.where(group == 0, 0, given - 1 + group)
        for chunk in range(chunks):
            out[:, piece(chunk)] = guess[relaxed, chunk, HALO:low] + error[group, chunk, HALO:low]


def unpack_kernel(own, from_core, from_x, from_both, out, sems):
    width = own.shape[1]
    member = lax.axis_index("tm")
    copies = []
    for slot, ref in enumerate((own, from_core, from_x, from_both)):
        at = pl.ds(pl.multiple_of((member ^ slot) * width, LANE), width)
        copies.append(pltpu.make_async_copy(ref, out.at[0, :, at], sems.at[slot]))
    for copy in copies:
        copy.start()
    for copy in copies:
        copy.wait()


def call(kernel, outs, scratch, operands, whole=(), outside=False, copies=0):
    vmem, anywhere = (pl.BlockSpec(memory_space=space) for space in (pltpu.VMEM, pltpu.HBM))
    specs = [anywhere if slot in whole else vmem for slot in range(len(operands))]
    operands = [
        pltpu.with_memory_space_constraint(value, pltpu.HBM) if slot in whole else value
        for slot, value in enumerate(operands)
    ]
    return pl.pallas_call(
        kernel,
        out_shape=[jax.ShapeDtypeStruct(shape, jnp.float32) for shape in outs],
        in_specs=specs,
        out_specs=[anywhere if outside else vmem] * len(outs),
        scratch_shapes=[pltpu.VMEM(shape, jnp.float32) for shape in scratch]
        + ([pltpu.SemaphoreType.DMA((copies,))] if copies else []),
        compiler_params=pltpu.CompilerParams(vmem_limit_bytes=VMEM_LIMIT),
    )(*operands)


def shards(guesses, cond_x, cond_y, source, inflow):
    groups, strips = lax.axis_size("tm"), lax.axis_size("space")
    rows, columns = cond_x.shape
    fits = groups == len(FIELD_ROWS) + 1 and strips % 2 == 0 and rows == 16
    if not fits or columns % (2 * groups * LANE) != 0:
        return general_shards(guesses, cond_x, cond_y, source, inflow)
    own = columns // groups
    chunks = own // LANE
    pairs_a = [(i, i ^ 1) for i in range(strips)]
    pairs_b = [(i, j) for k in range(1, strips - 1, 2) for i, j in ((k, k + 1), (k + 1, k))]

    def trade(blocks):
        moved = [blocks[0]]
        for slot in range(1, groups):
            moved.append(lax.ppermute(blocks[slot], "tm", [(i, i ^ slot) for i in range(groups)]))
        return moved

    def whole(count):
        return (count + 7) // 8 * 8

    def folded(count):
        return count * chunks + (count + 3) // 4

    block = (whole(folded(rows)), LANE)
    halo = (whole(folded(sum(COEF_ROWS)) + (chunks // 2 + 1) * COARSE_ROWS), LANE)
    edge = (whole(folded(sum(FIELD_ROWS))), LANE)
    spare = (32, LANE)
    *blocks, halo_a, halo_b, coefs, coarse = call(
        pack_kernel,
        [block] * groups + [halo, halo, (3, chunks + 1, rows, LANE), (chunks // 2 + 1, rows // 2, LANE)],
        [(rows, columns), (3, rows, own + 2 * LANE), (rows // 2, columns // 2), spare],
        [guesses[0], cond_x, cond_y, source, inflow], whole=range(5), copies=5,
    )
    coef_a = lax.ppermute(halo_a, "space", pairs_a)
    coef_b = lax.ppermute(halo_b, "space", pairs_b)
    blocks = trade(blocks)
    sent_a, sent_b, fields = call(edge_kernel, [edge, edge, (groups, chunks + 1, rows, LANE)], [spare], blocks)
    edge_a = lax.ppermute(sent_a, "space", pairs_a)
    edge_b = lax.ppermute(sent_b, "space", pairs_b)
    buffer = (chunks + 1, rows + 2 * HALO, LANE)
    prepared = call(
        prepare_kernel,
        [buffer] * 13,
        [(chunks // 2 + 1, rows // 2 + 8, LANE), spare, buffer, (FINE_STEPS - 1, *buffer)],
        [coefs, coarse, coef_a, coef_b],
    )
    blocks = call(
        main_kernel,
        [(rows, own)] * groups,
        [(3 * groups - 4, *buffer), (2 * groups - 2, *buffer), (groups, *buffer), spare],
        [fields, *prepared, edge_a, edge_b],
    )
    return call(unpack_kernel, [(1, rows, columns)], [], trade(blocks), outside=True, copies=groups)[0]


def solution(mesh):
    return jax.shard_map(
        shards,
        mesh=mesh,
        in_specs=(
            P("tm", "space", None),
            P("space", None),
            P("space", None),
            P("space", None),
            P("space", None),
        ),
        out_specs=P("tm", "space", None),
        check_vma=False,
    )
```

```python
import functools

import jax
import jax.numpy as jnp
from jax import lax
from jax.experimental import pallas as pl
from jax.experimental.pallas import tpu as pltpu
from jax.sharding import PartitionSpec as P

FINE_STEPS = 4
LANE = 128
FRINGE = 16
HALO = 16
COEF_ROWS = (10, 9, 9)
FIELD_ROWS = (10, 8, 4)
COARSE_ROWS = 3
VMEM_LIMIT = 40 * 1024 * 1024


def padded(value, sides, width):
    for axis, dim in sides:
        devices, length = (lax.axis_size(axis), value.shape[dim])
        up = [(i, (i + 1) % devices) for i in range(devices - 1)]
        down = [(j, i) for i, j in up]
        last = lax.slice_in_dim(value, length - width, length, axis=dim)
        leading = lax.slice_in_dim(value, 0, width, axis=dim)
        before = lax.ppermute(last, axis, up)
        after = lax.ppermute(leading, axis, down)
        value = jnp.concatenate([before, value, after], axis=dim)
    return value


def from_behind(value, axis, steps):
    count = lax.axis_size(axis)
    leading, last = (max(0, -steps), min(count, count - steps))
    return lax.ppermute(value, axis, [(source, source + steps) for source in range(leading, last)])


def interior(field_ext, cond_rows, cond_cols):
    centre = field_ext[1:-1]
    flux_sum = cond_rows[1:-1] * (field_ext[2:] - centre) - cond_rows[:-2] * (
        centre - field_ext[:-2]
    )
    widened = jnp.pad(centre, ((0, 0), (1, 1)))
    cond_own = cond_cols[1:-1]
    cond_west = jnp.pad(cond_own, ((0, 0), (1, 0)))[:, :-1]
    flux_sum = (
        flux_sum + cond_own * (widened[:, 2:] - centre) - cond_west * (centre - widened[:, :-2])
    )
    return centre + flux_sum


def propagate(field, coef_pad):
    strip_rows = field.shape[0]
    cond_rows = coef_pad[0, 3 : strip_rows + 5]
    cond_cols = coef_pad[1, 3 : strip_rows + 5]
    source_rows = coef_pad[2, 4 : strip_rows + 4]
    for section in range(FINE_STEPS):
        extended = padded(field, (("space", 0),), 1)
        field = interior(extended, cond_rows, cond_cols) + source_rows
    return field


def restrict(field):
    lead = field.shape[:-2]
    shaped = field.reshape(lead + (field.shape[-2] // 2, 2, field.shape[-1] // 2, 2))
    return jnp.mean(shaped, axis=(-3, -1))


def general_shards(guesses, cond_x, cond_y, source, inflow):
    strip_rows = cond_x.shape[0]
    columns = cond_x.shape[1]
    stacked = jnp.stack([cond_x, cond_y, source])
    edge_rows = from_behind(cond_x[strip_rows - 2 :], "space", 1)
    cond_upper = jnp.concatenate([jnp.zeros((2, columns), jnp.float32), edge_rows], axis=0)
    blank_rows = jnp.zeros((4, columns), jnp.float32)
    upper = jnp.stack([cond_upper, blank_rows, blank_rows])
    lower = jnp.zeros((3, 4, columns), jnp.float32)
    coef_pad = jnp.concatenate([upper, stacked, lower], axis=1)
    first_group = lax.axis_index("tm") == 0
    c_point = guesses[0]
    first_pass = propagate(c_point, coef_pad)
    received = from_behind(first_pass, "tm", 1)
    relaxed = jnp.where(first_group, c_point, received)
    second_pass = propagate(relaxed, coef_pad)
    fine_next = from_behind(second_pass, "tm", 1)
    residual = restrict(fine_next - relaxed)
    residual = jnp.where(first_group, 0.0, residual)
    coarse_coef = restrict(coef_pad[:2, 2 : strip_rows + 6])

    def chain_round(index, error_field):
        extended = padded(error_field, (("space", 0),), 1)
        stepped = interior(extended, coarse_coef[0], coarse_coef[1])
        arrived = from_behind(stepped, "tm", 1)
        return jnp.where(first_group, inflow, arrived + residual)

    start_error = jnp.where(first_group, inflow, jnp.zeros_like(residual))
    error_field = lax.fori_loop(0, lax.axis_size("tm") - 1, chain_round, start_error)
    widened = jnp.repeat(jnp.repeat(error_field, 2, axis=0), 2, axis=1)
    return (relaxed + widened)[None]


def piece(chunk):
    return slice(chunk * LANE, (chunk + 1) * LANE)


def lanes_of(shape):
    return lax.broadcasted_iota(jnp.int32, shape, len(shape) - 1)


def fringe_of(left, right, member, width):
    lane = lanes_of(left.shape)
    last = lax.axis_size("tm") - 1
    value = jnp.where(lane < jnp.where(member < last, width, 0), right, 0.0)
    return jnp.where(lane >= jnp.where(member > 0, LANE - width, LANE), left, value)


def fold(source, rows):
    part = rows // 4
    total = source[:part]
    for turn in range(1, 4):
        total = total + pltpu.roll(source[turn * part : (turn + 1) * part], 2 * FRINGE * turn, 1)
    return total


def unfold(folded, target, rows):
    part = rows // 4
    lane = lanes_of(folded.shape)
    used = (lane < FRINGE) | (lane >= LANE - FRINGE)
    for turn in range(4):
        turned = pltpu.roll(folded, LANE - 2 * FRINGE * turn, 1) if turn else folded
        target[turn * part : (turn + 1) * part] = jnp.where(used, turned, 0.0)


def sides(rows):
    strip, strips = lax.axis_index("space"), lax.axis_size("space")
    return lax.rem(strip, 2) == 0, jnp.where(strip == strips - 1, HALO + rows, 2 * HALO + rows)


def by_side(even, fill, first, second):
    @pl.when(even)
    def _():
        fill(first, second)

    @pl.when(jnp.logical_not(even))
    def _():
        fill(second, first)


def pack_kernel(
    guess, cond_x, cond_y, source, inflow, own, to_core, to_x, to_both, halo_a, halo_b, coefs, coarse,
    guess_in, coefs_in, inflow_in, spare, sems,
):
    rows, columns = guess.shape
    groups, member = lax.axis_size("tm"), lax.axis_index("tm")
    width = columns // groups
    chunks = width // LANE

    def at(column):
        return pl.ds(pl.multiple_of(column, LANE), LANE)

    around = jnp.clip(width * member - LANE, 0, columns - width - 2 * LANE)
    span = pl.ds(pl.multiple_of(around, LANE), width + 2 * LANE)
    copies = [pltpu.make_async_copy(guess, guess_in, sems.at[0])]
    for slot, ref in enumerate((cond_x, cond_y, source)):
        copies.append(pltpu.make_async_copy(ref.at[:, span], coefs_in.at[slot], sems.at[1 + slot]))
    copies.append(pltpu.make_async_copy(inflow, inflow_in, sems.at[4]))
    for copy in copies:
        copy.start()
    copies[0].wait()
    for slot, out in enumerate((own, to_core, to_x, to_both)):
        target = member ^ slot
        first = width * target
        for chunk in range(chunks):
            out[chunk * rows : (chunk + 1) * rows] = guess_in[:, at(first + chunk * LANE)]
        left = guess_in[:, at(jnp.maximum(first - LANE, 0))]
        right = guess_in[:, at(jnp.minimum(first + width, columns - LANE))]
        spare[:rows] = fringe_of(left, right, target, FRINGE)
        out[chunks * rows : chunks * rows + rows // 4] = fold(spare, rows)
    for copy in copies[1:]:
        copy.wait()
    skip = width * member - around
    for slot in range(3):
        for chunk in range(chunks):
            coefs[slot, chunk] = coefs_in[slot, :, at(skip + chunk * LANE)]
        left = coefs_in[slot, :, at(jnp.maximum(skip - LANE, 0))]
        right = coefs_in[slot, :, at(jnp.minimum(skip + width, width + LANE))]
        coefs[slot, chunks] = fringe_of(left, right, member, FRINGE)
    first, half = width // 2 * member, chunks // 2
    for chunk in range(half):
        coarse[chunk] = inflow_in[:, at(first + chunk * LANE)]
    left = inflow_in[:, at(jnp.maximum(first - LANE, 0))]
    right = inflow_in[:, at(jnp.minimum(first + width // 2, columns // 2 - LANE))]
    coarse[half] = fringe_of(left, right, member, FRINGE // 2)

    def take(halo, bottom):
        base = fringe = 0
        for slot, deep in enumerate(COEF_ROWS):
            edge = slice(rows - deep, rows) if bottom else slice(0, deep)
            for chunk in range(chunks):
                halo[base : base + deep] = coefs[slot, chunk, edge]
                base += deep
            spare[fringe : fringe + deep] = coefs[slot, chunks, edge]
            fringe += deep
        halo[base : base + fringe // 4] = fold(spare, fringe)
        base += fringe // 4
        edge = slice(rows // 2 - COARSE_ROWS, rows // 2) if bottom else slice(0, COARSE_ROWS)
        for chunk in range(half + 1):
            halo[base : base + COARSE_ROWS] = coarse[chunk, edge]
            base += COARSE_ROWS

    def fill(below, above):
        take(below, True)
        take(above, False)

    by_side(sides(rows)[0], fill, halo_a, halo_b)


def edge_kernel(own, from_core, from_x, from_both, edge_a, edge_b, fields, spare):
    member = lax.axis_index("tm")
    chunks, rows = fields.shape[1] - 1, fields.shape[2]
    for slot, ref in enumerate((own, from_core, from_x, from_both)):
        target = fields.at[member ^ slot]
        for chunk in range(chunks):
            target[chunk] = ref[chunk * rows : (chunk + 1) * rows]
        unfold(ref[chunks * rows : chunks * rows + rows // 4], target.at[chunks], rows)

    def take(edge, bottom):
        base = fringe = 0
        for group, deep in enumerate(FIELD_ROWS):
            here = slice(rows - deep, rows) if bottom else slice(0, deep)
            for chunk in range(chunks):
                edge[base : base + deep] = fields[group, chunk, here]
                base += deep
            spare[fringe : fringe + deep] = fields[group, chunks, here]
            fringe += deep
        fringe = (fringe + 3) // 4 * 4
        edge[base : base + fringe // 4] = fold(spare, fringe)

    def fill(below, above):
        take(below, True)
        take(above, False)

    spare[...] = jnp.zeros_like(spare)
    by_side(sides(rows)[0], fill, edge_a, edge_b)


def spread(value):
    rows, lanes = value.shape
    value = value.reshape(rows // 8, 8, lanes)
    row_even = lax.broadcasted_iota(jnp.int32, value.shape, 1) % 2 == 0
    lane_even = lax.broadcasted_iota(jnp.int32, value.shape, 2) % 2 == 0
    value = value + jnp.where(row_even, pltpu.roll(value, 7, 1), pltpu.roll(value, 1, 1))
    value = value + jnp.where(lane_even, pltpu.roll(value, lanes - 1, 2), pltpu.roll(value, 1, 2))
    return (value * 0.25).reshape(rows, lanes)


def weights(cond_x, cond_y, chunk, rows, width, limit, out):
    diagonal, up, west = out
    chunks = cond_x.shape[0]
    first, count = rows
    here = slice(first, first + count)
    own_x, own_y = cond_x[chunk, here], cond_y[chunk, here]
    above = cond_x[chunk, first - width : first - width + count]
    lane = lanes_of(own_x.shape)
    row = lax.broadcasted_iota(jnp.int32, own_x.shape, 0)
    before = pltpu.roll(cond_y[(chunk - 1) % chunks, here], width, 1)
    beside = jnp.where(lane < width, before, pltpu.roll(own_y, width, 1))
    diagonal[chunk, here] = 1.0 - ((own_x + above) + (own_y + beside))
    up[chunk, here] = jnp.where(row < limit - first, above, 0.0)
    if chunk == chunks - 1:
        closed = jnp.where(lax.axis_index("tm") == lax.axis_size("tm") - 1, width, 0)
        beside = jnp.where(lane < closed, 0.0, beside)
    west[chunk, here] = beside


def prepare_kernel(
    coefs, coarse, coef_a, coef_b,
    cond_x, cond_y, response, diagonal, up, west, coarse_x, coarse_y, coarse_d, coarse_u, coarse_w, error, carried,
    tall, spare, source, work,
):
    _, chunks, rows, _ = coefs.shape
    chunks, half = chunks - 1, (chunks - 1) // 2
    low = HALO + rows
    even, limit = sides(rows)
    targets = (cond_x, cond_y, source)
    tall[...] = jnp.zeros_like(tall)

    def give(halo, below):
        base = fringe = 0
        for ref, deep in zip(targets, COEF_ROWS):
            first = low if below else HALO - deep
            for chunk in range(chunks):
                ref[chunk, first : first + deep] = halo[base : base + deep]
                base += deep
        total = sum(COEF_ROWS)
        unfold(halo[base : base + total // 4], spare, total)
        base += total // 4
        for ref, deep in zip(targets, COEF_ROWS):
            first = low if below else HALO - deep
            ref[chunks, first : first + deep] = spare[fringe : fringe + deep]
            fringe += deep
        first = 4 + rows // 2 if below else 4 - COARSE_ROWS
        for chunk in range(half + 1):
            tall[chunk, first : first + COARSE_ROWS] = halo[base : base + COARSE_ROWS]
            base += COARSE_ROWS

    def fill(below, above):
        give(below, True)
        give(above, False)

    by_side(even, fill, coef_a, coef_b)
    for slot, ref in enumerate(targets):
        ref[:, HALO:low] = coefs[slot]
    tall[:, 4 : 4 + rows // 2] = coarse[...]
    for chunk in range(chunks + 1):
        weights(cond_x, cond_y, chunk, reach(rows, 9), 1, limit, (diagonal, up, west))
    near = slice(HALO - 8, low + 8)
    for chunk in range(chunks + 1):
        coarse_x[chunk, near] = spread(cond_x[chunk, near])
        coarse_y[chunk, near] = spread(cond_y[chunk, near])
    for chunk in range(chunks + 1):
        weights(coarse_x, coarse_y, chunk, reach(rows, 4), 2, limit, (coarse_d, coarse_u, coarse_w))
    lane = lanes_of((8, LANE))
    twice = lax.broadcasted_iota(jnp.int32, (8, LANE), 0) // 2
    for chunk in range(chunks + 1):
        side = chunk % 2 * (LANE // 2)
        pick = lane // 2 + (side if chunk < chunks else jnp.where(lane < LANE // 2, 0, LANE // 2))
        for part in range((rows // 2 + 8) // 8):
            wide = jnp.take_along_axis(tall[chunk // 2, 8 * part : 8 * part + 8], pick, axis=1)
            for end in range(2):
                at = HALO - 8 + 16 * part + 8 * end
                error[chunk, at : at + 8] = jnp.take_along_axis(wide, twice + 4 * end, axis=0)
    fine = (diagonal, up, cond_x, cond_y, west)
    stops = [source] + [work.at[number] for number in range(FINE_STEPS - 1)]
    for number in range(FINE_STEPS - 1):
        sweep([(stops[number], stops[number + 1], span(rows, 8 - number), None, False)], 1, fine)
    first, count = reach(rows, 6)
    here = slice(first, first + count)
    for chunk in range(chunks + 1):
        total = source[chunk, here]
        for number in range(FINE_STEPS - 1):
            total = total + work[number, chunk, here]
        response[chunk, here] = total
    sweep([(error, carried, span(rows, 4), None, False)], 2, (coarse_d, coarse_u, coarse_x, coarse_y, coarse_w))


def sweep(items, width, factors):
    diagonal, up, down, east, west = factors
    chunks = diagonal.shape[0]
    lane = lanes_of((8, LANE))
    origin = min(item[2][0] for item in items)
    end = max(item[2][1] for item in items)
    for first in reversed(range(origin, end, 8)):
        here, above, below = (slice(first + move, first + move + 8) for move in (0, -width, width))
        active = [item for item in items if item[2][0] < first + 8 and item[2][1] > first]

        def load(values, chunk):
            value = values[chunk % chunks, here]
            return value, pltpu.roll(value, LANE - width, 1), pltpu.roll(value, width, 1)

        states = [[load(item[0], -1), load(item[0], 0)] for item in active]
        ends = [tuple(state) for state in states]
        for chunk in range(chunks):
            own = [ref[chunk, here] for ref in (diagonal, up, down, east, west)]
            for (values, put, _, added, inner), state, (last, start) in zip(active, states, ends):
                if inner and chunk == chunks - 1:
                    continue
                before, now = state
                after = start if chunk + 1 == chunks else last if chunk + 2 == chunks else load(values, chunk + 1)
                right = jnp.where(lane < LANE - width, now[1], after[1])
                left = jnp.where(lane < width, before[2], now[2])
                total = (own[3] * right + own[4] * left) + (own[2] * values[chunk, below] + own[1] * values[chunk, above])
                total = own[0] * now[0] + total
                put[chunk, here] = total if added is None else total + added(chunk, here)
                state[:] = [now, after]


def reach(rows, deep):
    return HALO - deep, (rows + 2 * deep + 7) // 8 * 8


def span(rows, deep):
    return HALO - deep, HALO + rows + deep


def main_kernel(
    fields, cond_x, cond_y, response, diagonal, up, west, coarse_x, coarse_y, coarse_d, coarse_u, coarse_w,
    start_error, carried, edge_a, edge_b, own, to_core, to_x, to_both,
    guess, work, error, spare,
):
    groups, chunks, rows, _ = fields.shape
    chunks -= 1
    low = HALO + rows
    given = groups - 1

    def give(edge, below):
        base = fringe = 0
        for group, deep in enumerate(FIELD_ROWS):
            first = low if below else HALO - deep
            for chunk in range(chunks):
                guess[group, chunk, first : first + deep] = edge[base : base + deep]
                base += deep
        total = (sum(FIELD_ROWS) + 3) // 4 * 4
        unfold(edge[base : base + total // 4], spare, total)
        for group, deep in enumerate(FIELD_ROWS):
            first = low if below else HALO - deep
            guess[group, chunks, first : first + deep] = spare[fringe : fringe + deep]
            fringe += deep

    def fill(below, above):
        give(below, True)
        give(above, False)

    by_side(sides(rows)[0], fill, edge_a, edge_b)
    for group in range(given):
        guess[group, :, HALO:low] = fields[group]
    fine = (diagonal, up, cond_x, cond_y, west)
    coarse = (coarse_d, coarse_u, coarse_x, coarse_y, coarse_w)

    def add_response(chunk, here):
        return response[chunk, here]

    def propagate(slots, deeps):
        for number in range(FINE_STEPS):
            items = []
            for place, (slot, deep) in enumerate(zip(slots, deeps)):
                first, second = work.at[2 * place], work.at[2 * place + 1]
                stops = [guess.at[slot], first, second, first, guess.at[slot + given]]
                needed = span(rows, deep + FINE_STEPS - 1 - number)
                added = add_response if number == FINE_STEPS - 1 else None
                inner = deep == 0 and number == FINE_STEPS - 1
                items.append((stops[number], stops[number + 1], needed, added, inner))
            sweep(items, 1, fine)

    propagate((0, 1, 2), (6, 4, 0))
    propagate((3, 4), (2, 0))

    def residual(group, chunk, here):
        reached = given if group == 1 else 2 * given - 2 + group
        return spread(guess[reached, chunk, here] - guess[given - 1 + group, chunk, here])

    first, count = reach(rows, 2 * (groups - 2))
    here = slice(first, first + count)
    for chunk in range(chunks + 1):
        error[1, chunk, here] = carried[chunk, here] + residual(1, chunk, here)
    for group in range(2, groups):
        needed = span(rows, 2 * (groups - 1 - group))
        inner = group == groups - 1
        sweep([(error.at[group - 1], error.at[group], needed, functools.partial(residual, group), inner)], 2, coarse)
    error[0, :, HALO:low] = start_error[:, HALO:low]

    member = lax.axis_index("tm")
    for slot, out in enumerate((own, to_core, to_x, to_both)):
        group = member ^ slot
        relaxed = jnp.where(group == 0, 0, given - 1 + group)
        for chunk in range(chunks):
            out[:, piece(chunk)] = guess[relaxed, chunk, HALO:low] + error[group, chunk, HALO:low]


def unpack_kernel(own, from_core, from_x, from_both, out, sems):
    width = own.shape[1]
    member = lax.axis_index("tm")
    copies = []
    for slot, ref in enumerate((own, from_core, from_x, from_both)):
        at = pl.ds(pl.multiple_of((member ^ slot) * width, LANE), width)
        copies.append(pltpu.make_async_copy(ref, out.at[0, :, at], sems.at[slot]))
    for copy in copies:
        copy.start()
    for copy in copies:
        copy.wait()


def call(kernel, outs, scratch, operands, whole=(), outside=False, copies=0):
    vmem, anywhere = (pl.BlockSpec(memory_space=space) for space in (pltpu.VMEM, pltpu.HBM))
    specs = [anywhere if slot in whole else vmem for slot in range(len(operands))]
    operands = [
        pltpu.with_memory_space_constraint(value, pltpu.HBM) if slot in whole else value
        for slot, value in enumerate(operands)
    ]
    return pl.pallas_call(
        kernel,
        out_shape=[jax.ShapeDtypeStruct(shape, jnp.float32) for shape in outs],
        in_specs=specs,
        out_specs=[anywhere if outside else vmem] * len(outs),
        scratch_shapes=[pltpu.VMEM(shape, jnp.float32) for shape in scratch]
        + ([pltpu.SemaphoreType.DMA((copies,))] if copies else []),
        compiler_params=pltpu.CompilerParams(vmem_limit_bytes=VMEM_LIMIT),
    )(*operands)


def shards(guesses, cond_x, cond_y, source, inflow):
    groups, strips = lax.axis_size("tm"), lax.axis_size("space")
    rows, columns = cond_x.shape
    fits = groups == len(FIELD_ROWS) + 1 and strips % 2 == 0 and rows == 16
    if not fits or columns % (2 * groups * LANE) != 0:
        return general_shards(guesses, cond_x, cond_y, source, inflow)
    own = columns // groups
    chunks = own // LANE
    pairs_a = [(i, i ^ 1) for i in range(strips)]
    pairs_b = [(i, j) for k in range(1, strips - 1, 2) for i, j in ((k, k + 1), (k + 1, k))]

    def trade(blocks):
        moved = [blocks[0]]
        for slot in range(1, groups):
            moved.append(lax.ppermute(blocks[slot], "tm", [(i, i ^ slot) for i in range(groups)]))
        return moved

    def whole(count):
        return (count + 7) // 8 * 8

    def folded(count):
        return count * chunks + (count + 3) // 4

    block = (whole(folded(rows)), LANE)
    halo = (whole(folded(sum(COEF_ROWS)) + (chunks // 2 + 1) * COARSE_ROWS), LANE)
    edge = (whole(folded(sum(FIELD_ROWS))), LANE)
    spare = (32, LANE)
    *blocks, halo_a, halo_b, coefs, coarse = call(
        pack_kernel,
        [block] * groups + [halo, halo, (3, chunks + 1, rows, LANE), (chunks // 2 + 1, rows // 2, LANE)],
        [(rows, columns), (3, rows, own + 2 * LANE), (rows // 2, columns // 2), spare],
        [guesses[0], cond_x, cond_y, source, inflow], whole=range(5), copies=5,
    )
    coef_a = lax.ppermute(halo_a, "space", pairs_a)
    coef_b = lax.ppermute(halo_b, "space", pairs_b)
    blocks = trade(blocks)
    sent_a, sent_b, fields = call(edge_kernel, [edge, edge, (groups, chunks + 1, rows, LANE)], [spare], blocks)
    edge_a = lax.ppermute(sent_a, "space", pairs_a)
    edge_b = lax.ppermute(sent_b, "space", pairs_b)
    buffer = (chunks + 1, rows + 2 * HALO, LANE)
    prepared = call(
        prepare_kernel,
        [buffer] * 13,
        [(chunks // 2 + 1, rows // 2 + 8, LANE), spare, buffer, (FINE_STEPS - 1, *buffer)],
        [coefs, coarse, coef_a, coef_b],
    )
    blocks = call(
        main_kernel,
        [(rows, own)] * groups,
        [(3 * groups - 4, *buffer), (2 * groups - 2, *buffer), (groups, *buffer), spare],
        [fields, *prepared, edge_a, edge_b],
    )
    return call(unpack_kernel, [(1, rows, columns)], [], trade(blocks), outside=True, copies=groups)[0]


def solution(mesh):
    return jax.shard_map(
        shards,
        mesh=mesh,
        in_specs=(
            P("tm", "space", None),
            P("space", None),
            P("space", None),
            P("space", None),
            P("space", None),
        ),
        out_specs=P("tm", "space", None),
        check_vma=False,
    )
```

```python
import functools

import jax
import jax.numpy as jnp
from jax import lax
from jax.experimental import pallas as pl
from jax.experimental.pallas import tpu as pltpu
from jax.sharding import PartitionSpec as P

FINE_STEPS = 4
LANE = 128
FRINGE = 16
HALO = 16
COEF_ROWS = (10, 9, 9)
FIELD_ROWS = (10, 8, 4)
COARSE_ROWS = 3
VMEM_LIMIT = 40 * 1024 * 1024


def padded(value, sides, width):
    for axis, dim in sides:
        devices, length = (lax.axis_size(axis), value.shape[dim])
        up = [(i, (i + 1) % devices) for i in range(devices - 1)]
        down = [(j, i) for i, j in up]
        last = lax.slice_in_dim(value, length - width, length, axis=dim)
        leading = lax.slice_in_dim(value, 0, width, axis=dim)
        before = lax.ppermute(last, axis, up)
        after = lax.ppermute(leading, axis, down)
        value = jnp.concatenate([before, value, after], axis=dim)
    return value


def from_behind(value, axis, steps):
    count = lax.axis_size(axis)
    leading, last = (max(0, -steps), min(count, count - steps))
    return lax.ppermute(value, axis, [(source, source + steps) for source in range(leading, last)])


def interior(field_ext, cond_rows, cond_cols):
    centre = field_ext[1:-1]
    flux_sum = cond_rows[1:-1] * (field_ext[2:] - centre) - cond_rows[:-2] * (
        centre - field_ext[:-2]
    )
    widened = jnp.pad(centre, ((0, 0), (1, 1)))
    cond_own = cond_cols[1:-1]
    cond_west = jnp.pad(cond_own, ((0, 0), (1, 0)))[:, :-1]
    flux_sum = (
        flux_sum + cond_own * (widened[:, 2:] - centre) - cond_west * (centre - widened[:, :-2])
    )
    return centre + flux_sum


def propagate(field, coef_pad):
    strip_rows = field.shape[0]
    cond_rows = coef_pad[0, 3 : strip_rows + 5]
    cond_cols = coef_pad[1, 3 : strip_rows + 5]
    source_rows = coef_pad[2, 4 : strip_rows + 4]
    for section in range(FINE_STEPS):
        extended = padded(field, (("space", 0),), 1)
        field = interior(extended, cond_rows, cond_cols) + source_rows
    return field


def restrict(field):
    lead = field.shape[:-2]
    shaped = field.reshape(lead + (field.shape[-2] // 2, 2, field.shape[-1] // 2, 2))
    return jnp.mean(shaped, axis=(-3, -1))


def general_shards(guesses, cond_x, cond_y, source, inflow):
    strip_rows = cond_x.shape[0]
    columns = cond_x.shape[1]
    stacked = jnp.stack([cond_x, cond_y, source])
    edge_rows = from_behind(cond_x[strip_rows - 2 :], "space", 1)
    cond_upper = jnp.concatenate([jnp.zeros((2, columns), jnp.float32), edge_rows], axis=0)
    blank_rows = jnp.zeros((4, columns), jnp.float32)
    upper = jnp.stack([cond_upper, blank_rows, blank_rows])
    lower = jnp.zeros((3, 4, columns), jnp.float32)
    coef_pad = jnp.concatenate([upper, stacked, lower], axis=1)
    first_group = lax.axis_index("tm") == 0
    c_point = guesses[0]
    first_pass = propagate(c_point, coef_pad)
    received = from_behind(first_pass, "tm", 1)
    relaxed = jnp.where(first_group, c_point, received)
    second_pass = propagate(relaxed, coef_pad)
    fine_next = from_behind(second_pass, "tm", 1)
    residual = restrict(fine_next - relaxed)
    residual = jnp.where(first_group, 0.0, residual)
    coarse_coef = restrict(coef_pad[:2, 2 : strip_rows + 6])

    def chain_round(index, error_field):
        extended = padded(error_field, (("space", 0),), 1)
        stepped = interior(extended, coarse_coef[0], coarse_coef[1])
        arrived = from_behind(stepped, "tm", 1)
        return jnp.where(first_group, inflow, arrived + residual)

    start_error = jnp.where(first_group, inflow, jnp.zeros_like(residual))
    error_field = lax.fori_loop(0, lax.axis_size("tm") - 1, chain_round, start_error)
    widened = jnp.repeat(jnp.repeat(error_field, 2, axis=0), 2, axis=1)
    return (relaxed + widened)[None]


def piece(chunk):
    return slice(chunk * LANE, (chunk + 1) * LANE)


def lanes_of(shape):
    return lax.broadcasted_iota(jnp.int32, shape, len(shape) - 1)


def fringe_of(left, right, member, width):
    lane = lanes_of(left.shape)
    last = lax.axis_size("tm") - 1
    value = jnp.where(lane < jnp.where(member < last, width, 0), right, 0.0)
    return jnp.where(lane >= jnp.where(member > 0, LANE - width, LANE), left, value)


def fold(source, rows):
    part = rows // 4
    total = source[:part]
    for turn in range(1, 4):
        total = total + pltpu.roll(source[turn * part : (turn + 1) * part], 2 * FRINGE * turn, 1)
    return total


def unfold(folded, target, rows):
    part = rows // 4
    lane = lanes_of(folded.shape)
    used = (lane < FRINGE) | (lane >= LANE - FRINGE)
    for turn in range(4):
        turned = pltpu.roll(folded, LANE - 2 * FRINGE * turn, 1) if turn else folded
        target[turn * part : (turn + 1) * part] = jnp.where(used, turned, 0.0)


def sides(rows):
    strip, strips = lax.axis_index("space"), lax.axis_size("space")
    return lax.rem(strip, 2) == 0, jnp.where(strip == strips - 1, HALO + rows, 2 * HALO + rows)


def by_side(even, fill, first, second):
    @pl.when(even)
    def _():
        fill(first, second)

    @pl.when(jnp.logical_not(even))
    def _():
        fill(second, first)


def pack_kernel(
    guess, cond_x, cond_y, source, inflow, own, to_core, to_x, to_both, halo_a, halo_b, coefs, coarse,
    guess_in, coefs_in, inflow_in, spare, sems,
):
    rows, columns = guess.shape
    groups, member = lax.axis_size("tm"), lax.axis_index("tm")
    width = columns // groups
    chunks = width // LANE

    def at(column):
        return pl.ds(pl.multiple_of(column, LANE), LANE)

    around = jnp.clip(width * member - LANE, 0, columns - width - 2 * LANE)
    span = pl.ds(pl.multiple_of(around, LANE), width + 2 * LANE)
    copies = [pltpu.make_async_copy(guess, guess_in, sems.at[0])]
    for slot, ref in enumerate((cond_x, cond_y, source)):
        copies.append(pltpu.make_async_copy(ref.at[:, span], coefs_in.at[slot], sems.at[1 + slot]))
    copies.append(pltpu.make_async_copy(inflow, inflow_in, sems.at[4]))
    for copy in copies:
        copy.start()
    copies[0].wait()
    for slot, out in enumerate((own, to_core, to_x, to_both)):
        target = member ^ slot
        first = width * target
        for chunk in range(chunks):
            out[chunk * rows : (chunk + 1) * rows] = guess_in[:, at(first + chunk * LANE)]
        left = guess_in[:, at(jnp.maximum(first - LANE, 0))]
        right = guess_in[:, at(jnp.minimum(first + width, columns - LANE))]
        spare[:rows] = fringe_of(left, right, target, FRINGE)
        out[chunks * rows : chunks * rows + rows // 4] = fold(spare, rows)
    for copy in copies[1:]:
        copy.wait()
    skip = width * member - around
    for slot in range(3):
        for chunk in range(chunks):
            coefs[slot, chunk] = coefs_in[slot, :, at(skip + chunk * LANE)]
        left = coefs_in[slot, :, at(jnp.maximum(skip - LANE, 0))]
        right = coefs_in[slot, :, at(jnp.minimum(skip + width, width + LANE))]
        coefs[slot, chunks] = fringe_of(left, right, member, FRINGE)
    first, half = width // 2 * member, chunks // 2
    for chunk in range(half):
        coarse[chunk] = inflow_in[:, at(first + chunk * LANE)]
    left = inflow_in[:, at(jnp.maximum(first - LANE, 0))]
    right = inflow_in[:, at(jnp.minimum(first + width // 2, columns // 2 - LANE))]
    coarse[half] = fringe_of(left, right, member, FRINGE // 2)

    def take(halo, bottom):
        base = fringe = 0
        for slot, deep in enumerate(COEF_ROWS):
            edge = slice(rows - deep, rows) if bottom else slice(0, deep)
            for chunk in range(chunks):
                halo[base : base + deep] = coefs[slot, chunk, edge]
                base += deep
            spare[fringe : fringe + deep] = coefs[slot, chunks, edge]
            fringe += deep
        halo[base : base + fringe // 4] = fold(spare, fringe)
        base += fringe // 4
        edge = slice(rows // 2 - COARSE_ROWS, rows // 2) if bottom else slice(0, COARSE_ROWS)
        for chunk in range(half + 1):
            halo[base : base + COARSE_ROWS] = coarse[chunk, edge]
            base += COARSE_ROWS

    def fill(below, above):
        take(below, True)
        take(above, False)

    by_side(sides(rows)[0], fill, halo_a, halo_b)
    strip = lax.axis_index("space")

    @pl.when((strip == 0) | (strip == lax.axis_size("space") - 1))
    def _():
        halo_b[...] = jnp.zeros_like(halo_b)


def edge_kernel(own, from_core, from_x, from_both, edge_a, edge_b, fields, spare):
    member = lax.axis_index("tm")
    chunks, rows = fields.shape[1] - 1, fields.shape[2]
    for slot, ref in enumerate((own, from_core, from_x, from_both)):
        target = fields.at[member ^ slot]
        for chunk in range(chunks):
            target[chunk] = ref[chunk * rows : (chunk + 1) * rows]
        unfold(ref[chunks * rows : chunks * rows + rows // 4], target.at[chunks], rows)

    def take(edge, bottom):
        base = fringe = 0
        for group, deep in enumerate(FIELD_ROWS):
            here = slice(rows - deep, rows) if bottom else slice(0, deep)
            for chunk in range(chunks):
                edge[base : base + deep] = fields[group, chunk, here]
                base += deep
            spare[fringe : fringe + deep] = fields[group, chunks, here]
            fringe += deep
        fringe = (fringe + 3) // 4 * 4
        edge[base : base + fringe // 4] = fold(spare, fringe)

    def fill(below, above):
        take(below, True)
        take(above, False)

    spare[...] = jnp.zeros_like(spare)
    by_side(sides(rows)[0], fill, edge_a, edge_b)


def spread(value):
    rows, lanes = value.shape
    value = value.reshape(rows // 8, 8, lanes)
    row_even = lax.broadcasted_iota(jnp.int32, value.shape, 1) % 2 == 0
    lane_even = lax.broadcasted_iota(jnp.int32, value.shape, 2) % 2 == 0
    value = value + jnp.where(row_even, pltpu.roll(value, 7, 1), pltpu.roll(value, 1, 1))
    value = value + jnp.where(lane_even, pltpu.roll(value, lanes - 1, 2), pltpu.roll(value, 1, 2))
    return (value * 0.25).reshape(rows, lanes)


def weights(cond_x, cond_y, chunk, rows, width, limit, out):
    diagonal, up, west = out
    chunks = cond_x.shape[0]
    first, count = rows
    here = slice(first, first + count)
    own_x, own_y = cond_x[chunk, here], cond_y[chunk, here]
    above = cond_x[chunk, first - width : first - width + count]
    lane = lanes_of(own_x.shape)
    row = lax.broadcasted_iota(jnp.int32, own_x.shape, 0)
    before = pltpu.roll(cond_y[(chunk - 1) % chunks, here], width, 1)
    beside = jnp.where(lane < width, before, pltpu.roll(own_y, width, 1))
    diagonal[chunk, here] = 1.0 - ((own_x + above) + (own_y + beside))
    up[chunk, here] = jnp.where(row < limit - first, above, 0.0)
    if chunk == chunks - 1:
        closed = jnp.where(lax.axis_index("tm") == lax.axis_size("tm") - 1, width, 0)
        beside = jnp.where(lane < closed, 0.0, beside)
    west[chunk, here] = beside


def prepare_kernel(
    coefs, coarse, coef_a, coef_b,
    cond_x, cond_y, response, diagonal, up, west, coarse_x, coarse_y, coarse_d, coarse_u, coarse_w, error, carried,
    tall, spare, source, work,
):
    _, chunks, rows, _ = coefs.shape
    chunks, half = chunks - 1, (chunks - 1) // 2
    low = HALO + rows
    even, limit = sides(rows)
    targets = (cond_x, cond_y, source)
    tall[...] = jnp.zeros_like(tall)

    def give(halo, below):
        base = fringe = 0
        for ref, deep in zip(targets, COEF_ROWS):
            first = low if below else HALO - deep
            for chunk in range(chunks):
                ref[chunk, first : first + deep] = halo[base : base + deep]
                base += deep
        total = sum(COEF_ROWS)
        unfold(halo[base : base + total // 4], spare, total)
        base += total // 4
        for ref, deep in zip(targets, COEF_ROWS):
            first = low if below else HALO - deep
            ref[chunks, first : first + deep] = spare[fringe : fringe + deep]
            fringe += deep
        first = 4 + rows // 2 if below else 4 - COARSE_ROWS
        for chunk in range(half + 1):
            tall[chunk, first : first + COARSE_ROWS] = halo[base : base + COARSE_ROWS]
            base += COARSE_ROWS

    def fill(below, above):
        give(below, True)
        give(above, False)

    by_side(even, fill, coef_a, coef_b)
    for slot, ref in enumerate(targets):
        ref[:, HALO:low] = coefs[slot]
    tall[:, 4 : 4 + rows // 2] = coarse[...]
    for chunk in range(chunks + 1):
        weights(cond_x, cond_y, chunk, reach(rows, 9), 1, limit, (diagonal, up, west))
    near = slice(HALO - 8, low + 8)
    for chunk in range(chunks + 1):
        coarse_x[chunk, near] = spread(cond_x[chunk, near])
        coarse_y[chunk, near] = spread(cond_y[chunk, near])
    for chunk in range(chunks + 1):
        weights(coarse_x, coarse_y, chunk, reach(rows, 4), 2, limit, (coarse_d, coarse_u, coarse_w))
    lane = lanes_of((8, LANE))
    twice = lax.broadcasted_iota(jnp.int32, (8, LANE), 0) // 2
    for chunk in range(chunks + 1):
        side = chunk % 2 * (LANE // 2)
        pick = lane // 2 + (side if chunk < chunks else jnp.where(lane < LANE // 2, 0, LANE // 2))
        for part in range((rows // 2 + 8) // 8):
            wide = jnp.take_along_axis(tall[chunk // 2, 8 * part : 8 * part + 8], pick, axis=1)
            for end in range(2):
                at = HALO - 8 + 16 * part + 8 * end
                error[chunk, at : at + 8] = jnp.take_along_axis(wide, twice + 4 * end, axis=0)
    fine = (diagonal, up, cond_x, cond_y, west)
    stops = [source] + [work.at[number] for number in range(FINE_STEPS - 1)]
    for number in range(FINE_STEPS - 1):
        sweep([(stops[number], stops[number + 1], span(rows, 8 - number), None, False)], 1, fine)
    first, count = reach(rows, 6)
    here = slice(first, first + count)
    for chunk in range(chunks + 1):
        total = source[chunk, here]
        for number in range(FINE_STEPS - 1):
            total = total + work[number, chunk, here]
        response[chunk, here] = total
    sweep([(error, carried, span(rows, 4), None, False)], 2, (coarse_d, coarse_u, coarse_x, coarse_y, coarse_w))


def sweep(items, width, factors):
    diagonal, up, down, east, west = factors
    chunks = diagonal.shape[0]
    lane = lanes_of((8, LANE))
    origin = min(item[2][0] for item in items)
    end = max(item[2][1] for item in items)
    for first in reversed(range(origin, end, 8)):
        here, above, below = (slice(first + move, first + move + 8) for move in (0, -width, width))
        active = [item for item in items if item[2][0] < first + 8 and item[2][1] > first]

        def load(values, chunk):
            value = values[chunk % chunks, here]
            return value, pltpu.roll(value, LANE - width, 1), pltpu.roll(value, width, 1)

        states = [[load(item[0], -1), load(item[0], 0)] for item in active]
        ends = [tuple(state) for state in states]
        for chunk in range(chunks):
            own = [ref[chunk, here] for ref in (diagonal, up, down, east, west)]
            for (values, put, _, added, inner), state, (last, start) in zip(active, states, ends):
                if inner and chunk == chunks - 1:
                    continue
                before, now = state
                after = start if chunk + 1 == chunks else last if chunk + 2 == chunks else load(values, chunk + 1)
                right = jnp.where(lane < LANE - width, now[1], after[1])
                left = jnp.where(lane < width, before[2], now[2])
                total = (own[3] * right + own[4] * left) + (own[2] * values[chunk, below] + own[1] * values[chunk, above])
                total = own[0] * now[0] + total
                put[chunk, here] = total if added is None else total + added(chunk, here)
                state[:] = [now, after]


def reach(rows, deep):
    return HALO - deep, (rows + 2 * deep + 7) // 8 * 8


def span(rows, deep):
    return HALO - deep, HALO + rows + deep


def main_kernel(
    fields, cond_x, cond_y, response, diagonal, up, west, coarse_x, coarse_y, coarse_d, coarse_u, coarse_w,
    start_error, carried, edge_a, edge_b, own, to_core, to_x, to_both,
    guess, work, error, spare,
):
    groups, chunks, rows, _ = fields.shape
    chunks -= 1
    low = HALO + rows
    given = groups - 1

    def give(edge, below):
        base = fringe = 0
        for group, deep in enumerate(FIELD_ROWS):
            first = low if below else HALO - deep
            for chunk in range(chunks):
                guess[group, chunk, first : first + deep] = edge[base : base + deep]
                base += deep
        total = (sum(FIELD_ROWS) + 3) // 4 * 4
        unfold(edge[base : base + total // 4], spare, total)
        for group, deep in enumerate(FIELD_ROWS):
            first = low if below else HALO - deep
            guess[group, chunks, first : first + deep] = spare[fringe : fringe + deep]
            fringe += deep

    def fill(below, above):
        give(below, True)
        give(above, False)

    by_side(sides(rows)[0], fill, edge_a, edge_b)
    for group in range(given):
        guess[group, :, HALO:low] = fields[group]
    fine = (diagonal, up, cond_x, cond_y, west)
    coarse = (coarse_d, coarse_u, coarse_x, coarse_y, coarse_w)

    def add_response(chunk, here):
        return response[chunk, here]

    def propagate(slots, deeps):
        for number in range(FINE_STEPS):
            items = []
            for place, (slot, deep) in enumerate(zip(slots, deeps)):
                first, second = work.at[2 * place], work.at[2 * place + 1]
                stops = [guess.at[slot], first, second, first, guess.at[slot + given]]
                needed = span(rows, deep + FINE_STEPS - 1 - number)
                added = add_response if number == FINE_STEPS - 1 else None
                inner = deep == 0 and number == FINE_STEPS - 1
                items.append((stops[number], stops[number + 1], needed, added, inner))
            sweep(items, 1, fine)

    propagate((0, 1, 2), (6, 4, 0))
    propagate((3, 4), (2, 0))

    def residual(group, chunk, here):
        reached = given if group == 1 else 2 * given - 2 + group
        return spread(guess[reached, chunk, here] - guess[given - 1 + group, chunk, here])

    first, count = reach(rows, 2 * (groups - 2))
    here = slice(first, first + count)
    for chunk in range(chunks + 1):
        error[1, chunk, here] = carried[chunk, here] + residual(1, chunk, here)
    for group in range(2, groups):
        needed = span(rows, 2 * (groups - 1 - group))
        inner = group == groups - 1
        sweep([(error.at[group - 1], error.at[group], needed, functools.partial(residual, group), inner)], 2, coarse)
    error[0, :, HALO:low] = start_error[:, HALO:low]

    member = lax.axis_index("tm")
    for slot, out in enumerate((own, to_core, to_x, to_both)):
        group = member ^ slot
        relaxed = jnp.where(group == 0, 0, given - 1 + group)
        for chunk in range(chunks):
            out[:, piece(chunk)] = guess[relaxed, chunk, HALO:low] + error[group, chunk, HALO:low]


def unpack_kernel(own, from_core, from_x, from_both, out, sems):
    width = own.shape[1]
    member = lax.axis_index("tm")
    copies = []
    for slot, ref in enumerate((own, from_core, from_x, from_both)):
        at = pl.ds(pl.multiple_of((member ^ slot) * width, LANE), width)
        copies.append(pltpu.make_async_copy(ref, out.at[0, :, at], sems.at[slot]))
    for copy in copies:
        copy.start()
    for copy in copies:
        copy.wait()


def call(kernel, outs, scratch, operands, whole=(), outside=False, copies=0):
    vmem, anywhere = (pl.BlockSpec(memory_space=space) for space in (pltpu.VMEM, pltpu.HBM))
    specs = [anywhere if slot in whole else vmem for slot in range(len(operands))]
    operands = [
        pltpu.with_memory_space_constraint(value, pltpu.HBM) if slot in whole else value
        for slot, value in enumerate(operands)
    ]
    return pl.pallas_call(
        kernel,
        out_shape=[jax.ShapeDtypeStruct(shape, jnp.float32) for shape in outs],
        in_specs=specs,
        out_specs=[anywhere if outside else vmem] * len(outs),
        scratch_shapes=[pltpu.VMEM(shape, jnp.float32) for shape in scratch]
        + ([pltpu.SemaphoreType.DMA((copies,))] if copies else []),
        compiler_params=pltpu.CompilerParams(vmem_limit_bytes=VMEM_LIMIT),
    )(*operands)


def shards(guesses, cond_x, cond_y, source, inflow):
    groups, strips = lax.axis_size("tm"), lax.axis_size("space")
    rows, columns = cond_x.shape
    fits = groups == len(FIELD_ROWS) + 1 and strips % 2 == 0 and rows == 16
    if not fits or columns % (2 * groups * LANE) != 0:
        return general_shards(guesses, cond_x, cond_y, source, inflow)
    own = columns // groups
    chunks = own // LANE
    pairs_a = [(i, i ^ 1) for i in range(strips)]
    pairs_b = [(i, j) for k in range(1, strips - 1, 2) for i, j in ((k, k + 1), (k + 1, k))]
    ring_b = [(i, j) for k in range(1, strips, 2) for i, j in ((k, (k + 1) % strips), ((k + 1) % strips, k))]

    def trade(blocks):
        moved = [blocks[0]]
        for slot in range(1, groups):
            moved.append(lax.ppermute(blocks[slot], "tm", [(i, i ^ slot) for i in range(groups)]))
        return moved

    def whole(count):
        return (count + 7) // 8 * 8

    def folded(count):
        return count * chunks + (count + 3) // 4

    block = (whole(folded(rows)), LANE)
    halo = (whole(folded(sum(COEF_ROWS)) + (chunks // 2 + 1) * COARSE_ROWS), LANE)
    edge = (whole(folded(sum(FIELD_ROWS))), LANE)
    spare = (32, LANE)
    *blocks, halo_a, halo_b, coefs, coarse = call(
        pack_kernel,
        [block] * groups + [halo, halo, (3, chunks + 1, rows, LANE), (chunks // 2 + 1, rows // 2, LANE)],
        [(rows, columns), (3, rows, own + 2 * LANE), (rows // 2, columns // 2), spare],
        [guesses[0], cond_x, cond_y, source, inflow], whole=range(5), copies=5,
    )
    coef_a = lax.ppermute(halo_a, "space", pairs_a)
    coef_b = lax.ppermute(halo_b, "space", ring_b)
    blocks = trade(blocks)
    sent_a, sent_b, fields = call(edge_kernel, [edge, edge, (groups, chunks + 1, rows, LANE)], [spare], blocks)
    edge_a = lax.ppermute(sent_a, "space", pairs_a)
    edge_b = lax.ppermute(sent_b, "space", pairs_b)
    buffer = (chunks + 1, rows + 2 * HALO, LANE)
    prepared = call(
        prepare_kernel,
        [buffer] * 13,
        [(chunks // 2 + 1, rows // 2 + 8, LANE), spare, buffer, (FINE_STEPS - 1, *buffer)],
        [coefs, coarse, coef_a, coef_b],
    )
    blocks = call(
        main_kernel,
        [(rows, own)] * groups,
        [(3 * groups - 4, *buffer), (2 * groups - 2, *buffer), (groups, *buffer), spare],
        [fields, *prepared, edge_a, edge_b],
    )
    return call(unpack_kernel, [(1, rows, columns)], [], trade(blocks), outside=True, copies=groups)[0]


def solution(mesh):
    return jax.shard_map(
        shards,
        mesh=mesh,
        in_specs=(
            P("tm", "space", None),
            P("space", None),
            P("space", None),
            P("space", None),
            P("space", None),
        ),
        out_specs=P("tm", "space", None),
        check_vma=False,
    )
```

```python
import functools

import jax
import jax.numpy as jnp
from jax import lax
from jax.experimental import pallas as pl
from jax.experimental.pallas import tpu as pltpu
from jax.sharding import PartitionSpec as P

FINE_STEPS = 4
LANE = 128
FRINGE = 16
HALO = 16
COEF_ROWS = (10, 9, 9)
FIELD_ROWS = (10, 8, 4)
COARSE_ROWS = 3
SLOTS = (0, 2, 3, 1)
VMEM_LIMIT = 40 * 1024 * 1024


def padded(value, sides, width):
    for axis, dim in sides:
        devices, length = (lax.axis_size(axis), value.shape[dim])
        up = [(i, (i + 1) % devices) for i in range(devices - 1)]
        down = [(j, i) for i, j in up]
        last = lax.slice_in_dim(value, length - width, length, axis=dim)
        leading = lax.slice_in_dim(value, 0, width, axis=dim)
        before = lax.ppermute(last, axis, up)
        after = lax.ppermute(leading, axis, down)
        value = jnp.concatenate([before, value, after], axis=dim)
    return value


def from_behind(value, axis, steps):
    count = lax.axis_size(axis)
    leading, last = (max(0, -steps), min(count, count - steps))
    return lax.ppermute(value, axis, [(source, source + steps) for source in range(leading, last)])


def interior(field_ext, cond_rows, cond_cols):
    centre = field_ext[1:-1]
    flux_sum = cond_rows[1:-1] * (field_ext[2:] - centre) - cond_rows[:-2] * (
        centre - field_ext[:-2]
    )
    widened = jnp.pad(centre, ((0, 0), (1, 1)))
    cond_own = cond_cols[1:-1]
    cond_west = jnp.pad(cond_own, ((0, 0), (1, 0)))[:, :-1]
    flux_sum = (
        flux_sum + cond_own * (widened[:, 2:] - centre) - cond_west * (centre - widened[:, :-2])
    )
    return centre + flux_sum


def propagate(field, coef_pad):
    strip_rows = field.shape[0]
    cond_rows = coef_pad[0, 3 : strip_rows + 5]
    cond_cols = coef_pad[1, 3 : strip_rows + 5]
    source_rows = coef_pad[2, 4 : strip_rows + 4]
    for section in range(FINE_STEPS):
        extended = padded(field, (("space", 0),), 1)
        field = interior(extended, cond_rows, cond_cols) + source_rows
    return field


def restrict(field):
    lead = field.shape[:-2]
    shaped = field.reshape(lead + (field.shape[-2] // 2, 2, field.shape[-1] // 2, 2))
    return jnp.mean(shaped, axis=(-3, -1))


def general_shards(guesses, cond_x, cond_y, source, inflow):
    strip_rows = cond_x.shape[0]
    columns = cond_x.shape[1]
    stacked = jnp.stack([cond_x, cond_y, source])
    edge_rows = from_behind(cond_x[strip_rows - 2 :], "space", 1)
    cond_upper = jnp.concatenate([jnp.zeros((2, columns), jnp.float32), edge_rows], axis=0)
    blank_rows = jnp.zeros((4, columns), jnp.float32)
    upper = jnp.stack([cond_upper, blank_rows, blank_rows])
    lower = jnp.zeros((3, 4, columns), jnp.float32)
    coef_pad = jnp.concatenate([upper, stacked, lower], axis=1)
    first_group = lax.axis_index("tm") == 0
    c_point = guesses[0]
    first_pass = propagate(c_point, coef_pad)
    received = from_behind(first_pass, "tm", 1)
    relaxed = jnp.where(first_group, c_point, received)
    second_pass = propagate(relaxed, coef_pad)
    fine_next = from_behind(second_pass, "tm", 1)
    residual = restrict(fine_next - relaxed)
    residual = jnp.where(first_group, 0.0, residual)
    coarse_coef = restrict(coef_pad[:2, 2 : strip_rows + 6])

    def chain_round(index, error_field):
        extended = padded(error_field, (("space", 0),), 1)
        stepped = interior(extended, coarse_coef[0], coarse_coef[1])
        arrived = from_behind(stepped, "tm", 1)
        return jnp.where(first_group, inflow, arrived + residual)

    start_error = jnp.where(first_group, inflow, jnp.zeros_like(residual))
    error_field = lax.fori_loop(0, lax.axis_size("tm") - 1, chain_round, start_error)
    widened = jnp.repeat(jnp.repeat(error_field, 2, axis=0), 2, axis=1)
    return (relaxed + widened)[None]


def piece(chunk):
    return slice(chunk * LANE, (chunk + 1) * LANE)


def lanes_of(shape):
    return lax.broadcasted_iota(jnp.int32, shape, len(shape) - 1)


def fringe_of(left, right, member, width):
    lane = lanes_of(left.shape)
    last = lax.axis_size("tm") - 1
    value = jnp.where(lane < jnp.where(member < last, width, 0), right, 0.0)
    return jnp.where(lane >= jnp.where(member > 0, LANE - width, LANE), left, value)


def fold(source, rows):
    part = rows // 4
    total = source[:part]
    for turn in range(1, 4):
        total = total + pltpu.roll(source[turn * part : (turn + 1) * part], 2 * FRINGE * turn, 1)
    return total


def unfold(folded, target, rows):
    part = rows // 4
    lane = lanes_of(folded.shape)
    used = (lane < FRINGE) | (lane >= LANE - FRINGE)
    for turn in range(4):
        turned = pltpu.roll(folded, LANE - 2 * FRINGE * turn, 1) if turn else folded
        target[turn * part : (turn + 1) * part] = jnp.where(used, turned, 0.0)


def sides(rows):
    strip, strips = lax.axis_index("space"), lax.axis_size("space")
    return lax.rem(strip, 2) == 0, jnp.where(strip == strips - 1, HALO + rows, 2 * HALO + rows)


def by_side(even, fill, first, second):
    @pl.when(even)
    def _():
        fill(first, second)

    @pl.when(jnp.logical_not(even))
    def _():
        fill(second, first)


def pack_kernel(
    guess, cond_x, cond_y, source, inflow, own, to_x, to_both, to_core, halo_a, halo_b, coefs, coarse,
    guess_in, coefs_in, inflow_in, spare, sems,
):
    rows, columns = guess.shape
    groups, member = lax.axis_size("tm"), lax.axis_index("tm")
    width = columns // groups
    chunks = width // LANE

    def at(column):
        return pl.ds(pl.multiple_of(column, LANE), LANE)

    around = jnp.clip(width * member - LANE, 0, columns - width - 2 * LANE)
    span = pl.ds(pl.multiple_of(around, LANE), width + 2 * LANE)
    copies = [pltpu.make_async_copy(guess, guess_in, sems.at[0])]
    for slot, ref in enumerate((cond_x, cond_y, source)):
        copies.append(pltpu.make_async_copy(ref.at[:, span], coefs_in.at[slot], sems.at[1 + slot]))
    copies.append(pltpu.make_async_copy(inflow, inflow_in, sems.at[4]))
    for copy in copies:
        copy.start()
    copies[0].wait()
    for slot, out in zip(SLOTS, (own, to_x, to_both, to_core)):
        target = member ^ slot
        first = width * target
        for chunk in range(chunks):
            out[chunk * rows : (chunk + 1) * rows] = guess_in[:, at(first + chunk * LANE)]
        left = guess_in[:, at(jnp.maximum(first - LANE, 0))]
        right = guess_in[:, at(jnp.minimum(first + width, columns - LANE))]
        spare[:rows] = fringe_of(left, right, target, FRINGE)
        out[chunks * rows : chunks * rows + rows // 4] = fold(spare, rows)
    for copy in copies[1:]:
        copy.wait()
    skip = width * member - around
    for slot in range(3):
        for chunk in range(chunks):
            coefs[slot, chunk] = coefs_in[slot, :, at(skip + chunk * LANE)]
        left = coefs_in[slot, :, at(jnp.maximum(skip - LANE, 0))]
        right = coefs_in[slot, :, at(jnp.minimum(skip + width, width + LANE))]
        coefs[slot, chunks] = fringe_of(left, right, member, FRINGE)
    first, half = width // 2 * member, chunks // 2
    for chunk in range(half):
        coarse[chunk] = inflow_in[:, at(first + chunk * LANE)]
    left = inflow_in[:, at(jnp.maximum(first - LANE, 0))]
    right = inflow_in[:, at(jnp.minimum(first + width // 2, columns // 2 - LANE))]
    coarse[half] = fringe_of(left, right, member, FRINGE // 2)

    def take(halo, bottom):
        base = fringe = 0
        for slot, deep in enumerate(COEF_ROWS):
            edge = slice(rows - deep, rows) if bottom else slice(0, deep)
            for chunk in range(chunks):
                halo[base : base + deep] = coefs[slot, chunk, edge]
                base += deep
            spare[fringe : fringe + deep] = coefs[slot, chunks, edge]
            fringe += deep
        halo[base : base + fringe // 4] = fold(spare, fringe)
        base += fringe // 4
        edge = slice(rows // 2 - COARSE_ROWS, rows // 2) if bottom else slice(0, COARSE_ROWS)
        for chunk in range(half + 1):
            halo[base : base + COARSE_ROWS] = coarse[chunk, edge]
            base += COARSE_ROWS

    def fill(below, above):
        take(below, True)
        take(above, False)

    by_side(sides(rows)[0], fill, halo_a, halo_b)
    strip = lax.axis_index("space")

    @pl.when((strip == 0) | (strip == lax.axis_size("space") - 1))
    def _():
        halo_b[...] = jnp.zeros_like(halo_b)


def edge_kernel(own, from_x, from_both, from_core, edge_a, edge_b, fields, spare):
    member = lax.axis_index("tm")
    chunks, rows = fields.shape[1] - 1, fields.shape[2]
    for slot, ref in zip(SLOTS, (own, from_x, from_both, from_core)):
        target = fields.at[member ^ slot]
        for chunk in range(chunks):
            target[chunk] = ref[chunk * rows : (chunk + 1) * rows]
        unfold(ref[chunks * rows : chunks * rows + rows // 4], target.at[chunks], rows)

    def take(edge, bottom):
        base = fringe = 0
        for group, deep in enumerate(FIELD_ROWS):
            here = slice(rows - deep, rows) if bottom else slice(0, deep)
            for chunk in range(chunks):
                edge[base : base + deep] = fields[group, chunk, here]
                base += deep
            spare[fringe : fringe + deep] = fields[group, chunks, here]
            fringe += deep
        fringe = (fringe + 3) // 4 * 4
        edge[base : base + fringe // 4] = fold(spare, fringe)

    def fill(below, above):
        take(below, True)
        take(above, False)

    spare[...] = jnp.zeros_like(spare)
    by_side(sides(rows)[0], fill, edge_a, edge_b)


def spread(value):
    rows, lanes = value.shape
    value = value.reshape(rows // 8, 8, lanes)
    row_even = lax.broadcasted_iota(jnp.int32, value.shape, 1) % 2 == 0
    lane_even = lax.broadcasted_iota(jnp.int32, value.shape, 2) % 2 == 0
    value = value + jnp.where(row_even, pltpu.roll(value, 7, 1), pltpu.roll(value, 1, 1))
    value = value + jnp.where(lane_even, pltpu.roll(value, lanes - 1, 2), pltpu.roll(value, 1, 2))
    return (value * 0.25).reshape(rows, lanes)


def weights(cond_x, cond_y, chunk, rows, width, limit, out):
    diagonal, up, west = out
    chunks = cond_x.shape[0]
    first, count = rows
    here = slice(first, first + count)
    own_x, own_y = cond_x[chunk, here], cond_y[chunk, here]
    above = cond_x[chunk, first - width : first - width + count]
    lane = lanes_of(own_x.shape)
    row = lax.broadcasted_iota(jnp.int32, own_x.shape, 0)
    before = pltpu.roll(cond_y[(chunk - 1) % chunks, here], width, 1)
    beside = jnp.where(lane < width, before, pltpu.roll(own_y, width, 1))
    diagonal[chunk, here] = 1.0 - ((own_x + above) + (own_y + beside))
    up[chunk, here] = jnp.where(row < limit - first, above, 0.0)
    if chunk == chunks - 1:
        closed = jnp.where(lax.axis_index("tm") == lax.axis_size("tm") - 1, width, 0)
        beside = jnp.where(lane < closed, 0.0, beside)
    west[chunk, here] = beside


def prepare_kernel(
    coefs, coarse, coef_a, coef_b,
    cond_x, cond_y, response, diagonal, up, west, coarse_x, coarse_y, coarse_d, coarse_u, coarse_w, error, carried,
    tall, spare, source, work,
):
    _, chunks, rows, _ = coefs.shape
    chunks, half = chunks - 1, (chunks - 1) // 2
    low = HALO + rows
    even, limit = sides(rows)
    targets = (cond_x, cond_y, source)
    tall[...] = jnp.zeros_like(tall)

    def give(halo, below):
        base = fringe = 0
        for ref, deep in zip(targets, COEF_ROWS):
            first = low if below else HALO - deep
            for chunk in range(chunks):
                ref[chunk, first : first + deep] = halo[base : base + deep]
                base += deep
        total = sum(COEF_ROWS)
        unfold(halo[base : base + total // 4], spare, total)
        base += total // 4
        for ref, deep in zip(targets, COEF_ROWS):
            first = low if below else HALO - deep
            ref[chunks, first : first + deep] = spare[fringe : fringe + deep]
            fringe += deep
        first = 4 + rows // 2 if below else 4 - COARSE_ROWS
        for chunk in range(half + 1):
            tall[chunk, first : first + COARSE_ROWS] = halo[base : base + COARSE_ROWS]
            base += COARSE_ROWS

    def fill(below, above):
        give(below, True)
        give(above, False)

    by_side(even, fill, coef_a, coef_b)
    for slot, ref in enumerate(targets):
        ref[:, HALO:low] = coefs[slot]
    tall[:, 4 : 4 + rows // 2] = coarse[...]
    for chunk in range(chunks + 1):
        weights(cond_x, cond_y, chunk, reach(rows, 9), 1, limit, (diagonal, up, west))
    near = slice(HALO - 8, low + 8)
    for chunk in range(chunks + 1):
        coarse_x[chunk, near] = spread(cond_x[chunk, near])
        coarse_y[chunk, near] = spread(cond_y[chunk, near])
    for chunk in range(chunks + 1):
        weights(coarse_x, coarse_y, chunk, reach(rows, 4), 2, limit, (coarse_d, coarse_u, coarse_w))
    lane = lanes_of((8, LANE))
    twice = lax.broadcasted_iota(jnp.int32, (8, LANE), 0) // 2
    for chunk in range(chunks + 1):
        side = chunk % 2 * (LANE // 2)
        pick = lane // 2 + (side if chunk < chunks else jnp.where(lane < LANE // 2, 0, LANE // 2))
        for part in range((rows // 2 + 8) // 8):
            wide = jnp.take_along_axis(tall[chunk // 2, 8 * part : 8 * part + 8], pick, axis=1)
            for end in range(2):
                at = HALO - 8 + 16 * part + 8 * end
                error[chunk, at : at + 8] = jnp.take_along_axis(wide, twice + 4 * end, axis=0)
    fine = (diagonal, up, cond_x, cond_y, west)
    stops = [source] + [work.at[number] for number in range(FINE_STEPS - 1)]
    for number in range(FINE_STEPS - 1):
        sweep([(stops[number], stops[number + 1], span(rows, 8 - number), None, False)], 1, fine)
    first, count = reach(rows, 6)
    here = slice(first, first + count)
    for chunk in range(chunks + 1):
        total = source[chunk, here]
        for number in range(FINE_STEPS - 1):
            total = total + work[number, chunk, here]
        response[chunk, here] = total
    sweep([(error, carried, span(rows, 4), None, False)], 2, (coarse_d, coarse_u, coarse_x, coarse_y, coarse_w))


def sweep(items, width, factors):
    diagonal, up, down, east, west = factors
    chunks = diagonal.shape[0]
    lane = lanes_of((8, LANE))
    origin = min(item[2][0] for item in items)
    end = max(item[2][1] for item in items)
    for first in reversed(range(origin, end, 8)):
        here, above, below = (slice(first + move, first + move + 8) for move in (0, -width, width))
        active = [item for item in items if item[2][0] < first + 8 and item[2][1] > first]

        def load(values, chunk):
            value = values[chunk % chunks, here]
            return value, pltpu.roll(value, LANE - width, 1), pltpu.roll(value, width, 1)

        states = [[load(item[0], -1), load(item[0], 0)] for item in active]
        ends = [tuple(state) for state in states]
        for chunk in range(chunks):
            own = [ref[chunk, here] for ref in (diagonal, up, down, east, west)]
            for (values, put, _, added, inner), state, (last, start) in zip(active, states, ends):
                if inner and chunk == chunks - 1:
                    continue
                before, now = state
                after = start if chunk + 1 == chunks else last if chunk + 2 == chunks else load(values, chunk + 1)
                right = jnp.where(lane < LANE - width, now[1], after[1])
                left = jnp.where(lane < width, before[2], now[2])
                total = (own[3] * right + own[4] * left) + (own[2] * values[chunk, below] + own[1] * values[chunk, above])
                total = own[0] * now[0] + total
                put[chunk, here] = total if added is None else total + added(chunk, here)
                state[:] = [now, after]


def reach(rows, deep):
    return HALO - deep, (rows + 2 * deep + 7) // 8 * 8


def span(rows, deep):
    return HALO - deep, HALO + rows + deep


def main_kernel(
    fields, cond_x, cond_y, response, diagonal, up, west, coarse_x, coarse_y, coarse_d, coarse_u, coarse_w,
    start_error, carried, edge_a, edge_b, own, to_x, to_both, to_core,
    guess, work, error, spare,
):
    groups, chunks, rows, _ = fields.shape
    chunks -= 1
    low = HALO + rows
    given = groups - 1

    def give(edge, below):
        base = fringe = 0
        for group, deep in enumerate(FIELD_ROWS):
            first = low if below else HALO - deep
            for chunk in range(chunks):
                guess[group, chunk, first : first + deep] = edge[base : base + deep]
                base += deep
        total = (sum(FIELD_ROWS) + 3) // 4 * 4
        unfold(edge[base : base + total // 4], spare, total)
        for group, deep in enumerate(FIELD_ROWS):
            first = low if below else HALO - deep
            guess[group, chunks, first : first + deep] = spare[fringe : fringe + deep]
            fringe += deep

    def fill(below, above):
        give(below, True)
        give(above, False)

    by_side(sides(rows)[0], fill, edge_a, edge_b)
    for group in range(given):
        guess[group, :, HALO:low] = fields[group]
    fine = (diagonal, up, cond_x, cond_y, west)
    coarse = (coarse_d, coarse_u, coarse_x, coarse_y, coarse_w)

    def add_response(chunk, here):
        return response[chunk, here]

    def propagate(slots, deeps):
        for number in range(FINE_STEPS):
            items = []
            for place, (slot, deep) in enumerate(zip(slots, deeps)):
                first, second = work.at[2 * place], work.at[2 * place + 1]
                stops = [guess.at[slot], first, second, first, guess.at[slot + given]]
                needed = span(rows, deep + FINE_STEPS - 1 - number)
                added = add_response if number == FINE_STEPS - 1 else None
                inner = deep == 0 and number == FINE_STEPS - 1
                items.append((stops[number], stops[number + 1], needed, added, inner))
            sweep(items, 1, fine)

    propagate((0, 1, 2), (6, 4, 0))
    propagate((3, 4), (2, 0))

    def residual(group, chunk, here):
        reached = given if group == 1 else 2 * given - 2 + group
        return spread(guess[reached, chunk, here] - guess[given - 1 + group, chunk, here])

    first, count = reach(rows, 2 * (groups - 2))
    here = slice(first, first + count)
    for chunk in range(chunks + 1):
        error[1, chunk, here] = carried[chunk, here] + residual(1, chunk, here)
    for group in range(2, groups):
        needed = span(rows, 2 * (groups - 1 - group))
        inner = group == groups - 1
        sweep([(error.at[group - 1], error.at[group], needed, functools.partial(residual, group), inner)], 2, coarse)
    error[0, :, HALO:low] = start_error[:, HALO:low]

    member = lax.axis_index("tm")
    for slot, out in zip(SLOTS, (own, to_x, to_both, to_core)):
        group = member ^ slot
        relaxed = jnp.where(group == 0, 0, given - 1 + group)
        for chunk in range(chunks):
            out[:, piece(chunk)] = guess[relaxed, chunk, HALO:low] + error[group, chunk, HALO:low]


def unpack_kernel(own, from_x, from_both, from_core, out, sems):
    width = own.shape[1]
    member = lax.axis_index("tm")
    copies = []
    for slot, ref in zip(SLOTS, (own, from_x, from_both, from_core)):
        at = pl.ds(pl.multiple_of((member ^ slot) * width, LANE), width)
        copies.append(pltpu.make_async_copy(ref, out.at[0, :, at], sems.at[slot]))
    for copy in copies:
        copy.start()
    for copy in copies:
        copy.wait()


def call(kernel, outs, scratch, operands, whole=(), outside=False, copies=0):
    vmem, anywhere = (pl.BlockSpec(memory_space=space) for space in (pltpu.VMEM, pltpu.HBM))
    specs = [anywhere if slot in whole else vmem for slot in range(len(operands))]
    operands = [
        pltpu.with_memory_space_constraint(value, pltpu.HBM) if slot in whole else value
        for slot, value in enumerate(operands)
    ]
    return pl.pallas_call(
        kernel,
        out_shape=[jax.ShapeDtypeStruct(shape, jnp.float32) for shape in outs],
        in_specs=specs,
        out_specs=[anywhere if outside else vmem] * len(outs),
        scratch_shapes=[pltpu.VMEM(shape, jnp.float32) for shape in scratch]
        + ([pltpu.SemaphoreType.DMA((copies,))] if copies else []),
        compiler_params=pltpu.CompilerParams(vmem_limit_bytes=VMEM_LIMIT),
    )(*operands)


def shards(guesses, cond_x, cond_y, source, inflow):
    groups, strips = lax.axis_size("tm"), lax.axis_size("space")
    rows, columns = cond_x.shape
    fits = groups == len(SLOTS) and strips % 2 == 0 and rows == 16
    if not fits or columns % (2 * groups * LANE) != 0:
        return general_shards(guesses, cond_x, cond_y, source, inflow)
    own = columns // groups
    chunks = own // LANE
    pairs_a = [(i, i ^ 1) for i in range(strips)]
    pairs_b = [(i, j) for k in range(1, strips - 1, 2) for i, j in ((k, k + 1), (k + 1, k))]
    ring_b = [(i, j) for k in range(1, strips, 2) for i, j in ((k, (k + 1) % strips), ((k + 1) % strips, k))]

    def trade(blocks):
        moved = [blocks[0]]
        for slot, block in zip(SLOTS[1:], blocks[1:]):
            moved.append(lax.ppermute(block, "tm", [(i, i ^ slot) for i in range(groups)]))
        return moved

    def whole(count):
        return (count + 7) // 8 * 8

    def folded(count):
        return count * chunks + (count + 3) // 4

    block = (whole(folded(rows)), LANE)
    halo = (whole(folded(sum(COEF_ROWS)) + (chunks // 2 + 1) * COARSE_ROWS), LANE)
    edge = (whole(folded(sum(FIELD_ROWS))), LANE)
    spare = (32, LANE)
    *blocks, halo_a, halo_b, coefs, coarse = call(
        pack_kernel,
        [block] * groups + [halo, halo, (3, chunks + 1, rows, LANE), (chunks // 2 + 1, rows // 2, LANE)],
        [(rows, columns), (3, rows, own + 2 * LANE), (rows // 2, columns // 2), spare],
        [guesses[0], cond_x, cond_y, source, inflow], whole=range(5), copies=5,
    )
    coef_a = lax.ppermute(halo_a, "space", pairs_a)
    coef_b = lax.ppermute(halo_b, "space", ring_b)
    blocks = trade(blocks)
    sent_a, sent_b, fields = call(edge_kernel, [edge, edge, (groups, chunks + 1, rows, LANE)], [spare], blocks)
    edge_a = lax.ppermute(sent_a, "space", pairs_a)
    edge_b = lax.ppermute(sent_b, "space", pairs_b)
    buffer = (chunks + 1, rows + 2 * HALO, LANE)
    prepared = call(
        prepare_kernel,
        [buffer] * 13,
        [(chunks // 2 + 1, rows // 2 + 8, LANE), spare, buffer, (FINE_STEPS - 1, *buffer)],
        [coefs, coarse, coef_a, coef_b],
    )
    blocks = call(
        main_kernel,
        [(rows, own)] * groups,
        [(3 * groups - 4, *buffer), (2 * groups - 2, *buffer), (groups, *buffer), spare],
        [fields, *prepared, edge_a, edge_b],
    )
    return call(unpack_kernel, [(1, rows, columns)], [], trade(blocks), outside=True, copies=groups)[0]


def solution(mesh):
    return jax.shard_map(
        shards,
        mesh=mesh,
        in_specs=(
            P("tm", "space", None),
            P("space", None),
            P("space", None),
            P("space", None),
            P("space", None),
        ),
        out_specs=P("tm", "space", None),
        check_vma=False,
    )
```
